32 devices in a mesh: experts: 2 (over y), context: 4 (over z), dp: 4 (over x, core).
Axes of the slice: x: 2, y: 2, z: 4, core: 2. Of those that a mesh axis runs over, the one named last changes fastest.
Arguments:
- decoder_input: bfloat16 [8, 2048, 1024], P(('experts', 'dp'), 'context'), may hold values from -6 to 6
- gain_attn: float32 [1024], replicated, may hold values from 0.5 to 1.5
- query_weight: bfloat16 [1024, 1024], replicated, may hold values from -0.1875 to 0.1875
- keyval_weight: bfloat16 [1024, 1024], replicated, may hold values from -0.1875 to 0.1875
- output_weight: bfloat16 [1024, 1024], replicated, may hold values from -0.75 to 0.75
- gain_moe: float32 [1024], replicated, may hold values from 0.5 to 1.5
- w_router: bfloat16 [1024, 32], replicated, may hold values from -0.09375 to 0.09375
- w_gateup: bfloat16 [32, 1024, 1024], P('experts'), may hold values from -0.1875 to 0.1875
- w_down: bfloat16 [32, 512, 1024], P('experts'), may hold values from -0.75 to 0.75
- top_idx: int32 [8, 2048, 8], P(('experts', 'dp'), 'context'), may hold values from 0 to 31, all different within a row
- slot_order: int32 [8, 4, 512], P(('experts', 'dp'), 'context'), may hold values from 0 to 511, each once within a row
- cotangent: bfloat16 [8, 2048, 1024], P(('experts', 'dp'), 'context'), may hold values from -6 to 6
Outputs:
- layer_output: bfloat16 [8, 2048, 1024], P(('experts', 'dp'), 'context')
- grad_input: bfloat16 [8, 2048, 1024], P(('experts', 'dp'), 'context')
- grad_gain_attn: float32 [1024], P(('experts', 'context', 'dp'))
- grad_query: float32 [1024, 1024], P(('experts', 'context', 'dp'))
- grad_keyval: float32 [1024, 1024], P(('experts', 'context', 'dp'))
- grad_out: float32 [1024, 1024], P(('experts', 'context', 'dp'))
- grad_gain_moe: float32 [1024], P(('experts', 'context', 'dp'))
- grad_router: float32 [1024, 32], P(('experts', 'context', 'dp'))
- grad_gateup: float32 [32, 1024, 1024], P('experts', ('context', 'dp'))
- grad_down: float32 [32, 512, 1024], P('experts', None, ('context', 'dp'))
The draws below stay inside these ranges and needn't reach their ends.
Inputs may be any that keep to these rules, and one draw needn't show every extreme that they name: `top_idx`: each token names 8 different experts; every expert is named by some token. `slot_order`: within each routing group every value appears once.
All inputs are finite; a program needn't handle non-finite values.
Results may differ from the reference program's by a relative error of at most 0.02.
Values may be sent and summed in bfloat16 or wider, within the bound.
No kernel may reach another device: no remote copies, remote signals or barrier semaphores. Data moves between devices by JAX's collectives and lax.ppermute only.
A program may use at most 256 MiB of HBM per device.

```python
from functools import partial
import jax
import jax.numpy as jnp
from jax import lax

D = 1024
QH = 16
KVH = 8
HD = 64
FF = 512
EXPERTS = 32
TOPK = 8
BLOCK = 256
SPAN = 512
LEN = 2048
SEQS = 8
CAP = 160
N_CONTEXT = 4


def block_levels(key, shape, split, low, high):
    level = 1.0
    for position, shards_of in split:
        heights = jax.random.uniform(jax.random.fold_in(jax.random.fold_in(key, 6), position), (shards_of,), jnp.float32, low / len(split), high / len(split))
        level = level * jnp.repeat(jnp.exp(heights), shape[position] // shards_of).reshape((-1,) + (1,) * (len(shape) - 1 - position))
    return level


def different_ones(key, rows, count, top, lift):
    order = jax.random.permutation(jax.random.fold_in(key, 1), count)
    pull = order
    for power in range(3):
        pull = pull * pull // count
    pull = pull * lift // count
    tickets = jax.random.randint(jax.random.fold_in(key, 2), (rows, count), 0, 4096) + pull
    sure = jax.random.permutation(jax.random.fold_in(key, 3), rows)[jnp.arange(count) % rows]
    tickets = jnp.where(jnp.arange(rows)[:, None] == sure[None, :], 1 << 14, tickets)
    priority = tickets * count + jnp.arange(count)
    return lax.top_k(priority.astype(jnp.int32), top)[1].astype(jnp.int32)


def centred(own_key, shape, width, limit, split=(), held_as=jnp.bfloat16):
    entries = width * jax.random.normal(own_key, shape, jnp.float32)
    if split:
        entries = entries * block_levels(own_key, shape, split, -0.22, 0.18)
    return jnp.clip(entries, -limit, limit).astype(held_as)


def setup_inputs(seed: int = 0) -> dict:
    seeds = jax.random.split(jax.random.key(seed), 13)
    decoder_input = centred(seeds[0], (SEQS, LEN, D), 1.0, 6.0, ((0, 8), (1, 4)))
    gain_attn = jnp.clip(1.0 + 0.1 * jax.random.normal(seeds[1], (D,), jnp.float32), 0.5, 1.5)
    query_weight = centred(seeds[2], (D, QH * HD), D ** -0.5, 0.1875)
    keyval_weight = centred(seeds[3], (D, 2 * KVH * HD), D ** -0.5, 0.1875)
    output_weight = centred(seeds[4], (QH * HD, D), HD ** -0.5, 0.75)
    gain_moe = jnp.clip(1.0 + 0.1 * jax.random.normal(seeds[5], (D,), jnp.float32), 0.5, 1.5)
    w_router = centred(seeds[6], (D, EXPERTS), 0.015625, 0.09375)
    w_gateup = centred(seeds[7], (EXPERTS, D, 2 * FF), D ** -0.5, 0.1875, ((0, 2),))
    w_down = centred(seeds[8], (EXPERTS, FF, D), (FF // 8) ** -0.5, 0.75, ((0, 2),))
    top_idx = different_ones(seeds[9], SEQS * LEN, EXPERTS, TOPK, 2048).reshape((SEQS, LEN, TOPK))
    slot_order = jax.vmap(lambda own: jax.random.permutation(own, SPAN))(jax.random.split(seeds[10], SEQS * N_CONTEXT)).reshape((SEQS, N_CONTEXT, SPAN)).astype(jnp.int32)
    cotangent = centred(seeds[11], (SEQS, LEN, D), 1.0, 6.0, ((0, 8), (1, 4)))
    return {"decoder_input": decoder_input, "gain_attn": gain_attn, "query_weight": query_weight, "keyval_weight": keyval_weight, "output_weight": output_weight, "gain_moe": gain_moe, "w_router": w_router, "w_gateup": w_gateup, "w_down": w_down, "top_idx": top_idx, "slot_order": slot_order, "cotangent": cotangent}


@jax.custom_vjp
def low(v):
    return lax.optimization_barrier(v.astype(jnp.bfloat16)).astype(jnp.float32)

@jax.custom_vjp
def reduced_backward(v):
    return v

def low_keep(v):
    return (low(v), None)

def low_pass(kept, grad):
    return (grad,)

def back_keep(v):
    return (v, None)

def back_low(kept, grad):
    return (low(grad),)
low.defvjp(low_keep, low_pass)
reduced_backward.defvjp(back_keep, back_low)
EPSILON = 1e-06
MASKED = -1e+30
FULL_PRECISION = lax.Precision.HIGHEST

def rms_norm(tensor, gain):
    inverse = lax.rsqrt(lax.optimization_barrier(jnp.mean(tensor * tensor, axis=-1, keepdims=True)) + EPSILON)
    return tensor * inverse * gain

def rotary_tables(offset, length, head_size):
    half_size = head_size // 2
    places = (offset + jnp.arange(length)).astype(jnp.float32)
    frequency = 10000.0 ** (-jnp.arange(half_size).astype(jnp.float32) * 2.0 / head_size)
    angles = places[:, None] * frequency[None, :]
    return (jnp.cos(angles)[:, None, :], jnp.sin(angles)[:, None, :])

def rotate(tensor, cos_table, sin_table):
    half_size = tensor.shape[-1] // 2
    first_half = tensor[..., :half_size]
    second_half = tensor[..., half_size:]
    return jnp.concatenate([first_half * cos_table - second_half * sin_table, second_half * cos_table + first_half * sin_table], axis=-1)

def attend(sequence_item):
    queries, keyval = sequence_item
    kv_half = KVH * HD
    grouped = queries.reshape(LEN, KVH, QH // KVH, HD)
    key_rows = keyval[:, :kv_half].reshape(LEN, KVH, HD)
    value_rows = keyval[:, kv_half:].reshape(LEN, KVH, HD)
    scores = reduced_backward(jnp.einsum('qhgd,khd->hgqk', grouped, key_rows, precision=FULL_PRECISION) * HD ** (-0.5))
    blocks = jnp.arange(LEN) // BLOCK
    allowed = (blocks[None, :] <= blocks[:, None])[None, None]
    weights = low(jax.nn.softmax(jnp.where(allowed, scores, MASKED), axis=-1))
    attended = jnp.einsum('hgqk,khd->qhgd', weights, value_rows, precision=FULL_PRECISION)
    return attended.reshape(LEN, QH * HD)

def slot_places(chosen_ids, rank_order):
    chosen_hot = (chosen_ids[:, :, None] == jnp.arange(EXPERTS)[None, None, :]).astype(jnp.int32)
    earlier = (rank_order[None, :] < rank_order[:, None]).astype(jnp.int32)
    before_count = jnp.dot(earlier, lax.optimization_barrier(jnp.sum(chosen_hot, axis=1)))
    slot_index = lax.optimization_barrier(jnp.sum(before_count[:, None, :] * chosen_hot, axis=2))
    kept_pair = slot_index < CAP
    target = jnp.where(kept_pair, chosen_ids * CAP + slot_index, EXPERTS * CAP)
    return (target, kept_pair)

def mixture(token_rows, chosen_ids, rank_order, w_router, w_gateup, w_down):
    logits = reduced_backward(jnp.dot(token_rows, w_router, precision=FULL_PRECISION))
    gates = jax.nn.softmax(jnp.take_along_axis(logits, chosen_ids, axis=1), axis=-1)
    target, kept_pair = slot_places(chosen_ids, rank_order)
    filled = jnp.zeros((EXPERTS * CAP, D), jnp.float32).at[target.reshape(-1)].set(jnp.repeat(token_rows, TOPK, axis=0), mode='drop')
    filled = reduced_backward(filled.reshape(EXPERTS, CAP, D))
    both = reduced_backward(jnp.einsum('ecd,edf->ecf', filled, w_gateup, precision=FULL_PRECISION))
    hidden = low(jax.nn.silu(both[..., :FF]) * both[..., FF:])
    expert_out = reduced_backward(low(jnp.einsum('ecf,efd->ecd', hidden, w_down, precision=FULL_PRECISION)))
    expert_out = expert_out.reshape(EXPERTS * CAP, D)
    picked = jnp.take(expert_out, jnp.minimum(target, EXPERTS * CAP - 1).reshape(-1), axis=0).reshape(SPAN, TOPK, D)
    gate_kept = jnp.where(kept_pair, gates, 0.0)
    return jnp.einsum('tk,tkd->td', gate_kept, picked, precision=FULL_PRECISION)

def layer(top_idx, slot_order, decoder_input, gain_attn, query_weight, keyval_weight, output_weight, gain_moe, w_router, w_gateup, w_down):
    cos_table, sin_table = rotary_tables(0, LEN, HD)
    kv_half = KVH * HD
    normed_rows = low(rms_norm(decoder_input, gain_attn))
    query_unrotated = reduced_backward(jnp.einsum('eqp,pn->eqn', normed_rows, query_weight, precision=FULL_PRECISION))
    keyval_unrotated = reduced_backward(jnp.einsum('eqp,pn->eqn', normed_rows, keyval_weight, precision=FULL_PRECISION))
    queries = low(rotate(query_unrotated.reshape(SEQS, LEN, QH, HD), cos_table, sin_table).reshape(SEQS, LEN, QH * HD))
    key_part = rotate(keyval_unrotated[..., :kv_half].reshape(SEQS, LEN, KVH, HD), cos_table, sin_table).reshape(SEQS, LEN, kv_half)
    keyval = low(jnp.concatenate([key_part, keyval_unrotated[..., kv_half:]], axis=-1))
    attention_output = lax.map(jax.checkpoint(attend), (queries, keyval))
    attention_output = reduced_backward(low(attention_output))
    residual_middle = decoder_input + reduced_backward(jnp.einsum('pmb,bw->pmw', attention_output, output_weight, precision=FULL_PRECISION))
    normed_moe = low(rms_norm(residual_middle, gain_moe))
    group_count = SEQS * N_CONTEXT

    def group_mixture(group_item):
        token_rows, chosen_ids, rank_order = group_item
        return mixture(token_rows, chosen_ids, rank_order, w_router, w_gateup, w_down)
    mixed = lax.map(jax.checkpoint(group_mixture), (normed_moe.reshape(group_count, SPAN, D), top_idx.reshape(group_count, SPAN, TOPK), slot_order.reshape(group_count, SPAN)))
    return residual_middle + mixed.reshape(SEQS, LEN, D)

def reference(decoder_input, gain_attn, query_weight, keyval_weight, output_weight, gain_moe, w_router, w_gateup, w_down, top_idx, slot_order, cotangent):
    floats = [tensor.astype(jnp.float32) for tensor in (decoder_input, gain_attn, query_weight, keyval_weight, output_weight, gain_moe, w_router, w_gateup, w_down)]
    result, pullback = jax.vjp(partial(layer, top_idx, slot_order), *floats)
    grads = pullback(cotangent.astype(jnp.float32))
    return (result.astype(jnp.bfloat16), grads[0].astype(jnp.bfloat16), grads[1], grads[2], grads[3], grads[4], grads[5], grads[6], grads[7], grads[8])
```

```python
import functools

import jax
import jax.numpy as jnp
from jax import lax
from jax.experimental import pallas as pl
from jax.experimental.pallas import tpu as pltpu
from jax.sharding import PartitionSpec as P

KVH = 8
HD = 64
FF = 512
EXPERTS = 32
TOPK = 8
BLOCK = 256
CAP = 160


EPSILON = 1e-06
MASKED = -1e30
VMEM_LIMIT = 56 * 1024 * 1024
F32 = jnp.float32
BF16 = jnp.bfloat16


def rotary_tables(offset, length, head_size):
    half_size = head_size // 2
    places = (offset + jnp.arange(length)).astype(jnp.float32)
    frequency = 10000.0 ** (-jnp.arange(half_size).astype(jnp.float32) * 2.0 / head_size)
    angles = places[:, None] * frequency[None, :]
    return (jnp.cos(angles)[:, None, :], jnp.sin(angles)[:, None, :])


def rotate(tensor, cos_table, sin_table):
    half_size = tensor.shape[-1] // 2
    first_half = tensor[..., :half_size]
    second_half = tensor[..., half_size:]
    return jnp.concatenate(
        [
            first_half * cos_table - second_half * sin_table,
            second_half * cos_table + first_half * sin_table,
        ],
        axis=-1,
    )


def norm_forward(tensor, gain):
    inverse = lax.rsqrt(jnp.mean(tensor * tensor, axis=-1, keepdims=True) + EPSILON)
    return (tensor * inverse * gain, inverse)


def norm_backward(tensor, inverse, gain, upstream):
    scaled = gain * upstream
    grad_gain = jnp.sum(upstream * tensor * inverse, axis=0)
    grad_tensor = inverse * scaled - tensor * inverse**3 * jnp.mean(
        tensor * scaled, axis=-1, keepdims=True
    )
    return (grad_tensor, grad_gain)


def hop(value, axis, stride):
    count = lax.axis_size(axis)
    return lax.ppermute(value, axis, [(i, i ^ stride) for i in range(count)])


def turn(value, axis, step):
    count = lax.axis_size(axis)
    return lax.ppermute(value, axis, [(i, (i + step) % count) for i in range(count)])


def core_hop(value):
    return hop(value, "dp", 1)


def x_hop(value):
    return hop(value, "dp", lax.axis_size("dp") // 2)


def add_low(*terms):
    total = terms[0].astype(F32)
    for term in terms[1:]:
        total = total + term.astype(F32)
    return total.astype(BF16)


def packed_rows(table, width):
    experts, tokens = table.shape
    parts = width // tokens
    return jnp.transpose(
        table.reshape(parts, experts // parts, tokens), (1, 0, 2)
    ).reshape(experts // parts, width)


def unpacked_rows(rows, tokens):
    count, width = rows.shape
    parts = width // tokens
    return jnp.transpose(rows.reshape(count, parts, tokens), (1, 0, 2)).reshape(
        count * parts, tokens
    )


def gather_groups(first, second):
    owners = lax.axis_size("experts")
    chips = [(first, second)]
    from_x = (x_hop(first), x_hop(second))
    from_y = [(turn(first, "experts", k), turn(second, "experts", k)) for k in range(1, owners)]
    chips.append(from_x)
    chips.extend(from_y)
    for k in range(1, owners):
        chips.append((x_hop(from_y[k - 1][0]), turn(from_x[1], "experts", k)))
    return [[chip, (core_hop(chip[0]), core_hop(chip[1]))] for chip in chips]


def return_groups(chips):
    owners = lax.axis_size("experts")
    sums = [None] * len(chips)
    order = list(range(owners + 1, 2 * owners)) + list(range(1, owners + 1)) + [0]
    for number in order:
        own, other = chips[number]
        sums[number] = [add_low(own[i], core_hop(other[i])) for i in range(2)]
    for k in range(1, owners):
        diagonal = sums[owners + k]
        sums[1 + k][0] = add_low(sums[1 + k][0], x_hop(diagonal[0]))
        sums[1][1] = add_low(sums[1][1], turn(diagonal[1], "experts", -k))
    result = []
    for i in range(2):
        total = sums[0][i].astype(F32) + x_hop(sums[1][i]).astype(F32)
        for k in range(1, owners):
            total = total + turn(sums[1 + k][i], "experts", -k).astype(F32)
        result.append(total)
    return result


def expert_place(expert, rows):
    return lax.div(expert, rows), lax.rem(expert, rows)


def picked_row(block, part, row, tokens):
    chosen = block[:, :tokens]
    for number in range(1, block.shape[1] // tokens):
        chosen = jnp.where(part == number, block[:, number * tokens : (number + 1) * tokens], chosen)
    places = lax.broadcasted_iota(jnp.int32, chosen.shape, 0)
    return jnp.sum(jnp.where(places == row, chosen, 0.0), axis=0, keepdims=True)


def dispatch_kernel(groups, own_experts, place_ref, *refs):
    sources = refs[: 4 * groups]
    xs_ref, gus_ref, table_ref = refs[-3:]
    half = sources[0].shape[0]
    tokens = 2 * half
    base = place_ref[0]
    for number in range(groups):
        x0, x1, u0, u1 = sources[4 * number : 4 * number + 4]
        gate_block = x1[half:, :].astype(F32)
        slot_block = u1[half:, :].astype(F32)
        picks = []
        gate_columns = []
        places = lax.broadcasted_iota(jnp.int32, (CAP, tokens), 0).astype(F32)
        for e in range(own_experts):
            part, row = expert_place(base + e, gate_block.shape[0])
            slot_row = picked_row(slot_block, part, row, tokens)
            gate_row = picked_row(gate_block, part, row, tokens)
            table_ref[number, e : e + 1, :] = slot_row
            table_ref[number, own_experts + e : own_experts + e + 1, :] = gate_row
            match = places == slot_row
            picks.append(jnp.where(match, 1.0, 0.0).astype(BF16))
            gate_columns.append(jnp.sum(jnp.where(match, gate_row, 0.0), axis=1, keepdims=True))
        pick = jnp.concatenate(picks, axis=0)
        left, right = pick[:, :half], pick[:, half:]
        rows = jnp.dot(left, x0[...], preferred_element_type=F32) + jnp.dot(
            right, x1[:half, :], preferred_element_type=F32
        )
        grads = jnp.dot(left, u0[...], preferred_element_type=F32) + jnp.dot(
            right, u1[:half, :], preferred_element_type=F32
        )
        for e in range(own_experts):
            span = slice(e * CAP, (e + 1) * CAP)
            xs_ref[e, number] = rows[span].astype(BF16)
            gus_ref[e, number] = (grads[span] * gate_columns[e]).astype(BF16)


def dispatch(place, pair, pairs, own_experts, rows_pieces, grad_pieces, earlier):
    groups = len(rows_pieces)
    half, width = rows_pieces[0][0].shape
    tokens = 2 * half
    operands = []
    for rows, grads in zip(rows_pieces, grad_pieces):
        operands += [rows[0], rows[1], grads[0], grads[1]]
    whole = lambda array: pl.BlockSpec(array.shape, lambda i, s: (0, 0))
    slots_shape = (own_experts, pairs * groups, CAP, width)
    table_shape = (pairs * groups, 2 * own_experts, tokens)
    slots_block = (own_experts, groups, CAP, width)
    out_specs = [
        pl.BlockSpec(slots_block, lambda i, s: (0, pair, 0, 0)),
        pl.BlockSpec(slots_block, lambda i, s: (0, pair, 0, 0)),
        pl.BlockSpec((groups, 2 * own_experts, tokens), lambda i, s: (pair, 0, 0)),
    ]
    in_specs = [whole(array) for array in operands]
    aliases = {}
    if earlier is not None:
        aliases = {1 + len(operands) + i: i for i in range(3)}
        in_specs += [pl.BlockSpec(memory_space=pl.ANY)] * 3
        operands = operands + list(earlier)
    flops = 2 * 2 * groups * own_experts * CAP * tokens * width
    return pl.pallas_call(
        functools.partial(dispatch_kernel, groups, own_experts),
        out_shape=[
            jax.ShapeDtypeStruct(slots_shape, BF16),
            jax.ShapeDtypeStruct(slots_shape, BF16),
            jax.ShapeDtypeStruct(table_shape, F32),
        ],
        grid_spec=pltpu.PrefetchScalarGridSpec(
            num_scalar_prefetch=1, grid=(1,), in_specs=in_specs, out_specs=out_specs
        ),
        input_output_aliases=aliases,
        compiler_params=pltpu.CompilerParams(vmem_limit_bytes=VMEM_LIMIT),
        cost_estimate=pl.CostEstimate(
            flops=flops, bytes_accessed=4 * groups * (tokens + own_experts * CAP) * width, transcendentals=0
        ),
        name="dispatch",
    )(place, *operands)


def experts_kernel(chunks, spans, place_ref, xs_ref, gus_ref, up_ref, down_ref, outs_ref, rows_ref, terms_ref,
                   send_ref, keep_ref, x_all, gu_all, grad_all, hidden_all, piece):
    step = pl.program_id(0)
    chunk = xs_ref.shape[1]
    ff = down_ref.shape[1]

    @pl.when(step < chunks)
    def _():
        x = xs_ref[0]
        gu = gus_ref[0]
        both = jnp.dot(x, up_ref[0], preferred_element_type=F32)
        gate_pre, up_pre = both[:, :ff], both[:, ff:]
        sigmoid = jax.nn.sigmoid(gate_pre)
        activated = gate_pre * sigmoid
        hidden = (activated * up_pre).astype(BF16)
        grad_hidden = lax.dot_general(
            gu, down_ref[0], (((1,), (1,)), ((), ())), preferred_element_type=F32
        )
        terms = jnp.sum(grad_hidden * hidden.astype(F32), axis=1, keepdims=True)
        terms_ref[...] = jnp.broadcast_to(terms, terms_ref.shape)
        outs_ref[...] = jnp.dot(hidden, down_ref[0], preferred_element_type=F32).astype(BF16)
        grad_gate = grad_hidden * up_pre * sigmoid * (1.0 + gate_pre * (1.0 - sigmoid))
        grad_both = jnp.concatenate(
            [grad_gate.astype(BF16), (grad_hidden * activated).astype(BF16)], axis=1
        )
        rows_ref[...] = lax.dot_general(
            grad_both, up_ref[0], (((1,), (1,)), ((), ())), preferred_element_type=F32
        ).astype(BF16)
        at = pl.ds(pl.multiple_of(step * chunk, chunk), chunk)
        x_all[at, :] = x
        gu_all[at, :] = gu
        grad_all[at, :] = grad_both
        hidden_all[at, :] = hidden

    @pl.when(step >= chunks)
    def _():
        number = step - chunks
        relative = lax.rem(number, 2) * 2 + jnp.where(number < 2, 1, 0)
        owner = lax.bitwise_xor(place_ref[1], relative)
        rows = piece.shape[0]
        columns = pl.ds(pl.multiple_of(owner * rows, rows), rows)
        over_rows = (((0,), (0,)), ((), ()))
        width = grad_all.shape[1]
        piece[:, :width] = lax.dot_general(
            x_all[:, columns], grad_all[...], over_rows, preferred_element_type=F32
        )
        piece[:, width:] = lax.dot_general(
            gu_all[:, columns], hidden_all[...], over_rows, preferred_element_type=F32
        )
        part = rows // spans

        def put(target):
            for near in range(spans):
                wanted = lax.bitwise_xor(place_ref[2], near)
                at = pl.ds(pl.multiple_of(wanted * part, part), part)
                target[0, near * part : (near + 1) * part, :] = piece[at, :].astype(BF16)

        @pl.when(number < 2)
        def _():
            put(send_ref)

        @pl.when(number >= 2)
        def _():
            put(keep_ref)


def experts_work(place, number, slots, slot_grads, w_gateup, w_down, contexts, spans):
    own_experts, total, width = slots.shape
    ff = w_down.shape[1]
    chunk = 256
    chunks = total // chunk
    rows = width // contexts
    place = place.at[0].add(number)
    half = contexts // 2
    row_block = lambda s, p: (jnp.minimum(s, chunks - 1), 0)
    slot_block = lambda s, p: (number, jnp.minimum(s, chunks - 1), 0)
    piece_width = w_gateup.shape[2] + ff
    flops = 2 * 3 * total * width * 3 * ff
    return pl.pallas_call(
        functools.partial(experts_kernel, chunks, spans),
        out_shape=[
            jax.ShapeDtypeStruct((total, width), BF16),
            jax.ShapeDtypeStruct((total, width), BF16),
            jax.ShapeDtypeStruct((total, 128), F32),
            jax.ShapeDtypeStruct((half, rows, piece_width), BF16),
            jax.ShapeDtypeStruct((half, rows, piece_width), BF16),
        ],
        grid_spec=pltpu.PrefetchScalarGridSpec(
            num_scalar_prefetch=1,
            grid=(chunks + contexts,),
            in_specs=[
                pl.BlockSpec((1, chunk, width), slot_block),
                pl.BlockSpec((1, chunk, width), slot_block),
                pl.BlockSpec((1,) + w_gateup.shape[1:], lambda s, p: (p[0], 0, 0)),
                pl.BlockSpec((1,) + w_down.shape[1:], lambda s, p: (p[0], 0, 0)),
            ],
            out_specs=[
                pl.BlockSpec((chunk, width), row_block),
                pl.BlockSpec((chunk, width), row_block),
                pl.BlockSpec((chunk, 128), row_block),
                pl.BlockSpec((1, rows, piece_width), lambda s, p: (jnp.clip(s - chunks, 0, half - 1), 0, 0)),
                pl.BlockSpec(
                    (1, rows, piece_width), lambda s, p: (jnp.clip(s - chunks - half, 0, half - 1), 0, 0)
                ),
            ],
            scratch_shapes=[
                pltpu.VMEM((total, width), BF16),
                pltpu.VMEM((total, width), BF16),
                pltpu.VMEM((total, 2 * ff), BF16),
                pltpu.VMEM((total, ff), BF16),
                pltpu.VMEM((rows, piece_width), F32),
            ],
        ),
        compiler_params=pltpu.CompilerParams(vmem_limit_bytes=VMEM_LIMIT),
        cost_estimate=pl.CostEstimate(
            flops=flops, bytes_accessed=8 * total * width + 12 * width * ff, transcendentals=total * ff
        ),
        name="experts",
    )(place, slots, slot_grads, w_gateup, w_down)


def combine_kernel(groups, own_experts, place_ref, table_ref, *refs):
    outs = refs[:own_experts]
    rows = refs[own_experts : 2 * own_experts]
    terms = refs[2 * own_experts : 3 * own_experts]
    results = refs[3 * own_experts :]
    tokens = table_ref.shape[2]
    half = tokens // 2
    over_rows = (((0,), (0,)), ((), ()))
    base = place_ref[0]
    for number in range(groups):
        mix0, mix1, row0, row1 = results[4 * number : 4 * number + 4]
        extra_rows = row1.shape[0] - half
        span = slice(number * CAP, (number + 1) * CAP)
        places = lax.broadcasted_iota(jnp.int32, (CAP, tokens), 0).astype(F32)
        extra_places = lax.broadcasted_iota(jnp.int32, (extra_rows, tokens), 0)
        picks, weighted = [], []
        extras = [jnp.zeros((extra_rows, tokens), F32) for _ in range(EXPERTS // extra_rows)]
        for e in range(own_experts):
            slot_row = table_ref[number, e : e + 1, :]
            gate_row = table_ref[number, own_experts + e : own_experts + e + 1, :]
            match = places == slot_row
            picks.append(jnp.where(match, 1.0, 0.0).astype(BF16))
            weighted.append(jnp.where(match, gate_row, 0.0).astype(BF16))
            term_row = jnp.sum(jnp.where(match, terms[e][span, 0:1], 0.0), axis=0, keepdims=True)
            part, row = expert_place(base + e, extra_rows)
            for k in range(len(extras)):
                extras[k] = jnp.where(
                    jnp.logical_and(extra_places == row, part == k), term_row, extras[k]
                )
        pick = jnp.concatenate(picks, axis=0)
        weights = jnp.concatenate(weighted, axis=0)
        out_block = jnp.concatenate([ref[span, :] for ref in outs], axis=0)
        row_block = jnp.concatenate([ref[span, :] for ref in rows], axis=0)
        mixture = lax.dot_general(weights, out_block, over_rows, preferred_element_type=F32)
        summed = lax.dot_general(pick, row_block, over_rows, preferred_element_type=F32)
        mix0[...] = mixture[:half].astype(BF16)
        mix1[...] = mixture[half:].astype(BF16)
        row0[...] = summed[:half].astype(BF16)
        row1[:half, :] = summed[half:].astype(BF16)
        for k, extra in enumerate(extras):
            row1[half:, k * tokens : (k + 1) * tokens] = extra.astype(BF16)


def combine(place, pair, groups, table, outs, rows, terms, extra_rows):
    own_experts = len(outs)
    tokens = table.shape[2]
    width = outs[0].shape[1]
    half = tokens // 2
    piece = lambda count: jax.ShapeDtypeStruct((count, width), BF16)
    out_shape = [piece(half), piece(half), piece(half), piece(half + extra_rows)] * groups
    slot_spec = pl.BlockSpec((groups * CAP, width), lambda i, s: (pair, 0))
    term_spec = pl.BlockSpec((groups * CAP, 128), lambda i, s: (pair, 0))
    results = pl.pallas_call(
        functools.partial(combine_kernel, groups, own_experts),
        out_shape=out_shape,
        grid_spec=pltpu.PrefetchScalarGridSpec(
            num_scalar_prefetch=1,
            grid=(1,),
            in_specs=[pl.BlockSpec((groups,) + table.shape[1:], lambda i, s: (pair, 0, 0))]
            + [slot_spec] * (2 * own_experts)
            + [term_spec] * own_experts,
            out_specs=[pl.BlockSpec(shape.shape, lambda i, s: (0, 0)) for shape in out_shape],
        ),
        compiler_params=pltpu.CompilerParams(vmem_limit_bytes=VMEM_LIMIT),
        cost_estimate=pl.CostEstimate(
            flops=4 * groups * own_experts * CAP * tokens * width,
            bytes_accessed=4 * groups * (tokens + own_experts * CAP) * width,
            transcendentals=0,
        ),
        name="combine",
    )(place, table, *outs, *rows, *terms)
    mixtures, sums = [], []
    for number in range(groups):
        mix0, mix1, row0, row1 = results[4 * number : 4 * number + 4]
        mixtures.append((mix0, mix1))
        sums.append((row0, row1))
    return mixtures, sums


def halved(matrix, axis, stride):
    bit = jnp.bitwise_and(lax.div(lax.axis_index(axis), stride), 1)
    kept = lax.dynamic_index_in_dim(matrix, bit, 0, keepdims=False)
    sent = lax.dynamic_index_in_dim(matrix, 1 - bit, 0, keepdims=False)
    return kept.astype(F32) + hop(sent.astype(BF16), axis, stride).astype(F32)


def summed_rows(matrix):
    rows, columns = matrix.shape
    owners, contexts, spans = (lax.axis_size(a) for a in ("experts", "context", "dp"))
    part = rows // (owners * contexts * spans)
    count, stride = spans, 1
    while count > 1:
        matrix = jnp.moveaxis(matrix.reshape(-1, count // 2, 2, part, columns), 2, 0)
        matrix = halved(matrix, "dp", stride).reshape(-1, columns)
        count, stride = count // 2, stride * 2
    count = owners
    while count > 1:
        matrix = halved(matrix.reshape(2, -1, columns), "experts", count // 2)
        count //= 2
    count, stride = contexts, 1
    while count > 1:
        matrix = jnp.moveaxis(matrix.reshape(count // 2, 2, part, columns), 1, 0)
        matrix = halved(matrix, "context", stride).reshape(-1, columns)
        count, stride = count // 2, stride * 2
    return matrix


def on_device(
    decoder_input,
    gain_attn,
    query_weight,
    keyval_weight,
    output_weight,
    gain_moe,
    w_router,
    w_gateup,
    w_down,
    top_idx,
    slot_order,
    cotangent,
):
    owners, contexts, spans = (lax.axis_size(a) for a in ("experts", "context", "dp"))
    inputs = decoder_input[0].astype(jnp.float32)
    length = inputs.shape[0]
    width = inputs.shape[1]
    half = length // 2
    heads = query_weight.shape[1] // HD
    kv_width = keyval_weight.shape[1]
    kv_half = kv_width // 2
    grouped = heads // KVH
    scale = HD ** (-0.5)
    local_experts = w_gateup.shape[0]
    own_experts = local_experts // spans
    y_place, z_place, dp_place = (lax.axis_index(a) for a in ("experts", "context", "dp"))

    ids = top_idx[0].T
    chosen = jnp.any(ids[None, :, :] == jnp.arange(EXPERTS)[:, None, None], axis=1)
    rank_order = slot_order[0, 0]
    earlier = (rank_order[:, None] < rank_order[None, :]).astype(BF16)
    before = jnp.dot(chosen.astype(BF16), earlier, preferred_element_type=F32)
    kept = jnp.logical_and(chosen, before < CAP)
    slot_table = jnp.where(kept, before, -1.0)
    upstream_low = cotangent[0]
    upstream = upstream_low.astype(jnp.float32)
    upstream_groups = gather_groups(
        upstream_low[:half],
        jnp.concatenate([upstream_low[half:], packed_rows(slot_table, width).astype(BF16)], axis=0),
    )

    offset = z_place * length
    cos_table, sin_table = rotary_tables(offset, length, HD)
    normed_rows, inverse_attn = norm_forward(inputs, gain_attn)
    normed_low = normed_rows.astype(jnp.bfloat16)
    query_unrotated = jnp.dot(normed_low, query_weight, preferred_element_type=jnp.float32)
    keyval_unrotated = jnp.dot(normed_low, keyval_weight, preferred_element_type=jnp.float32)
    queries = (
        rotate(query_unrotated.reshape(length, heads, HD), cos_table, sin_table)
        .astype(jnp.bfloat16)
        .reshape(length, KVH, grouped, HD)
    )
    keys_turned = rotate(
        keyval_unrotated[:, :kv_half].reshape(length, KVH, HD), cos_table, sin_table
    ).reshape(length, kv_half)
    keyval = jnp.concatenate([keys_turned, keyval_unrotated[:, kv_half:]], axis=1).astype(
        jnp.bfloat16
    )
    query_block = (offset + jnp.arange(length)) // BLOCK

    def block_scores(block_rows, block_start):
        keys_part = block_rows[:, :kv_half].reshape(BLOCK, KVH, HD)
        values_part = block_rows[:, kv_half:].reshape(BLOCK, KVH, HD)
        scores = (
            jnp.einsum("qhgd,khd->hgqk", queries, keys_part, preferred_element_type=jnp.float32)
            * scale
        )
        allowed = (block_start // BLOCK <= query_block)[None, None, :, None]
        return (jnp.where(allowed, scores, MASKED), allowed, keys_part, values_part)

    start_state = (
        jnp.full((KVH, grouped, length), MASKED, jnp.float32),
        jnp.zeros((KVH, grouped, length), jnp.float32),
        jnp.zeros((length, KVH, grouped, HD), jnp.float32),
    )
    blocks = lax.all_gather(keyval, "context", axis=0, tiled=True).reshape(-1, BLOCK, kv_width)

    def attend_step(state_now, block_item):
        running_max, running_sum, weighted = state_now
        block_rows, number = block_item
        scores, allowed, keys_part, values_part = block_scores(block_rows, number * BLOCK)
        new_max = jnp.maximum(running_max, jnp.max(scores, axis=-1))
        weights = jnp.where(allowed, jnp.exp(scores - new_max[..., None]), 0.0)
        factor = jnp.exp(running_max - new_max)
        running_sum = running_sum * factor + jnp.sum(weights, axis=-1)
        update = jnp.einsum(
            "hgqk,khd->qhgd",
            weights.astype(jnp.bfloat16),
            values_part,
            preferred_element_type=jnp.float32,
        )
        weighted = weighted * jnp.transpose(factor, (2, 0, 1))[..., None] + update
        return ((new_max, running_sum, weighted), None)

    running_max, running_sum, weighted = lax.scan(
        attend_step, start_state, (blocks, jnp.arange(blocks.shape[0]))
    )[0]
    log_total = running_max + jnp.log(running_sum)
    attention_output = weighted / jnp.transpose(running_sum, (2, 0, 1))[..., None]
    attn_low = attention_output.reshape(length, heads * HD).astype(jnp.bfloat16)
    residual_middle = inputs + jnp.dot(attn_low, output_weight, preferred_element_type=jnp.float32)
    normed_moe, inverse_moe = norm_forward(residual_middle, gain_moe)
    moe_low = normed_moe.astype(jnp.bfloat16)
    logits = lax.dot_general(
        w_router, moe_low, (((0,), (1,)), ((), ())), preferred_element_type=jnp.float32
    )
    top_logit = jnp.max(jnp.where(chosen, logits, MASKED), axis=0, keepdims=True)
    raised = jnp.where(chosen, jnp.exp(logits - top_logit), 0.0)
    gates = raised / jnp.sum(raised, axis=0, keepdims=True)

    moe_groups = gather_groups(
        moe_low[:half],
        jnp.concatenate([moe_low[half:], packed_rows(gates, width).astype(BF16)], axis=0),
    )
    extra_rows = EXPERTS * length // width
    first_expert = y_place * local_experts + dp_place * own_experts
    place = jnp.stack([first_expert]).astype(jnp.int32)
    pairs = len(moe_groups)
    state = None
    for pair in range(pairs):
        state = dispatch(
            place, pair, pairs, own_experts, moe_groups[pair], upstream_groups[pair], state
        )
    slots, slot_grads, table = state
    total = slots.shape[1] * CAP
    slots = slots.reshape(own_experts, total, width)
    slot_grads = slot_grads.reshape(own_experts, total, width)
    work_place = jnp.stack([dp_place * own_experts, z_place, dp_place]).astype(jnp.int32)
    outs, rows, terms, finals = [], [], [], []
    for number in range(own_experts):
        out, row, term, sent, keep = experts_work(
            work_place, number, slots, slot_grads, w_gateup, w_down, contexts, spans
        )
        outs.append(out)
        rows.append(row)
        terms.append(term)
        arrived = hop(sent, "context", 1)
        near = add_low(keep[0], arrived[0])
        far = add_low(keep[1], arrived[1])
        finals.append(add_low(near, hop(far, "context", 2)))
    mixtures, sums = [None] * pairs, [None] * pairs
    for pair in reversed(range(pairs)):
        mixtures[pair], sums[pair] = combine(
            place, pair, 2, table, outs, rows, terms, extra_rows
        )
    row_total = return_groups(sums)
    grad_gate_terms = unpacked_rows(row_total[1][half:], length)
    grad_moe_rows = jnp.concatenate([row_total[0], row_total[1][:half]], axis=0)
    grad_selected = grad_gate_terms - gates * jnp.sum(grad_gate_terms, axis=0, keepdims=True)
    grad_logits = grad_selected.astype(BF16)
    router_local = lax.dot_general(
        moe_low, grad_logits, (((0,), (1,)), ((), ())), preferred_element_type=jnp.float32
    )
    grad_moe_rows = grad_moe_rows + lax.dot_general(
        grad_logits, w_router, (((0,), (1,)), ((), ())), preferred_element_type=jnp.float32
    )
    grad_middle, gain_moe_local = norm_backward(
        residual_middle, inverse_moe, gain_moe, grad_moe_rows
    )
    grad_middle = grad_middle + upstream
    mixed = jnp.concatenate(return_groups(mixtures), axis=0)
    layer_output = (residual_middle + mixed).astype(jnp.bfloat16)[None]

    grad_attn = grad_middle.astype(jnp.bfloat16)
    out_local = jnp.einsum("tf,td->fd", attn_low, grad_attn, preferred_element_type=jnp.float32)
    grad_heads = (
        jnp.einsum("td,fd->tf", grad_attn, output_weight, preferred_element_type=jnp.float32)
        .astype(jnp.bfloat16)
        .reshape(length, KVH, grouped, HD)
    )
    row_terms = jnp.transpose(
        jnp.sum(grad_heads.astype(jnp.float32) * attention_output, axis=-1), (1, 2, 0)
    )
    grad_queries = jnp.zeros((length, KVH, grouped, HD), jnp.float32)

    def back_step(grad_now, block_item):
        block_rows, number = block_item
        scores, allowed, keys_part, values_part = block_scores(block_rows, number * BLOCK)
        probs = jnp.where(allowed, jnp.exp(scores - log_total[..., None]), 0.0)
        grad_values = jnp.einsum(
            "hgqk,qhgd->khd",
            probs.astype(jnp.bfloat16),
            grad_heads,
            preferred_element_type=jnp.float32,
        )
        grad_probs = jnp.einsum(
            "qhgd,khd->hgqk", grad_heads, values_part, preferred_element_type=jnp.float32
        )
        grad_scores = (probs * (grad_probs - row_terms[..., None])).astype(jnp.bfloat16)
        grad_now = grad_now + scale * jnp.einsum(
            "hgqk,khd->qhgd", grad_scores, keys_part, preferred_element_type=jnp.float32
        )
        grad_keys = scale * jnp.einsum(
            "hgqk,qhgd->khd", grad_scores, queries, preferred_element_type=jnp.float32
        )
        return (
            grad_now,
            jnp.concatenate(
                [grad_keys.reshape(BLOCK, kv_half), grad_values.reshape(BLOCK, kv_half)], axis=1
            ),
        )

    grad_queries, block_grads = lax.scan(
        back_step, grad_queries, (blocks, jnp.arange(blocks.shape[0]))
    )
    grad_keyvals = block_grads.reshape(-1, kv_width)
    grad_keyval_own = lax.psum_scatter(
        grad_keyvals.astype(jnp.bfloat16), "context", scatter_dimension=0, tiled=True
    ).astype(jnp.float32)
    grad_query_pre = (
        rotate(grad_queries.reshape(length, heads, HD), cos_table, -sin_table)
        .reshape(length, heads * HD)
        .astype(jnp.bfloat16)
    )
    grad_keys_pre = rotate(
        grad_keyval_own[:, :kv_half].reshape(length, KVH, HD), cos_table, -sin_table
    ).reshape(length, kv_half)
    grad_keyval_pre = jnp.concatenate([grad_keys_pre, grad_keyval_own[:, kv_half:]], axis=1).astype(
        jnp.bfloat16
    )
    query_local = jnp.einsum(
        "td,tf->df", normed_low, grad_query_pre, preferred_element_type=jnp.float32
    )
    keyval_local = jnp.einsum(
        "td,tf->df", normed_low, grad_keyval_pre, preferred_element_type=jnp.float32
    )
    grad_normed = jnp.einsum(
        "tf,df->td", grad_query_pre, query_weight, preferred_element_type=jnp.float32
    )
    grad_normed = grad_normed + jnp.einsum(
        "tf,df->td", grad_keyval_pre, keyval_weight, preferred_element_type=jnp.float32
    )
    grad_inputs, gain_attn_local = norm_backward(inputs, inverse_attn, gain_attn, grad_normed)
    grad_input = (grad_inputs + grad_middle).astype(jnp.bfloat16)[None]

    column = lambda vector, filled: jnp.pad(vector[:, None], ((0, 0), (0, filled - 1)))
    early = summed_rows(
        jnp.concatenate([out_local, router_local, column(gain_moe_local, 128 - EXPERTS)], axis=1)
    )
    late = summed_rows(
        jnp.concatenate([query_local, keyval_local, column(gain_attn_local, 128)], axis=1)
    )
    grad_out = early[:, :width]
    grad_router = early[:, width : width + EXPERTS]
    grad_gain_moe = early[:, width + EXPERTS]
    grad_query = late[:, : query_local.shape[1]]
    grad_keyval = late[:, query_local.shape[1] : -128]
    grad_gain_attn = late[:, -128]

    stacked = jnp.stack(finals)
    part = stacked.shape[1] // spans
    across = x_hop(stacked[:, 2 * part :])
    beside = core_hop(jnp.concatenate([stacked[:, part : 2 * part], across[:, part:]], axis=1))
    near_blocks = jnp.stack(
        [stacked[:, :part], beside[:, :part], across[:, :part], beside[:, part:]]
    )
    arranged = jnp.concatenate(
        [
            lax.dynamic_index_in_dim(near_blocks, jnp.bitwise_xor(dp_place, b), 0, keepdims=False)
            for b in range(spans)
        ],
        axis=0,
    ).astype(F32)
    grad_gateup = arranged[:, :, : w_gateup.shape[2]]
    grad_down = jnp.transpose(arranged[:, :, w_gateup.shape[2] :], (0, 2, 1))
    return (
        layer_output,
        grad_input,
        grad_gain_attn,
        grad_query,
        grad_keyval,
        grad_out,
        grad_gain_moe,
        grad_router,
        grad_gateup,
        grad_down,
    )


def solution(mesh):
    in_specs = (
        P(("experts", "dp"), "context", None),
        P(),
        P(),
        P(),
        P(),
        P(),
        P(),
        P("experts", None, None),
        P("experts", None, None),
        P(("experts", "dp"), "context", None),
        P(("experts", "dp"), "context", None),
        P(("experts", "dp"), "context", None),
    )
    out_specs = (
        P(("experts", "dp"), "context", None),
        P(("experts", "dp"), "context", None),
        P(("experts", "context", "dp")),
        P(("experts", "context", "dp"), None),
        P(("experts", "context", "dp"), None),
        P(("experts", "context", "dp"), None),
        P(("experts", "context", "dp")),
        P(("experts", "context", "dp"), None),
        P("experts", ("context", "dp"), None),
        P("experts", None, ("context", "dp")),
    )
    return jax.shard_map(
        on_device, mesh=mesh, in_specs=in_specs, out_specs=out_specs, check_vma=False
    )
```

```python
import functools

import jax
import jax.numpy as jnp
from jax import lax
from jax.experimental import pallas as pl
from jax.experimental.pallas import tpu as pltpu
from jax.sharding import PartitionSpec as P

KVH = 8
HD = 64
FF = 512
EXPERTS = 32
TOPK = 8
BLOCK = 256
CAP = 160


EPSILON = 1e-06
MASKED = -1e30
VMEM_LIMIT = 56 * 1024 * 1024
SMALL = pl.CostEstimate(flops=1, bytes_accessed=1, transcendentals=0)
F32 = jnp.float32
BF16 = jnp.bfloat16


def rotary_tables(offset, length, head_size):
    half_size = head_size // 2
    places = (offset + jnp.arange(length)).astype(jnp.float32)
    frequency = 10000.0 ** (-jnp.arange(half_size).astype(jnp.float32) * 2.0 / head_size)
    angles = places[:, None] * frequency[None, :]
    return (jnp.cos(angles)[:, None, :], jnp.sin(angles)[:, None, :])


def rotate(tensor, cos_table, sin_table):
    half_size = tensor.shape[-1] // 2
    first_half = tensor[..., :half_size]
    second_half = tensor[..., half_size:]
    return jnp.concatenate(
        [
            first_half * cos_table - second_half * sin_table,
            second_half * cos_table + first_half * sin_table,
        ],
        axis=-1,
    )


def norm_forward(tensor, gain):
    inverse = lax.rsqrt(jnp.mean(tensor * tensor, axis=-1, keepdims=True) + EPSILON)
    return (tensor * inverse * gain, inverse)


def norm_backward(tensor, inverse, gain, upstream):
    scaled = gain * upstream
    grad_gain = upstream * tensor * inverse
    grad_tensor = inverse * scaled - tensor * inverse**3 * jnp.mean(
        tensor * scaled, axis=-1, keepdims=True
    )
    return (grad_tensor, grad_gain)


def hop(value, axis, stride):
    count = lax.axis_size(axis)
    return lax.ppermute(value, axis, [(i, i ^ stride) for i in range(count)])


def turn(value, axis, step):
    count = lax.axis_size(axis)
    return lax.ppermute(value, axis, [(i, (i + step) % count) for i in range(count)])


def core_hop(value):
    return hop(value, "dp", 1)


def x_hop(value):
    return hop(value, "dp", lax.axis_size("dp") // 2)


def add_low(*terms):
    total = terms[0].astype(F32)
    for term in terms[1:]:
        total = total + term.astype(F32)
    return total.astype(BF16)


def packed_rows(table, width):
    experts, tokens = table.shape
    parts = width // tokens
    return jnp.transpose(
        table.reshape(parts, experts // parts, tokens), (1, 0, 2)
    ).reshape(experts // parts, width)


def unpacked_rows(rows, tokens):
    count, width = rows.shape
    parts = width // tokens
    return jnp.transpose(rows.reshape(count, parts, tokens), (1, 0, 2)).reshape(
        count * parts, tokens
    )


def after(value, *others):
    return lax.optimization_barrier((value, others))[0]


def gather_near(whole):
    owners = lax.axis_size("experts")
    return [x_hop(whole)] + [turn(whole, "experts", k) for k in range(1, owners)]


def gather_far(near, half):
    owners = lax.axis_size("experts")
    return [(x_hop(near[k][:half]), turn(near[0][half:], "experts", k)) for k in range(1, owners)]


def return_far(sums):
    owners = lax.axis_size("experts")
    return [
        (x_hop(sums[owners + k][0]), turn(sums[owners + k][1], "experts", -k)) for k in range(1, owners)
    ]


def far_parts(far, group):
    if group == 1:
        return [(1, pieces[1]) for pieces in far]
    return [(0, far[group - 2][0])]


def return_near(sums):
    owners = lax.axis_size("experts")
    return [x_hop(sums[1])] + [turn(sums[1 + k], "experts", -k) for k in range(1, owners)]


def return_total(own, arrivals):
    total = own.astype(F32)
    for piece in arrivals:
        total = total + piece.astype(F32)
    return total


def picked_row(block, expert, tokens):
    rows = block.shape[0]
    part, row = lax.div(expert, rows), lax.rem(expert, rows)
    chosen = block[:, :tokens]
    for number in range(1, block.shape[1] // tokens):
        chosen = jnp.where(part == number, block[:, number * tokens : (number + 1) * tokens], chosen)
    places = lax.broadcasted_iota(jnp.int32, chosen.shape, 0)
    return jnp.sum(jnp.where(places == row, chosen, 0.0), axis=0, keepdims=True)


def expert_of(place_ref, number, pair_experts):
    own = pair_experts // 2
    return place_ref[0] + number if number < own else place_ref[1] + number - own


def one_hot(slot_row):
    places = lax.broadcasted_iota(jnp.int32, (CAP, slot_row.shape[1]), 0).astype(F32)
    return places == slot_row


def dispatch_kernel(pair_experts, half, pieces, with_gates, place_ref, *refs):
    if pieces == 1:
        first, second = refs[0].at[:half], refs[0].at[half:]
    else:
        first, second = refs[:2]
    if with_gates:
        slots_ref = refs[pieces]
        out_ref, gate_ref, table_ref = refs[-3:]
    else:
        out_ref, table_ref = refs[-2:]
    tokens = 2 * half
    extra = second[half:, :].astype(F32)
    picks = []
    for e in range(pair_experts):
        row = picked_row(extra, expert_of(place_ref, e, pair_experts), tokens)
        table_ref[0, e : e + 1, :] = row
        if with_gates:
            match = one_hot(slots_ref[0, e : e + 1, :])
            gates = jnp.sum(jnp.where(match, row, 0.0), axis=1, keepdims=True)
            gate_ref[e, 0] = jnp.broadcast_to(gates, gate_ref.shape[2:])
        else:
            match = one_hot(row)
        picks.append(jnp.where(match, 1.0, 0.0).astype(BF16))
    pick = jnp.concatenate(picks, axis=0)
    rows = jnp.dot(pick[:, :half], first[...], preferred_element_type=F32) + jnp.dot(
        pick[:, half:], second[:half, :], preferred_element_type=F32
    )
    for e in range(pair_experts):
        out_ref[e, 0] = rows[e * CAP : (e + 1) * CAP].astype(BF16)


def dispatch(place, group, groups, pair_experts, half, pieces, slots, earlier):
    width = pieces[0].shape[1]
    tokens = 2 * half
    whole = lambda array: pl.BlockSpec(array.shape, lambda i, s: (0, 0))
    operands = list(pieces)
    in_specs = [whole(array) for array in operands]
    slots_shape = (pair_experts, groups, CAP, width)
    gate_shape = (pair_experts, groups, CAP, 128)
    table_shape = (groups, pair_experts, tokens)
    table_spec = pl.BlockSpec((1, pair_experts, tokens), lambda i, s: (group, 0, 0))
    out_specs = [pl.BlockSpec((pair_experts, 1, CAP, width), lambda i, s: (0, group, 0, 0))]
    out_shape = [jax.ShapeDtypeStruct(slots_shape, BF16)]
    if slots is not None:
        operands.append(slots)
        in_specs.append(table_spec)
        out_specs.append(pl.BlockSpec((pair_experts, 1, CAP, 128), lambda i, s: (0, group, 0, 0)))
        out_shape.append(jax.ShapeDtypeStruct(gate_shape, F32))
    out_specs.append(table_spec)
    out_shape.append(jax.ShapeDtypeStruct(table_shape, F32))
    aliases = {}
    if earlier is not None:
        aliases = {1 + len(operands) + i: i for i in range(len(earlier))}
        in_specs += [pl.BlockSpec(memory_space=pl.ANY)] * len(earlier)
        operands = operands + list(earlier)
    return pl.pallas_call(
        functools.partial(dispatch_kernel, pair_experts, half, len(pieces), slots is not None),
        out_shape=out_shape,
        grid_spec=pltpu.PrefetchScalarGridSpec(
            num_scalar_prefetch=1, grid=(1,), in_specs=in_specs, out_specs=out_specs
        ),
        input_output_aliases=aliases,
        compiler_params=pltpu.CompilerParams(vmem_limit_bytes=VMEM_LIMIT),
        cost_estimate=SMALL,
        name="dispatch",
    )(place, *operands)


def experts_kernel(slot, chunk, spans, own, place_ref, *refs):
    xs_ref, us_ref, gates_ref, up_ref, down_ref = refs[:5]
    refs = refs[5:]
    arrived_refs = ()
    if own:
        arrived_refs, refs = refs[:2], refs[2:]
    outs_ref, rows_ref, terms_ref = refs[:3]
    pieces_refs = refs[3:5]
    refs = refs[5:]
    x_all, gu_all, gate_all, up_all, down_all, out_all, row_all, term_all, grad_all, hidden_all = refs[:10]
    piece, pieces_all, *arrived_all, load_sems, store_sems = refs[10:]
    total = x_all.shape[0]
    ff = down_all.shape[0]
    sources = [
        (xs_ref.at[slot], x_all),
        (up_ref.at[place_ref[0]], up_all),
        (us_ref.at[slot], gu_all),
        (gates_ref.at[slot], gate_all),
        (down_ref.at[place_ref[0]], down_all),
    ]
    for i, arrived_ref in enumerate(arrived_refs):
        count = arrived_ref.shape[0]
        sources.append((arrived_ref, arrived_all[0].at[pl.ds(i * count, count)]))
    loads = [
        pltpu.make_async_copy(source, target, load_sems.at[i]) for i, (source, target) in enumerate(sources)
    ]
    for load in loads:
        load.start()
    stores = []

    def store(source, target):
        stores.append(pltpu.make_async_copy(source, target, store_sems.at[len(stores)]))
        stores[-1].start()

    loads[0].wait()
    loads[1].wait()
    for number in range(total // chunk):
        span = slice(number * chunk, (number + 1) * chunk)
        at = pl.ds(number * chunk, chunk)
        both = jnp.dot(x_all[span], up_all[...], preferred_element_type=F32)
        if number == 0:
            for load in loads[2:5]:
                load.wait()
        gate_pre, up_pre = both[:, :ff], both[:, ff:]
        gu = (gu_all[span].astype(F32) * gate_all[span, 0:1]).astype(BF16)
        gu_all[span] = gu
        sigmoid = jax.nn.sigmoid(gate_pre)
        activated = gate_pre * sigmoid
        hidden = (activated * up_pre).astype(BF16)
        hidden_all[span] = hidden
        grad_hidden = lax.dot_general(gu, down_all[...], NT, preferred_element_type=F32)
        out_all[span] = jnp.dot(hidden, down_all[...], preferred_element_type=F32).astype(BF16)
        store(out_all.at[at], outs_ref.at[at])
        terms = jnp.sum(grad_hidden * hidden.astype(F32), axis=1, keepdims=True)
        term_all[span] = jnp.broadcast_to(terms, (chunk, term_all.shape[1]))
        store(term_all.at[at], terms_ref.at[at])
        grad_gate = grad_hidden * up_pre * sigmoid * (1.0 + gate_pre * (1.0 - sigmoid))
        grad_both = jnp.concatenate(
            [grad_gate.astype(BF16), (grad_hidden * activated).astype(BF16)], axis=1
        )
        grad_all[span] = grad_both
        row_all[span] = lax.dot_general(
            grad_both, up_all[...], NT, preferred_element_type=F32
        ).astype(BF16)
        store(row_all.at[at], rows_ref.at[at])
    for load in loads[5:]:
        load.wait()
    contexts = pieces_all.shape[0]
    half = contexts // 2
    rows = piece.shape[0]
    part = rows // spans
    over_rows = (((0,), (0,)), ((), ()))
    width = grad_all.shape[1]
    for number in range(contexts):
        relative = (number % half) * 2 + (1 if number < half else 0)
        owner = lax.bitwise_xor(place_ref[1], relative)
        columns = pl.ds(pl.multiple_of(owner * rows, rows), rows)
        piece[:, :width] = lax.dot_general(
            x_all[:, columns], grad_all[...], over_rows, preferred_element_type=F32
        )
        piece[:, width:] = lax.dot_general(
            gu_all[:, columns], hidden_all[...], over_rows, preferred_element_type=F32
        )
        for near in range(spans):
            wanted = lax.bitwise_xor(place_ref[2], near)
            value = piece[pl.ds(pl.multiple_of(wanted * part, part), part), :]
            to = slice(near * part, (near + 1) * part)
            if own:
                value = value + arrived_all[0][number, to, :].astype(F32)
            pieces_all[number, to, :] = value.astype(BF16)
        store(pieces_all.at[number], pieces_refs[number // half].at[number % half])
    for copy in stores:
        copy.wait()


def experts_work(place, slot, slots, slot_grads, slot_gates, w_gateup, w_down, contexts, spans, arrived):
    total, width = slots.shape[1:]
    ff = w_down.shape[1]
    chunk = 2 * CAP
    rows = width // contexts
    half = contexts // 2
    own = arrived is not None
    piece_width = w_gateup.shape[2] + ff
    piece_shape = lambda count: jax.ShapeDtypeStruct((count, rows, piece_width), BF16)
    operands = [slots, slot_grads, slot_gates, w_gateup, w_down]
    out_shape = [
        jax.ShapeDtypeStruct((total, width), BF16),
        jax.ShapeDtypeStruct((total, width), BF16),
        jax.ShapeDtypeStruct((total, 128), F32),
    ]
    scratch = [
        pltpu.VMEM((total, width), BF16),
        pltpu.VMEM((total, width), BF16),
        pltpu.VMEM((total, 128), F32),
        pltpu.VMEM(w_gateup.shape[1:], BF16),
        pltpu.VMEM(w_down.shape[1:], BF16),
        pltpu.VMEM((total, width), BF16),
        pltpu.VMEM((total, width), BF16),
        pltpu.VMEM((total, 128), F32),
        pltpu.VMEM((total, 2 * ff), BF16),
        pltpu.VMEM((total, ff), BF16),
        pltpu.VMEM((rows, piece_width), F32),
        pltpu.VMEM((contexts, rows, piece_width), BF16),
    ]
    out_shape += [piece_shape(half), piece_shape(half)]
    if own:
        operands += list(arrived)
        scratch.append(pltpu.VMEM((contexts, rows, piece_width), BF16))
    scratch.append(pltpu.SemaphoreType.DMA((7,)))
    scratch.append(pltpu.SemaphoreType.DMA((3 * (total // chunk) + contexts,)))
    return pl.pallas_call(
        functools.partial(experts_kernel, slot, chunk, spans, own),
        out_shape=out_shape,
        grid_spec=pltpu.PrefetchScalarGridSpec(
            num_scalar_prefetch=1,
            grid=(1,),
            in_specs=[pl.BlockSpec(memory_space=pl.ANY)] * len(operands),
            out_specs=[pl.BlockSpec(memory_space=pl.ANY)] * len(out_shape),
            scratch_shapes=scratch,
        ),
        compiler_params=pltpu.CompilerParams(vmem_limit_bytes=VMEM_LIMIT),
        cost_estimate=SMALL,
        name="experts",
    )(place, *operands)


def combine_kernel(pair_experts, half, extra_rows, added, results, with_terms, place_ref, slots_ref, *refs):
    scale_ref, terms = None, ()
    if with_terms:
        values = refs[:pair_experts]
        terms = refs[pair_experts : 2 * pair_experts]
        refs = refs[2 * pair_experts :]
    else:
        scale_ref = refs[0]
        values = refs[1 : 1 + pair_experts]
        refs = refs[1 + pair_experts :]
    added_refs = refs[: len(added)]
    if results == 1:
        first, second = refs[-1].at[:half], refs[-1].at[half:]
    else:
        first, second = refs[-2:]
    tokens = 2 * half
    extra_places = lax.broadcasted_iota(jnp.int32, (max(extra_rows, 8), tokens), 0)
    picks = []
    extras = [jnp.zeros(extra_places.shape, F32) for _ in range(first.shape[1] // tokens)]
    for e in range(pair_experts):
        match = one_hot(slots_ref[0, e : e + 1, :])
        if with_terms:
            picks.append(jnp.where(match, 1.0, 0.0).astype(BF16))
            term_row = jnp.sum(jnp.where(match, terms[e][:, 0:1], 0.0), axis=0, keepdims=True)
            expert = expert_of(place_ref, e, pair_experts)
            part, row = lax.div(expert, extra_rows), lax.rem(expert, extra_rows)
            for k in range(len(extras)):
                extras[k] = jnp.where(
                    jnp.logical_and(extra_places == row, part == k), term_row, extras[k]
                )
        else:
            picks.append(jnp.where(match, scale_ref[0, e : e + 1, :], 0.0).astype(BF16))
    pick = jnp.concatenate(picks, axis=0)
    block = jnp.concatenate([ref[...] for ref in values], axis=0)
    summed = lax.dot_general(pick, block, (((0,), (0,)), ((), ())), preferred_element_type=F32)
    halves = [summed[:half], summed[half:]]
    for piece, ref in zip(added, added_refs):
        halves[piece] = halves[piece] + ref[:half, :].astype(F32)
        if with_terms and piece == 1:
            extras = [
                extra + ref[half:, k * tokens : (k + 1) * tokens].astype(F32) for k, extra in enumerate(extras)
            ]
    first[...] = halves[0].astype(BF16)
    second[:half, :] = halves[1].astype(BF16)
    if with_terms:
        for k, extra in enumerate(extras):
            second[half:, k * tokens : (k + 1) * tokens] = extra.astype(BF16)


def combine(place, group, results, slot_table, scales, values, terms, extra_rows, parts=()):
    pair_experts = len(values)
    tokens = slot_table.shape[2]
    width = values[0].shape[1]
    half = tokens // 2
    table_spec = pl.BlockSpec((1,) + slot_table.shape[1:], lambda i, s: (group, 0, 0))
    whole = lambda array: pl.BlockSpec(array.shape, lambda i, s: (0, 0))
    in_specs = [table_spec]
    operands = [slot_table]
    if terms is None:
        in_specs.append(table_spec)
        operands.append(scales)
        extra_rows = 0
    in_specs += [pl.BlockSpec((CAP, width), lambda i, s: (group, 0))] * pair_experts
    operands += values
    if terms is not None:
        in_specs += [pl.BlockSpec((CAP, 128), lambda i, s: (group, 0))] * pair_experts
        operands += terms
    in_specs += [whole(array) for _, array in parts]
    operands += [array for _, array in parts]
    counts = [tokens + extra_rows] if results == 1 else [half, half + extra_rows]
    out_shape = [jax.ShapeDtypeStruct((count, width), BF16) for count in counts]
    result = pl.pallas_call(
        functools.partial(
            combine_kernel,
            pair_experts,
            half,
            extra_rows,
            [piece for piece, _ in parts],
            results,
            terms is not None,
        ),
        out_shape=out_shape,
        grid_spec=pltpu.PrefetchScalarGridSpec(
            num_scalar_prefetch=1,
            grid=(1,),
            in_specs=in_specs,
            out_specs=[whole(shape) for shape in out_shape],
        ),
        compiler_params=pltpu.CompilerParams(vmem_limit_bytes=VMEM_LIMIT),
        cost_estimate=SMALL,
        name="combine",
    )(place, *operands)
    return result[0] if results == 1 else result


NT = (((1,), (1,)), ((), ()))


def attend_kernel(first, last, distance, place_ref, q_ref, k_ref, v_ref, *refs):
    if first:
        state_in, stat_in = None, None
    else:
        state_in, stat_in = refs[:2]
        refs = refs[2:]
    state_ref, stat_ref = refs[:2]
    keys_count = k_ref.shape[0]
    length = q_ref.shape[0]
    heads = q_ref.shape[1] // HD
    grouped = heads // (k_ref.shape[1] // HD)

    def pieces():
        if first:
            return [(slice(b * BLOCK, (b + 1) * BLOCK), slice(0, (b + 1) * BLOCK)) for b in range(length // BLOCK)]
        return [(slice(0, length), slice(0, keys_count))]

    def work():
        turned_values = jnp.transpose(v_ref[...])
        for head in range(heads):
            kv_head = head // grouped
            own = slice(head * HD, (head + 1) * HD)
            shared = slice(kv_head * HD, (kv_head + 1) * HD)
            for q_span, k_span in pieces():
                scores = lax.dot_general(
                    k_ref[k_span, shared], q_ref[q_span, own], NT, preferred_element_type=F32
                )
                top = jnp.max(scores, axis=0, keepdims=True)
                if not first:
                    before = stat_in[0, head : head + 1, q_span]
                    top = jnp.maximum(top, before)
                weights = jnp.exp(scores - top)
                total = jnp.sum(weights, axis=0, keepdims=True)
                update = jnp.dot(
                    turned_values[shared, k_span], weights.astype(BF16), preferred_element_type=F32
                )
                if not first:
                    factor = jnp.exp(before - top)
                    total = total + factor * stat_in[0, heads + head : heads + head + 1, q_span]
                    update = update + factor * state_in[own, q_span]
                stat_ref[0, head : head + 1, q_span] = top
                stat_ref[0, heads + head : heads + head + 1, q_span] = total
                state_ref[own, q_span] = update

    if first:
        work()
    else:
        pl.when(place_ref[0] >= distance)(work)

        @pl.when(place_ref[0] < distance)
        def _():
            state_ref[...] = state_in[...]
            stat_ref[...] = stat_in[...]

    if last:
        low_ref = refs[2]
        for head in range(heads):
            own = slice(head * HD, (head + 1) * HD)
            total = stat_ref[0, heads + head : heads + head + 1, :]
            state_ref[own, :] = state_ref[own, :] / total
            stat_ref[0, head : head + 1, :] = stat_ref[0, head : head + 1, :] + jnp.log(total)
        low_ref[...] = jnp.transpose(state_ref[...]).astype(BF16)


def attend_chunk(place, distance, last, queries, keyval, state):
    length, width = queries.shape
    kv_half = keyval.shape[1] // 2
    pairs = kv_half // 128
    q_columns = width // pairs
    heads = q_columns // HD
    first = state is None
    q_spec = pl.BlockSpec((length, q_columns), lambda i, s: (0, i))
    state_spec = pl.BlockSpec((q_columns, length), lambda i, s: (i, 0))
    stat_spec = pl.BlockSpec((1, 2 * heads, length), lambda i, s: (i, 0, 0))
    in_specs = [
        q_spec,
        pl.BlockSpec((keyval.shape[0], 128), lambda i, s: (0, i)),
        pl.BlockSpec((keyval.shape[0], 128), lambda i, s: (0, pairs + i)),
    ]
    operands = [queries, keyval, keyval]
    out_specs = [state_spec, stat_spec]
    out_shape = [
        jax.ShapeDtypeStruct((width, length), F32),
        jax.ShapeDtypeStruct((pairs, 2 * heads, length), F32),
    ]
    if not first:
        in_specs += [state_spec, stat_spec]
        operands += list(state)
    if last:
        out_specs.append(q_spec)
        out_shape.append(jax.ShapeDtypeStruct((length, width), BF16))
    work = length * keyval.shape[0] * width
    return pl.pallas_call(
        functools.partial(attend_kernel, first, last, distance),
        out_shape=out_shape,
        grid_spec=pltpu.PrefetchScalarGridSpec(
            num_scalar_prefetch=1, grid=(pairs,), in_specs=in_specs, out_specs=out_specs
        ),
        compiler_params=pltpu.CompilerParams(vmem_limit_bytes=VMEM_LIMIT),
        cost_estimate=SMALL,
        name="attend",
    )(place, *operands)


def back_kernel(first, own_chunk, distance, arrives, place_ref, q_ref, k_ref, v_ref, grad_ref, state_ref, stat_ref, *refs):
    arrived_ref = None
    if arrives:
        arrived_ref, refs = refs[0], refs[1:]
    dq_in = None
    if not first:
        dq_in, refs = refs[0], refs[1:]
    dkv_ref, dq_ref = refs
    length = q_ref.shape[0]
    keys_count = k_ref.shape[0]
    heads = q_ref.shape[1] // HD
    kv_heads = k_ref.shape[1] // HD
    grouped = heads // kv_heads

    def work():
        turned_keys = jnp.transpose(k_ref[...])
        turned_grads = jnp.transpose(grad_ref[...].astype(F32))
        if own_chunk:
            pieces = [
                (slice(b * BLOCK, (b + 1) * BLOCK), slice(0, (b + 1) * BLOCK)) for b in range(length // BLOCK)
            ]
        else:
            pieces = [(slice(0, length), slice(0, keys_count))]
        for kv_head in range(kv_heads):
            shared = slice(kv_head * HD, (kv_head + 1) * HD)
            sums = {}
            for head in range(kv_head * grouped, (kv_head + 1) * grouped):
                own = slice(head * HD, (head + 1) * HD)
                row_term = jnp.sum(turned_grads[own, :] * state_ref[own, :], axis=0, keepdims=True)
                for q_span, k_span in pieces:
                    q = q_ref[q_span, own]
                    grad = grad_ref[q_span, own]
                    scores = lax.dot_general(k_ref[k_span, shared], q, NT, preferred_element_type=F32)
                    probs = jnp.exp(scores - stat_ref[0, head : head + 1, q_span])
                    grad_probs = lax.dot_general(v_ref[k_span, shared], grad, NT, preferred_element_type=F32)
                    grad_scores = (probs * (grad_probs - row_term[:, q_span])).astype(BF16)
                    grad_values = jnp.dot(probs.astype(BF16), grad, preferred_element_type=F32)
                    grad_keys = jnp.dot(grad_scores, q, preferred_element_type=F32)
                    blocks = grad_keys.shape[0] // BLOCK
                    for b in range(blocks):
                        part = slice(b * BLOCK, (b + 1) * BLOCK)
                        if b in sums:
                            sums[b] = (sums[b][0] + grad_keys[part], sums[b][1] + grad_values[part])
                        else:
                            sums[b] = (grad_keys[part], grad_values[part])
                    grad_q = jnp.dot(turned_keys[shared, k_span], grad_scores, preferred_element_type=F32)
                    if first:
                        dq_ref[own, q_span] = grad_q
                    else:
                        dq_ref[own, q_span] = dq_in[own, q_span] + grad_q
            for b, pair in sums.items():
                part = slice(b * BLOCK, (b + 1) * BLOCK)
                for i in range(2):
                    value = pair[i]
                    if arrives:
                        value = value + arrived_ref[i, part, shared].astype(F32)
                    dkv_ref[i, part, shared] = value.astype(BF16)

    if own_chunk:
        work()
    else:
        pl.when(place_ref[0] >= distance)(work)

        @pl.when(place_ref[0] < distance)
        def _():
            dkv_ref[...] = jnp.zeros_like(dkv_ref)
            dq_ref[...] = jnp.zeros_like(dq_ref) if first else dq_in[...]


def back_chunk(place, distance, queries, keyval, grad_heads, state, stats, arrived, dq):
    length, width = queries.shape
    kv_half = keyval.shape[1] // 2
    pairs = kv_half // 128
    q_columns = width // pairs
    heads = q_columns // HD
    q_spec = pl.BlockSpec((length, q_columns), lambda i, s: (0, i))
    state_spec = pl.BlockSpec((q_columns, length), lambda i, s: (i, 0))
    stat_spec = pl.BlockSpec((1, 2 * heads, length), lambda i, s: (i, 0, 0))
    dkv_spec = pl.BlockSpec((2, keyval.shape[0], 128), lambda i, s: (0, 0, i))
    in_specs = [
        q_spec,
        pl.BlockSpec((keyval.shape[0], 128), lambda i, s: (0, i)),
        pl.BlockSpec((keyval.shape[0], 128), lambda i, s: (0, pairs + i)),
        q_spec,
        state_spec,
        stat_spec,
    ]
    operands = [queries, keyval, keyval, grad_heads, state, stats]
    if arrived is not None:
        in_specs.append(dkv_spec)
        operands.append(arrived)
    if dq is not None:
        in_specs.append(state_spec)
        operands.append(dq)
    work = length * keyval.shape[0] * width
    return pl.pallas_call(
        functools.partial(back_kernel, dq is None, distance == 0, distance, arrived is not None),
        out_shape=[
            jax.ShapeDtypeStruct((2, keyval.shape[0], kv_half), BF16),
            jax.ShapeDtypeStruct((width, length), F32),
        ],
        grid_spec=pltpu.PrefetchScalarGridSpec(
            num_scalar_prefetch=1, grid=(pairs,), in_specs=in_specs, out_specs=[dkv_spec, state_spec]
        ),
        compiler_params=pltpu.CompilerParams(vmem_limit_bytes=VMEM_LIMIT),
        cost_estimate=SMALL,
        name="back",
    )(place, *operands)


TN = (((0,), (0,)), ((), ()))


def sum_hops():
    owners, contexts, spans = (lax.axis_size(a) for a in ("experts", "context", "dp"))
    hops = []
    for axis, count in (("dp", spans), ("experts", owners), ("context", contexts)):
        bit = 1
        while bit < count:
            hops.append((axis, bit))
            bit *= 2
    return hops


def put_arranged(value, columns, place_ref, plan, plain, arranged, keep_ref, send_ref):
    contexts, spans, masks = plan
    part = value.shape[0] // len(masks)
    half = value.shape[0] // 2
    width = value.shape[1]
    plain[:, :width] = value
    for number, (owner_mask, context_mask, span_mask) in enumerate(masks):
        block = (
            lax.bitwise_xor(place_ref[0], owner_mask) * contexts
            + lax.bitwise_xor(place_ref[1], context_mask)
        ) * spans + lax.bitwise_xor(place_ref[2], span_mask)
        source = pl.ds(pl.multiple_of(block * part, part), part)
        arranged[number * part : (number + 1) * part, :width] = plain[source, :width]
    keep_ref[:, columns] = arranged[:half, :width].astype(BF16)
    send_ref[:, columns] = arranged[half:, :width].astype(BF16)


def sum_plan():
    contexts, spans = lax.axis_size("context"), lax.axis_size("dp")
    hops = sum_hops()
    masks = []
    for number in range(2 ** len(hops)):
        mask = {"experts": 0, "context": 0, "dp": 0}
        for i, (axis, bit) in enumerate(hops):
            if (number >> (len(hops) - 1 - i)) & 1:
                mask[axis] |= bit
        masks.append((mask["experts"], mask["context"], mask["dp"]))
    return contexts, spans, masks


def summed(pair):
    keep, send = pair
    for i, (axis, bit) in enumerate(sum_hops()):
        total = keep.astype(F32) + hop(send, axis, bit).astype(F32)
        rows = total.shape[0] // 2
        if i + 1 == len(sum_hops()):
            return total
        keep, send = total[:rows], total[rows:].astype(BF16)


def turned_back(rows, cos, sin):
    parts = []
    for head in range(rows.shape[0] // HD):
        first = rows[head * HD : head * HD + HD // 2]
        second = rows[head * HD + HD // 2 : (head + 1) * HD]
        parts += [first * cos + second * sin, second * cos - first * sin]
    return jnp.concatenate(parts, axis=0)


STEP = 256


def step_columns():
    step = pl.program_id(0)
    return step, pl.ds(pl.multiple_of(step * STEP, STEP), STEP)


def out_grad_kernel(plan, steps, place_ref, low_ref, grad_ref, moe_ref, logits_ref, gain_ref, keep_ref, send_ref,
                    plain, arranged):
    step, columns = step_columns()

    @pl.when(step < steps)
    def _():
        value = lax.dot_general(low_ref[...], grad_ref[...], TN, preferred_element_type=F32)
        put_arranged(value, columns, place_ref, plan, plain, arranged, keep_ref, send_ref)

    @pl.when(step == steps)
    def _():
        lanes = lax.broadcasted_iota(jnp.int32, logits_ref.shape, 1)
        ones = jnp.where(lanes == EXPERTS, 1.0, 0.0).astype(BF16)
        value = lax.dot_general(moe_ref[...], logits_ref[...], TN, preferred_element_type=F32)
        value = value + lax.dot_general(gain_ref[...], ones, TN, preferred_element_type=F32)
        put_arranged(value, slice(steps * STEP, steps * STEP + 128), place_ref, plan, plain, arranged, keep_ref, send_ref)


def out_grad(place, attn_low, grad_attn, moe_low, grad_logits, gain_terms):
    length, rows = attn_low.shape
    width = grad_attn.shape[1]
    steps = width // STEP
    whole = lambda array: pl.BlockSpec(array.shape, lambda i, s: (0, 0))
    shape = jax.ShapeDtypeStruct((rows // 2, width + 128), BF16)
    return pl.pallas_call(
        functools.partial(out_grad_kernel, sum_plan(), steps),
        out_shape=[shape, shape],
        grid_spec=pltpu.PrefetchScalarGridSpec(
            num_scalar_prefetch=1,
            grid=(steps + 1,),
            in_specs=[
                whole(attn_low),
                pl.BlockSpec((length, STEP), lambda i, s: (0, jnp.minimum(i, steps - 1))),
                whole(moe_low),
                whole(grad_logits),
                whole(gain_terms),
            ],
            out_specs=[whole(shape), whole(shape)],
            scratch_shapes=[pltpu.VMEM((rows, STEP), F32)] * 2,
        ),
        compiler_params=pltpu.CompilerParams(vmem_limit_bytes=VMEM_LIMIT),
        cost_estimate=SMALL,
        name="out_grad",
    )(place, attn_low, grad_attn, moe_low, grad_logits, gain_terms)


def query_grad_kernel(plan, scale, place_ref, dq_ref, cos_ref, sin_ref, low_ref, weight_ref, keep_ref, send_ref,
                      normed_ref, plain, arranged):
    step, columns = step_columns()
    turned = turned_back(dq_ref[...] * scale, cos_ref[...], sin_ref[...])
    low = jnp.transpose(turned).astype(BF16)
    value = lax.dot_general(low_ref[...], low, TN, preferred_element_type=F32)
    put_arranged(value, columns, place_ref, plan, plain, arranged, keep_ref, send_ref)
    part = lax.dot_general(low, weight_ref[...], NT, preferred_element_type=F32)

    @pl.when(step == 0)
    def _():
        normed_ref[...] = part

    @pl.when(step > 0)
    def _():
        normed_ref[...] = normed_ref[...] + part


def query_grad(place, grad_queries, cos, sin, normed_low, query_weight, scale):
    columns, length = grad_queries.shape
    rows = normed_low.shape[1]
    whole = lambda array: pl.BlockSpec(array.shape, lambda i, s: (0, 0))
    shape = jax.ShapeDtypeStruct((rows // 2, columns), BF16)
    normed = jax.ShapeDtypeStruct((length, rows), F32)
    return pl.pallas_call(
        functools.partial(query_grad_kernel, sum_plan(), scale),
        out_shape=[shape, shape, normed],
        grid_spec=pltpu.PrefetchScalarGridSpec(
            num_scalar_prefetch=1,
            grid=(columns // STEP,),
            in_specs=[
                pl.BlockSpec((STEP, length), lambda i, s: (i, 0)),
                whole(cos),
                whole(sin),
                whole(normed_low),
                pl.BlockSpec((rows, STEP), lambda i, s: (0, i)),
            ],
            out_specs=[whole(shape), whole(shape), whole(normed)],
            scratch_shapes=[pltpu.VMEM((rows, STEP), F32)] * 2,
        ),
        compiler_params=pltpu.CompilerParams(vmem_limit_bytes=VMEM_LIMIT),
        cost_estimate=SMALL,
        name="query_grad",
    )(place, grad_queries, cos, sin, normed_low, query_weight)


def keyval_grad_kernel(plan, steps, place_ref, own_ref, arrived_ref, cos_ref, sin_ref, low_ref, weight_ref, part_ref,
                       input_ref, inverse_ref, gain_ref, middle_ref, keep_ref, send_ref, result_ref, total,
                       plain, arranged):
    step, columns = step_columns()

    def take(low):
        value = lax.dot_general(low_ref[...], low, TN, preferred_element_type=F32)
        put_arranged(value, columns, place_ref, plan, plain, arranged, keep_ref, send_ref)
        part = lax.dot_general(low, weight_ref[...], NT, preferred_element_type=F32)

        @pl.when(step == 0)
        def _():
            total[...] = part_ref[...] + part

        @pl.when(step > 0)
        def _():
            total[...] = total[...] + part

    def sum_block():
        return own_ref[0].astype(F32) + arrived_ref[0].astype(F32)

    @pl.when(step < steps // 2)
    def _():
        turned = turned_back(jnp.transpose(sum_block()), cos_ref[...], sin_ref[...])
        take(jnp.transpose(turned).astype(BF16))

    @pl.when(jnp.logical_and(step >= steps // 2, step < steps))
    def _():
        take(sum_block().astype(BF16))

    @pl.when(step == steps)
    def _():
        grad = total[...]
        inputs = input_ref[...].astype(F32)
        inverse = inverse_ref[...][:, 0:1]
        scaled = gain_ref[...] * grad
        mean = jnp.mean(inputs * scaled, axis=1, keepdims=True)
        result = inverse * scaled - inputs * (inverse * inverse * inverse * mean) + middle_ref[...]
        result_ref[...] = result.astype(BF16)
        terms = (grad * inputs * inverse).astype(BF16)
        ones = jnp.ones((terms.shape[0], 128), BF16)
        value = lax.dot_general(terms, ones, TN, preferred_element_type=F32)
        put_arranged(value, slice(steps * STEP, steps * STEP + 128), place_ref, plan, plain, arranged, keep_ref, send_ref)


def keyval_grad(place, own, arrived, cos, sin, normed_low, keyval_weight, part, inputs, inverse, gain, grad_middle):
    length, rows = normed_low.shape
    width = keyval_weight.shape[1]
    steps = width // STEP
    half = steps // 2
    whole = lambda array: pl.BlockSpec(array.shape, lambda i, s: (0,) * len(array.shape))
    shape = jax.ShapeDtypeStruct((rows // 2, width + 128), BF16)
    result = jax.ShapeDtypeStruct((length, rows), BF16)
    at = lambda i: jnp.minimum(i, steps - 1)
    chunk = pl.BlockSpec((1, length, STEP), lambda i, s: (at(i) // half, 0, at(i) % half))
    return pl.pallas_call(
        functools.partial(keyval_grad_kernel, sum_plan(), steps),
        out_shape=[shape, shape, result],
        grid_spec=pltpu.PrefetchScalarGridSpec(
            num_scalar_prefetch=1,
            grid=(steps + 1,),
            in_specs=[
                chunk,
                chunk,
                whole(cos),
                whole(sin),
                whole(normed_low),
                pl.BlockSpec((rows, STEP), lambda i, s: (0, at(i))),
                whole(part),
                whole(inputs),
                whole(inverse),
                whole(gain),
                whole(grad_middle),
            ],
            out_specs=[whole(shape), whole(shape), whole(result)],
            scratch_shapes=[pltpu.VMEM((length, rows), F32)] + [pltpu.VMEM((rows, STEP), F32)] * 2,
        ),
        compiler_params=pltpu.CompilerParams(vmem_limit_bytes=VMEM_LIMIT),
        cost_estimate=SMALL,
        name="keyval_grad",
    )(place, own, arrived, cos, sin, normed_low, keyval_weight, part, inputs, inverse, gain, grad_middle)


def on_device(
    decoder_input,
    gain_attn,
    query_weight,
    keyval_weight,
    output_weight,
    gain_moe,
    w_router,
    w_gateup,
    w_down,
    top_idx,
    slot_order,
    cotangent,
):
    owners, contexts, spans = (lax.axis_size(a) for a in ("experts", "context", "dp"))
    inputs = decoder_input[0].astype(jnp.float32)
    length = inputs.shape[0]
    width = inputs.shape[1]
    half = length // 2
    heads = query_weight.shape[1] // HD
    kv_width = keyval_weight.shape[1]
    kv_half = kv_width // 2
    scale = HD ** (-0.5)
    local_experts = w_gateup.shape[0]
    own_experts = local_experts // spans
    y_place, z_place, dp_place = (lax.axis_index(a) for a in ("experts", "context", "dp"))

    ids = top_idx[0].T
    chosen = jnp.any(ids[None, :, :] == jnp.arange(EXPERTS)[:, None, None], axis=1)
    rank_order = slot_order[0, 0]
    earlier = (rank_order[:, None] < rank_order[None, :]).astype(BF16)
    before = jnp.dot(chosen.astype(BF16), earlier, preferred_element_type=F32)
    kept = jnp.logical_and(chosen, before < CAP)
    slot_table = jnp.where(kept, before, -1.0)
    upstream_low = cotangent[0]
    upstream = upstream_low.astype(jnp.float32)
    pair_experts = 2 * own_experts
    other_core = jnp.bitwise_xor(dp_place, 1)
    expert_place = jnp.stack(
        [
            y_place * local_experts + dp_place * own_experts,
            y_place * local_experts + other_core * own_experts,
        ]
    ).astype(jnp.int32)
    own_upstream = jnp.concatenate([upstream_low, packed_rows(slot_table, width).astype(BF16)], axis=0)

    offset = z_place * length
    cos_table, sin_table = rotary_tables(offset, length, HD)
    cos_rows, sin_rows = (jnp.transpose(table[:, 0]) for table in (cos_table, sin_table))
    sum_place = jnp.stack([y_place, z_place, dp_place]).astype(jnp.int32)
    normed_rows, inverse_attn = norm_forward(inputs, gain_attn)
    normed_low = normed_rows.astype(jnp.bfloat16)
    query_unrotated = jnp.dot(normed_low, query_weight, preferred_element_type=jnp.float32)
    keyval_unrotated = jnp.dot(normed_low, keyval_weight, preferred_element_type=jnp.float32)
    queries = (
        rotate(query_unrotated.reshape(length, heads, HD), cos_table, sin_table)
        .astype(jnp.bfloat16)
        .reshape(length, heads * HD)
    ) * jnp.asarray(scale, BF16)
    keys_turned = rotate(
        keyval_unrotated[:, :kv_half].reshape(length, KVH, HD), cos_table, sin_table
    ).reshape(length, kv_half)
    keyval = jnp.concatenate([keys_turned, keyval_unrotated[:, kv_half:]], axis=1).astype(
        jnp.bfloat16
    )
    z_index = jnp.stack([z_place]).astype(jnp.int32)
    near_upstream = gather_near(own_upstream)
    groups = 2 * owners
    upstream_groups = [(rows,) for rows in [own_upstream] + near_upstream]
    attended, grad_state = None, None
    chunk = keyval
    chunks = [keyval]
    for distance in range(contexts):
        arriving = None
        if distance < contexts - 1:
            upward = [(i, i + 1) for i in range(distance, contexts - 1)]
            arriving = lax.ppermute(chunk, "context", upward)
        attended = attend_chunk(
            z_index,
            distance,
            distance == contexts - 1,
            queries,
            chunk,
            None if attended is None else attended[:2],
        )
        if arriving is not None:
            if distance == 1 or contexts < 3:
                near_upstream = after(near_upstream, attended[1])
                upstream_groups = upstream_groups[:groups] + gather_far(near_upstream, half)
            for group in range(groups):
                if group * (contexts - 1) // groups == distance:
                    pieces = after(upstream_groups[group], attended[1])
                    grad_state = dispatch(
                        expert_place, group, groups, pair_experts, half, pieces, None, grad_state
                    )
            chunk, attended, grad_state = lax.optimization_barrier((arriving, attended, grad_state))
            chunks.append(chunk)
    attention_output, attention_stats, attn_low = attended
    slot_grads, slot_rows = grad_state
    residual_middle = inputs + jnp.dot(attn_low, output_weight, preferred_element_type=jnp.float32)
    normed_moe, inverse_moe = norm_forward(residual_middle, gain_moe)
    moe_low = normed_moe.astype(jnp.bfloat16)
    logits = lax.dot_general(
        w_router, moe_low, (((0,), (1,)), ((), ())), preferred_element_type=jnp.float32
    )
    top_logit = jnp.max(jnp.where(chosen, logits, MASKED), axis=0, keepdims=True)
    raised = jnp.where(chosen, jnp.exp(logits - top_logit), 0.0)
    gates = raised / jnp.sum(raised, axis=0, keepdims=True)

    own_rows = jnp.concatenate([moe_low, packed_rows(gates, width).astype(BF16)], axis=0)
    near_rows = gather_near(own_rows)

    def place_rows(group, pieces, row_state):
        return dispatch(
            expert_place, group, groups, pair_experts, half, pieces, slot_rows, row_state
        )

    row_state = place_rows(0, (own_rows,), None)
    near_rows, row_state = lax.optimization_barrier((near_rows, row_state))
    far_rows = gather_far(near_rows, half)
    for group, rows in enumerate(near_rows):
        row_state = place_rows(1 + group, (rows,), row_state)
    far_rows, row_state = lax.optimization_barrier((far_rows, row_state))
    for group, pieces in enumerate(far_rows):
        row_state = place_rows(1 + owners + group, pieces, row_state)
    slots, slot_gates, gate_rows = row_state
    extra_rows = EXPERTS * length // width
    total = groups * CAP
    slots = slots.reshape(pair_experts, total, width)
    slot_gates = slot_gates.reshape(pair_experts, total, 128)
    slot_grads = slot_grads.reshape(pair_experts, total, width)

    def work(number, own, gate, arrived):
        owner = dp_place if own else other_core
        work_place = jnp.stack([owner * own_experts + number, z_place, owner]).astype(jnp.int32)
        slot = number if own else own_experts + number
        return experts_work(
            work_place,
            slot,
            after(slots, gate),
            slot_grads,
            slot_gates,
            w_gateup,
            w_down,
            contexts,
            spans,
            arrived,
        )

    outs, rows, terms = ([None] * pair_experts for _ in range(3))
    crossing, sent, kept_sums, near_sums, crossed, finals = ([None] * own_experts for _ in range(6))

    def arrive_near(number, gate):
        arrived = after(sent[number], gate)
        near_sums[number] = add_low(kept_sums[number][0], arrived[0])
        crossed[number] = add_low(kept_sums[number][1], arrived[1])
        return crossed[number]

    def cross(number, gate):
        crossed[number] = hop(after(crossed[number], gate), "context", 2)

    def fold_near(number, gate):
        far = arrive_near(number, gate)
        cross(number, far)
        return far

    def exchanged(numbers):
        stacked = jnp.stack([finals[number] for number in numbers])
        part = stacked.shape[1] // spans
        across = x_hop(stacked[:, 2 * part :])
        beside = core_hop(jnp.concatenate([stacked[:, part : 2 * part], across[:, part:]], axis=1))
        return jnp.stack([stacked[:, :part], beside[:, :part], across[:, :part], beside[:, part:]])

    def fold_far(number, gate):
        finals[number] = add_low(near_sums[number], after(crossed[number], gate))
        return finals[number]

    order = [(0, False)]
    for number in range(own_experts):
        if number + 1 < own_experts:
            order.append((number + 1, False))
        order.append((number, True))
    gate = slot_gates
    for number, own in order:
        if own and number == 2:
            gate = fold_near(0, gate)
        slot = number if own else own_experts + number
        result = work(number, own, gate, crossing[number] if own else None)
        outs[slot], rows[slot], terms[slot] = result[:3]
        gate = result[2]
        if own:
            kept_sums[number] = result[4]
            sent[number] = hop(result[3], "context", 1)
        else:
            crossing[number] = (core_hop(result[3]), core_hop(result[4]))

    def near_then(number, value):
        return after(value, fold_near(number, value)) if number < own_experts else value

    def far_then(number, value):
        return after(value, fold_far(number, value)) if number < own_experts else value

    def row_part(group, parts=()):
        results = 2 if group > owners else 1
        return combine(expert_place, group, results, slot_rows, None, rows, terms, extra_rows, parts)

    def mixture_part(group, gate, parts=()):
        results = 2 if group > owners else 1
        return combine(
            expert_place, group, results, after(slot_rows, gate), gate_rows, outs, None, 0, parts
        )

    row_sums, mixtures = [None] * groups, [None] * groups
    far_groups = range(1 + owners, groups)
    near_groups = range(1, 1 + owners)
    for group in far_groups:
        row_sums[group] = row_part(group)
    far_sums = return_far(row_sums)
    row_sums[0] = row_part(0)
    gate = row_sums[0]
    for group in far_groups:
        mixtures[group] = mixture_part(group, gate)
        gate = mixtures[group]
    if own_experts < 3:
        gate = near_then(0, gate)
    gate = near_then(1, gate)
    far_sums = after(far_sums, gate)
    for group in near_groups:
        row_sums[group] = row_part(group, far_parts(far_sums, group))
    arrivals = return_near(row_sums)
    mixtures[0] = mixture_part(0, row_sums[near_groups[-1]])
    arrivals = after(arrivals, mixtures[0])
    arrivals = far_then(0, near_then(2, arrivals))
    row_total = return_total(row_sums[0], arrivals)
    row_total = far_then(1, row_total)
    grad_gate_terms = unpacked_rows(row_total[length:], length)
    grad_moe_rows = row_total[:length]
    grad_selected = grad_gate_terms - gates * jnp.sum(grad_gate_terms, axis=0, keepdims=True)
    grad_logits = grad_selected.astype(BF16)
    grad_moe_rows = grad_moe_rows + lax.dot_general(
        grad_logits, w_router, (((0,), (1,)), ((), ())), preferred_element_type=jnp.float32
    )
    grad_middle, gain_moe_terms = norm_backward(
        residual_middle, inverse_moe, gain_moe, grad_moe_rows
    )
    grad_middle = grad_middle + upstream
    grad_attn = grad_middle.astype(jnp.bfloat16)
    grad_heads = (
        jnp.einsum("td,fd->tf", grad_attn, output_weight, preferred_element_type=jnp.float32)
        .astype(jnp.bfloat16)
    )
    grad_heads = near_then(3, grad_heads)

    def back(distance, grad_heads, arrived, grad_queries):
        return back_chunk(
            z_index,
            distance,
            queries,
            chunks[distance],
            grad_heads,
            attention_output,
            attention_stats,
            arrived,
            grad_queries,
        )

    def down(distance, grad_chunk):
        pairs = [(i, i - 1) for i in range(distance, contexts)]
        return lax.ppermute(grad_chunk, "context", pairs)

    grad_chunk, grad_queries = back(contexts - 1, grad_heads, None, None)
    arrived = down(contexts - 1, grad_chunk)
    for group in far_groups:
        mixtures[group] = after(mixtures[group], grad_chunk)
    far_mixtures = return_far(mixtures)
    own_chunk, grad_queries = back(0, after(grad_heads, grad_chunk), None, grad_queries)
    grad_queries = far_then(2, grad_queries)
    for distance in reversed(range(1, contexts - 1)):
        arrived = after(arrived, grad_queries)
        grad_chunk, grad_queries = back(distance, grad_heads, arrived, grad_queries)
        arrived = down(distance, grad_chunk)
        if distance == contexts - 2:
            for group in near_groups:
                mixtures[group] = mixture_part(group, grad_chunk, far_parts(far_mixtures, group))
            mixture_arrivals = return_near(mixtures)
            grad_queries = far_then(3, grad_queries)
    for number in range(4, own_experts):
        grad_queries = far_then(number, near_then(number, grad_queries))
    arrived = after(arrived, grad_queries)
    mixed = return_total(mixtures[0], mixture_arrivals)
    layer_output = (residual_middle + mixed).astype(jnp.bfloat16)[None]
    early = summed(
        out_grad(
            sum_place,
            attn_low,
            after(grad_attn, own_chunk),
            moe_low,
            jnp.pad(grad_logits.T, ((0, 0), (0, 128 - EXPERTS))),
            gain_moe_terms.astype(BF16),
        )
    )
    *query_sums, grad_normed = query_grad(
        sum_place, grad_queries, cos_rows, sin_rows, normed_low, query_weight, scale
    )
    grad_query = summed(query_sums)
    *keyval_sums, grad_input = keyval_grad(
        sum_place,
        own_chunk,
        arrived,
        cos_rows,
        sin_rows,
        normed_low,
        keyval_weight,
        grad_normed,
        decoder_input[0],
        jnp.broadcast_to(inverse_attn, (length, 128)),
        gain_attn[None, :],
        grad_middle,
    )
    grad_input = grad_input[None]
    late = summed(keyval_sums)
    grad_out = early[:, :width]
    grad_router = early[:, width : width + EXPERTS]
    grad_gain_moe = early[:, width + EXPERTS]
    grad_keyval = late[:, :kv_width]
    grad_gain_attn = late[:, kv_width]

    near_blocks = exchanged(range(own_experts))
    arranged = jnp.concatenate(
        [
            lax.dynamic_index_in_dim(near_blocks, jnp.bitwise_xor(dp_place, b), 0, keepdims=False)
            for b in range(spans)
        ],
        axis=0,
    ).astype(F32)
    grad_gateup = arranged[:, :, : w_gateup.shape[2]]
    grad_down = jnp.transpose(arranged[:, :, w_gateup.shape[2] :], (0, 2, 1))
    return (
        layer_output,
        grad_input,
        grad_gain_attn,
        grad_query,
        grad_keyval,
        grad_out,
        grad_gain_moe,
        grad_router,
        grad_gateup,
        grad_down,
    )


def solution(mesh):
    in_specs = (
        P(("experts", "dp"), "context", None),
        P(),
        P(),
        P(),
        P(),
        P(),
        P(),
        P("experts", None, None),
        P("experts", None, None),
        P(("experts", "dp"), "context", None),
        P(("experts", "dp"), "context", None),
        P(("experts", "dp"), "context", None),
    )
    out_specs = (
        P(("experts", "dp"), "context", None),
        P(("experts", "dp"), "context", None),
        P(("experts", "context", "dp")),
        P(("experts", "context", "dp"), None),
        P(("experts", "context", "dp"), None),
        P(("experts", "context", "dp"), None),
        P(("experts", "context", "dp")),
        P(("experts", "context", "dp"), None),
        P("experts", ("context", "dp"), None),
        P("experts", None, ("context", "dp")),
    )
    return jax.shard_map(
        on_device, mesh=mesh, in_specs=in_specs, out_specs=out_specs, check_vma=False
    )
```

```python
import functools

import jax
import jax.numpy as jnp
from jax import lax
from jax.experimental import pallas as pl
from jax.experimental.pallas import tpu as pltpu
from jax.sharding import PartitionSpec as P

KVH = 8
HD = 64
FF = 512
EXPERTS = 32
TOPK = 8
BLOCK = 256
CAP = 160


EPSILON = 1e-06
MASKED = -1e30
VMEM_LIMIT = 56 * 1024 * 1024
SMALL = pl.CostEstimate(flops=1, bytes_accessed=1, transcendentals=0)
F32 = jnp.float32
NT = (((1,), (1,)), ((), ()))
TN = (((0,), (0,)), ((), ()))
BF16 = jnp.bfloat16


def rotary_tables(offset, length, head_size):
    half_size = head_size // 2
    places = (offset + jnp.arange(length)).astype(jnp.float32)
    frequency = 10000.0 ** (-jnp.arange(half_size).astype(jnp.float32) * 2.0 / head_size)
    angles = places[:, None] * frequency[None, :]
    return (jnp.cos(angles)[:, None, :], jnp.sin(angles)[:, None, :])


def rotate(tensor, cos_table, sin_table):
    half_size = tensor.shape[-1] // 2
    first_half = tensor[..., :half_size]
    second_half = tensor[..., half_size:]
    return jnp.concatenate(
        [
            first_half * cos_table - second_half * sin_table,
            second_half * cos_table + first_half * sin_table,
        ],
        axis=-1,
    )


def norm_forward(tensor, gain):
    inverse = lax.rsqrt(jnp.mean(tensor * tensor, axis=-1, keepdims=True) + EPSILON)
    return (tensor * inverse * gain, inverse)


def norm_backward(tensor, inverse, gain, upstream):
    scaled = gain * upstream
    grad_gain = upstream * tensor * inverse
    grad_tensor = inverse * scaled - tensor * inverse**3 * jnp.mean(
        tensor * scaled, axis=-1, keepdims=True
    )
    return (grad_tensor, grad_gain)


def hop(value, axis, stride):
    count = lax.axis_size(axis)
    return lax.ppermute(value, axis, [(i, i ^ stride) for i in range(count)])


def turn(value, axis, step):
    count = lax.axis_size(axis)
    return lax.ppermute(value, axis, [(i, (i + step) % count) for i in range(count)])


def core_hop(value):
    return hop(value, "dp", 1)


def x_hop(value):
    return hop(value, "dp", lax.axis_size("dp") // 2)


def add_low(*terms):
    total = terms[0].astype(F32)
    for term in terms[1:]:
        total = total + term.astype(F32)
    return total.astype(BF16)


def packed_rows(table, width):
    experts, tokens = table.shape
    parts = width // tokens
    return jnp.transpose(
        table.reshape(parts, experts // parts, tokens), (1, 0, 2)
    ).reshape(experts // parts, width)


def unpacked_rows(rows, tokens):
    count, width = rows.shape
    parts = width // tokens
    return jnp.transpose(rows.reshape(count, parts, tokens), (1, 0, 2)).reshape(
        count * parts, tokens
    )


def after(value, *others):
    return lax.optimization_barrier((value, others))[0]


def gather_near(whole):
    owners = lax.axis_size("experts")
    return [x_hop(whole)] + [turn(whole, "experts", k) for k in range(1, owners)]


def gather_far(near, half):
    owners = lax.axis_size("experts")
    return [(x_hop(near[k][:half]), turn(near[0][half:], "experts", k)) for k in range(1, owners)]


def return_far(sums):
    owners = lax.axis_size("experts")
    return [
        (x_hop(sums[owners + k][0]), turn(sums[owners + k][1], "experts", -k)) for k in range(1, owners)
    ]


def far_parts(far, group):
    if group == 1:
        return [(1, pieces[1]) for pieces in far]
    return [(0, far[group - 2][0])]


def return_near(sums):
    owners = lax.axis_size("experts")
    return [x_hop(sums[1])] + [turn(sums[1 + k], "experts", -k) for k in range(1, owners)]


def return_total(own, arrivals):
    total = own.astype(F32)
    for piece in arrivals:
        total = total + piece.astype(F32)
    return total


def picked_row(block, expert, tokens):
    rows = block.shape[0]
    part, row = lax.div(expert, rows), lax.rem(expert, rows)
    chosen = block[:, :tokens]
    for number in range(1, block.shape[1] // tokens):
        chosen = jnp.where(part == number, block[:, number * tokens : (number + 1) * tokens], chosen)
    places = lax.broadcasted_iota(jnp.int32, chosen.shape, 0)
    return jnp.sum(jnp.where(places == row, chosen, 0.0), axis=0, keepdims=True)


def expert_of(place_ref, number, pair_experts):
    own = pair_experts // 2
    return place_ref[0] + number if number < own else place_ref[1] + number - own


def one_hot(slot_row):
    places = lax.broadcasted_iota(jnp.int32, (CAP, slot_row.shape[1]), 0).astype(F32)
    return places == slot_row


def dispatch_kernel(pair_experts, half, pieces, with_gates, place_ref, *refs):
    if pieces == 1:
        first, second = refs[0].at[:half], refs[0].at[half:]
    else:
        first, second = refs[:2]
    if with_gates:
        slots_ref = refs[pieces]
        out_ref, gate_ref, table_ref = refs[-3:]
    else:
        out_ref, table_ref = refs[-2:]
    tokens = 2 * half
    extra = second[half:, :].astype(F32)
    picks = []
    for e in range(pair_experts):
        row = picked_row(extra, expert_of(place_ref, e, pair_experts), tokens)
        table_ref[0, e : e + 1, :] = row
        if with_gates:
            match = one_hot(slots_ref[0, e : e + 1, :])
            gates = jnp.sum(jnp.where(match, row, 0.0), axis=1, keepdims=True)
            gate_ref[e, 0] = jnp.broadcast_to(gates, gate_ref.shape[2:])
        else:
            match = one_hot(row)
        picks.append(jnp.where(match, 1.0, 0.0).astype(BF16))
    pick = jnp.concatenate(picks, axis=0)
    rows = jnp.dot(pick[:, :half], first[...], preferred_element_type=F32) + jnp.dot(
        pick[:, half:], second[:half, :], preferred_element_type=F32
    )
    for e in range(pair_experts):
        out_ref[e, 0] = rows[e * CAP : (e + 1) * CAP].astype(BF16)


def dispatch(place, group, groups, pair_experts, half, pieces, slots, earlier):
    width = pieces[0].shape[1]
    tokens = 2 * half
    whole = lambda array: pl.BlockSpec(array.shape, lambda i, s: (0, 0))
    operands = list(pieces)
    in_specs = [whole(array) for array in operands]
    slots_shape = (pair_experts, groups, CAP, width)
    gate_shape = (pair_experts, groups, CAP, 128)
    table_shape = (groups, pair_experts, tokens)
    table_spec = pl.BlockSpec((1, pair_experts, tokens), lambda i, s: (group, 0, 0))
    out_specs = [pl.BlockSpec((pair_experts, 1, CAP, width), lambda i, s: (0, group, 0, 0))]
    out_shape = [jax.ShapeDtypeStruct(slots_shape, BF16)]
    if slots is not None:
        operands.append(slots)
        in_specs.append(table_spec)
        out_specs.append(pl.BlockSpec((pair_experts, 1, CAP, 128), lambda i, s: (0, group, 0, 0)))
        out_shape.append(jax.ShapeDtypeStruct(gate_shape, F32))
    out_specs.append(table_spec)
    out_shape.append(jax.ShapeDtypeStruct(table_shape, F32))
    aliases = {}
    if earlier is not None:
        aliases = {1 + len(operands) + i: i for i in range(len(earlier))}
        in_specs += [pl.BlockSpec(memory_space=pl.ANY)] * len(earlier)
        operands = operands + list(earlier)
    return pl.pallas_call(
        functools.partial(dispatch_kernel, pair_experts, half, len(pieces), slots is not None),
        out_shape=out_shape,
        grid_spec=pltpu.PrefetchScalarGridSpec(
            num_scalar_prefetch=1, grid=(1,), in_specs=in_specs, out_specs=out_specs
        ),
        input_output_aliases=aliases,
        compiler_params=pltpu.CompilerParams(vmem_limit_bytes=VMEM_LIMIT),
        cost_estimate=SMALL,
        name="dispatch",
    )(place, *operands)


def experts_kernel(first_slot, count, chunk, spans, arrived_at, place_ref, *refs):
    own = arrived_at is not None
    xs_ref, us_ref, gates_ref, up_ref, down_ref = refs[:5]
    arrived_ref, refs = (refs[5], refs[6:]) if own else (None, refs[5:])
    results, refs = refs[: 3 * count], refs[3 * count :]
    pieces_ref, refs = refs[0], refs[1:]
    x_all, gu_all, gate_all, up_all, down_all, out_all, row_all, term_all, pieces_all = refs[:9]
    grad_all, hidden_all, piece, *arrived_all, load_sems, store_sems = refs[9:]
    total = x_all.shape[1]
    ff = down_all.shape[1]
    contexts = pieces_all.shape[1]
    rows = piece.shape[0]
    part = rows // spans
    width = grad_all.shape[1]

    def loads_of(e):
        slot, weights = first_slot + e, place_ref[0] + e
        sources = [
            (xs_ref.at[slot], x_all.at[e]),
            (up_ref.at[weights], up_all.at[e]),
            (us_ref.at[slot], gu_all.at[e]),
            (gates_ref.at[slot], gate_all.at[e]),
            (down_ref.at[weights], down_all.at[e]),
        ]
        if own:
            sources.append((arrived_ref.at[pl.ds(0, contexts), arrived_at + e], arrived_all[0].at[e]))
        return [
            pltpu.make_async_copy(source, target, load_sems.at[e, i])
            for i, (source, target) in enumerate(sources)
        ]

    stores = []

    def store(source, target):
        stores.append(pltpu.make_async_copy(source, target, store_sems.at[len(stores)]))
        stores[-1].start()

    def start(loads):
        for load in loads:
            load.start()

    loads = loads_of(0)
    start(loads)
    for e in range(count):
        outs_ref, rows_ref, terms_ref = results[3 * e : 3 * e + 3]
        following = loads_of(e + 1) if e + 1 < count else []
        loads[0].wait()
        loads[1].wait()
        for number in range(total // chunk):
            span = slice(number * chunk, (number + 1) * chunk)
            at = pl.ds(number * chunk, chunk)
            both = jnp.dot(x_all[e, span], up_all[e], preferred_element_type=F32)
            if number == 0:
                for load in loads[2:]:
                    load.wait()
                start(following)
            gate_pre, up_pre = both[:, :ff], both[:, ff:]
            gu = (gu_all[e, span].astype(F32) * gate_all[e, span, 0:1]).astype(BF16)
            gu_all[e, span] = gu
            sigmoid = jax.nn.sigmoid(gate_pre)
            activated = gate_pre * sigmoid
            hidden = (activated * up_pre).astype(BF16)
            hidden_all[span] = hidden
            grad_hidden = lax.dot_general(gu, down_all[e], NT, preferred_element_type=F32)
            out_all[e, span] = jnp.dot(hidden, down_all[e], preferred_element_type=F32).astype(BF16)
            store(out_all.at[e, at], outs_ref.at[at])
            terms = jnp.sum(grad_hidden * hidden.astype(F32), axis=1, keepdims=True)
            term_all[e, span] = jnp.broadcast_to(terms, (chunk, term_all.shape[2]))
            store(term_all.at[e, at], terms_ref.at[at])
            grad_gate = grad_hidden * up_pre * sigmoid * (1.0 + gate_pre * (1.0 - sigmoid))
            grad_both = jnp.concatenate(
                [grad_gate.astype(BF16), (grad_hidden * activated).astype(BF16)], axis=1
            )
            grad_all[span] = grad_both
            row_all[e, span] = lax.dot_general(
                grad_both, up_all[e], NT, preferred_element_type=F32
            ).astype(BF16)
            store(row_all.at[e, at], rows_ref.at[at])
        for number in range(contexts):
            columns = slice(number * rows, (number + 1) * rows)
            piece[:, :width] = lax.dot_general(
                x_all[e, :, columns], grad_all[...], TN, preferred_element_type=F32
            )
            piece[:, width:] = lax.dot_general(
                gu_all[e, :, columns], hidden_all[...], TN, preferred_element_type=F32
            )
            for near in range(spans):
                wanted = lax.bitwise_xor(place_ref[1], near)
                value = piece[pl.ds(pl.multiple_of(wanted * part, part), part), :]
                to = slice(near * part, (near + 1) * part)
                if own:
                    value = value + arrived_all[0][e, number, to, :].astype(F32)
                pieces_all[e, number, to, :] = value.astype(BF16)
            store(pieces_all.at[e, number], pieces_ref.at[number, e])
        loads = following
    for copy in stores:
        copy.wait()


def experts_work(place, first_slot, count, slots, slot_grads, slot_gates, w_gateup, w_down, contexts, spans, arrived):
    total, width = slots.shape[1:]
    ff = w_down.shape[1]
    chunk = 2 * CAP
    rows = width // contexts
    own = arrived is not None
    piece_width = w_gateup.shape[2] + ff
    operands = [slots, slot_grads, slot_gates, w_gateup, w_down]
    out_shape = [
        jax.ShapeDtypeStruct((total, width), BF16),
        jax.ShapeDtypeStruct((total, width), BF16),
        jax.ShapeDtypeStruct((total, 128), F32),
    ] * count
    out_shape.append(jax.ShapeDtypeStruct((contexts, count, rows, piece_width), BF16))
    scratch = [
        pltpu.VMEM((count, total, width), BF16),
        pltpu.VMEM((count, total, width), BF16),
        pltpu.VMEM((count, total, 128), F32),
        pltpu.VMEM((count,) + w_gateup.shape[1:], BF16),
        pltpu.VMEM((count,) + w_down.shape[1:], BF16),
        pltpu.VMEM((count, total, width), BF16),
        pltpu.VMEM((count, total, width), BF16),
        pltpu.VMEM((count, total, 128), F32),
        pltpu.VMEM((count, contexts, rows, piece_width), BF16),
        pltpu.VMEM((total, 2 * ff), BF16),
        pltpu.VMEM((total, ff), BF16),
        pltpu.VMEM((rows, piece_width), F32),
    ]
    if own:
        operands.append(arrived[0])
        scratch.append(pltpu.VMEM((count, contexts, rows, piece_width), BF16))
    scratch.append(pltpu.SemaphoreType.DMA((count, 7)))
    scratch.append(pltpu.SemaphoreType.DMA((count * (3 * (total // chunk) + contexts),)))
    results = pl.pallas_call(
        functools.partial(
            experts_kernel, first_slot, count, chunk, spans, arrived[1] if own else None
        ),
        out_shape=out_shape,
        grid_spec=pltpu.PrefetchScalarGridSpec(
            num_scalar_prefetch=1,
            grid=(1,),
            in_specs=[pl.BlockSpec(memory_space=pl.ANY)] * len(operands),
            out_specs=[pl.BlockSpec(memory_space=pl.ANY)] * len(out_shape),
            scratch_shapes=scratch,
        ),
        compiler_params=pltpu.CompilerParams(vmem_limit_bytes=VMEM_LIMIT),
        cost_estimate=SMALL,
        name="experts",
    )(place, *operands)
    return [results[3 * e : 3 * e + 3] for e in range(count)], results[3 * count]


def combine_kernel(pair_experts, half, extra_rows, added, results, with_terms, place_ref, slots_ref, *refs):
    scale_ref, terms = None, ()
    if with_terms:
        values = refs[:pair_experts]
        terms = refs[pair_experts : 2 * pair_experts]
        refs = refs[2 * pair_experts :]
    else:
        scale_ref = refs[0]
        values = refs[1 : 1 + pair_experts]
        refs = refs[1 + pair_experts :]
    added_refs = refs[: len(added)]
    if results == 1:
        first, second = refs[-1].at[:half], refs[-1].at[half:]
    else:
        first, second = refs[-2:]
    tokens = 2 * half
    extra_places = lax.broadcasted_iota(jnp.int32, (max(extra_rows, 8), tokens), 0)
    picks = []
    extras = [jnp.zeros(extra_places.shape, F32) for _ in range(first.shape[1] // tokens)]
    for e in range(pair_experts):
        match = one_hot(slots_ref[0, e : e + 1, :])
        if with_terms:
            picks.append(jnp.where(match, 1.0, 0.0).astype(BF16))
            term_row = jnp.sum(jnp.where(match, terms[e][:, 0:1], 0.0), axis=0, keepdims=True)
            expert = expert_of(place_ref, e, pair_experts)
            part, row = lax.div(expert, extra_rows), lax.rem(expert, extra_rows)
            for k in range(len(extras)):
                extras[k] = jnp.where(
                    jnp.logical_and(extra_places == row, part == k), term_row, extras[k]
                )
        else:
            picks.append(jnp.where(match, scale_ref[0, e : e + 1, :], 0.0).astype(BF16))
    pick = jnp.concatenate(picks, axis=0)
    block = jnp.concatenate([ref[...] for ref in values], axis=0)
    summed = lax.dot_general(pick, block, (((0,), (0,)), ((), ())), preferred_element_type=F32)
    halves = [summed[:half], summed[half:]]
    for piece, ref in zip(added, added_refs):
        halves[piece] = halves[piece] + ref[:half, :].astype(F32)
        if with_terms and piece == 1:
            extras = [
                extra + ref[half:, k * tokens : (k + 1) * tokens].astype(F32) for k, extra in enumerate(extras)
            ]
    first[...] = halves[0].astype(BF16)
    second[:half, :] = halves[1].astype(BF16)
    if with_terms:
        for k, extra in enumerate(extras):
            second[half:, k * tokens : (k + 1) * tokens] = extra.astype(BF16)


def combine(place, group, results, slot_table, scales, values, terms, extra_rows, parts=()):
    pair_experts = len(values)
    tokens = slot_table.shape[2]
    width = values[0].shape[1]
    half = tokens // 2
    table_spec = pl.BlockSpec((1,) + slot_table.shape[1:], lambda i, s: (group, 0, 0))
    whole = lambda array: pl.BlockSpec(array.shape, lambda i, s: (0, 0))
    in_specs = [table_spec]
    operands = [slot_table]
    if terms is None:
        in_specs.append(table_spec)
        operands.append(scales)
        extra_rows = 0
    in_specs += [pl.BlockSpec((CAP, width), lambda i, s: (group, 0))] * pair_experts
    operands += values
    if terms is not None:
        in_specs += [pl.BlockSpec((CAP, 128), lambda i, s: (group, 0))] * pair_experts
        operands += terms
    in_specs += [whole(array) for _, array in parts]
    operands += [array for _, array in parts]
    counts = [tokens + extra_rows] if results == 1 else [half, half + extra_rows]
    out_shape = [jax.ShapeDtypeStruct((count, width), BF16) for count in counts]
    result = pl.pallas_call(
        functools.partial(
            combine_kernel,
            pair_experts,
            half,
            extra_rows,
            [piece for piece, _ in parts],
            results,
            terms is not None,
        ),
        out_shape=out_shape,
        grid_spec=pltpu.PrefetchScalarGridSpec(
            num_scalar_prefetch=1,
            grid=(1,),
            in_specs=in_specs,
            out_specs=[whole(shape) for shape in out_shape],
        ),
        compiler_params=pltpu.CompilerParams(vmem_limit_bytes=VMEM_LIMIT),
        cost_estimate=SMALL,
        name="combine",
    )(place, *operands)
    return result[0] if results == 1 else result


def attend_kernel(first, last, distance, place_ref, q_ref, k_ref, v_ref, *refs):
    if first:
        state_in, stat_in = None, None
    else:
        state_in, stat_in = refs[:2]
        refs = refs[2:]
    state_ref, stat_ref = refs[:2]
    keys_count = k_ref.shape[0]
    length = q_ref.shape[0]
    heads = q_ref.shape[1] // HD
    grouped = heads // (k_ref.shape[1] // HD)

    def pieces():
        if first:
            return [(slice(b * BLOCK, (b + 1) * BLOCK), slice(0, (b + 1) * BLOCK)) for b in range(length // BLOCK)]
        return [(slice(0, length), slice(0, keys_count))]

    def work():
        turned_values = jnp.transpose(v_ref[...])
        for head in range(heads):
            kv_head = head // grouped
            own = slice(head * HD, (head + 1) * HD)
            shared = slice(kv_head * HD, (kv_head + 1) * HD)
            for q_span, k_span in pieces():
                scores = lax.dot_general(
                    k_ref[k_span, shared], q_ref[q_span, own], NT, preferred_element_type=F32
                )
                top = jnp.max(scores, axis=0, keepdims=True)
                if not first:
                    before = stat_in[0, head : head + 1, q_span]
                    top = jnp.maximum(top, before)
                weights = jnp.exp(scores - top)
                total = jnp.sum(weights, axis=0, keepdims=True)
                update = jnp.dot(
                    turned_values[shared, k_span], weights.astype(BF16), preferred_element_type=F32
                )
                if not first:
                    factor = jnp.exp(before - top)
                    total = total + factor * stat_in[0, heads + head : heads + head + 1, q_span]
                    update = update + factor * state_in[own, q_span]
                stat_ref[0, head : head + 1, q_span] = top
                stat_ref[0, heads + head : heads + head + 1, q_span] = total
                state_ref[own, q_span] = update

    if first:
        work()
    else:
        pl.when(place_ref[0] >= distance)(work)

        @pl.when(place_ref[0] < distance)
        def _():
            state_ref[...] = state_in[...]
            stat_ref[...] = stat_in[...]

    if last:
        low_ref = refs[2]
        for head in range(heads):
            own = slice(head * HD, (head + 1) * HD)
            total = stat_ref[0, heads + head : heads + head + 1, :]
            state_ref[own, :] = state_ref[own, :] / total
            stat_ref[0, head : head + 1, :] = stat_ref[0, head : head + 1, :] + jnp.log(total)
        low_ref[...] = jnp.transpose(state_ref[...]).astype(BF16)


def attend_chunk(place, distance, last, queries, keyval, state):
    length, width = queries.shape
    kv_half = keyval.shape[1] // 2
    pairs = kv_half // 128
    q_columns = width // pairs
    heads = q_columns // HD
    first = state is None
    q_spec = pl.BlockSpec((length, q_columns), lambda i, s: (0, i))
    state_spec = pl.BlockSpec((q_columns, length), lambda i, s: (i, 0))
    stat_spec = pl.BlockSpec((1, 2 * heads, length), lambda i, s: (i, 0, 0))
    in_specs = [
        q_spec,
        pl.BlockSpec((keyval.shape[0], 128), lambda i, s: (0, i)),
        pl.BlockSpec((keyval.shape[0], 128), lambda i, s: (0, pairs + i)),
    ]
    operands = [queries, keyval, keyval]
    out_specs = [state_spec, stat_spec]
    out_shape = [
        jax.ShapeDtypeStruct((width, length), F32),
        jax.ShapeDtypeStruct((pairs, 2 * heads, length), F32),
    ]
    if not first:
        in_specs += [state_spec, stat_spec]
        operands += list(state)
    if last:
        out_specs.append(q_spec)
        out_shape.append(jax.ShapeDtypeStruct((length, width), BF16))
    work = length * keyval.shape[0] * width
    return pl.pallas_call(
        functools.partial(attend_kernel, first, last, distance),
        out_shape=out_shape,
        grid_spec=pltpu.PrefetchScalarGridSpec(
            num_scalar_prefetch=1, grid=(pairs,), in_specs=in_specs, out_specs=out_specs
        ),
        compiler_params=pltpu.CompilerParams(vmem_limit_bytes=VMEM_LIMIT),
        cost_estimate=SMALL,
        name="attend",
    )(place, *operands)


def back_kernel(first, own_chunk, distance, arrives, place_ref, q_ref, k_ref, v_ref, grad_ref, state_ref, stat_ref, *refs):
    arrived_ref = None
    if arrives:
        arrived_ref, refs = refs[0], refs[1:]
    dq_in = None
    if not first:
        dq_in, refs = refs[0], refs[1:]
    dkv_ref, dq_ref = refs
    length = q_ref.shape[0]
    keys_count = k_ref.shape[0]
    heads = q_ref.shape[1] // HD
    kv_heads = k_ref.shape[1] // HD
    grouped = heads // kv_heads

    def work():
        turned_keys = jnp.transpose(k_ref[...])
        turned_grads = jnp.transpose(grad_ref[...].astype(F32))
        if own_chunk:
            pieces = [
                (slice(b * BLOCK, (b + 1) * BLOCK), slice(0, (b + 1) * BLOCK)) for b in range(length // BLOCK)
            ]
        else:
            pieces = [(slice(0, length), slice(0, keys_count))]
        for kv_head in range(kv_heads):
            shared = slice(kv_head * HD, (kv_head + 1) * HD)
            sums = {}
            for head in range(kv_head * grouped, (kv_head + 1) * grouped):
                own = slice(head * HD, (head + 1) * HD)
                row_term = jnp.sum(turned_grads[own, :] * state_ref[own, :], axis=0, keepdims=True)
                for q_span, k_span in pieces:
                    q = q_ref[q_span, own]
                    grad = grad_ref[q_span, own]
                    scores = lax.dot_general(k_ref[k_span, shared], q, NT, preferred_element_type=F32)
                    probs = jnp.exp(scores - stat_ref[0, head : head + 1, q_span])
                    grad_probs = lax.dot_general(v_ref[k_span, shared], grad, NT, preferred_element_type=F32)
                    grad_scores = (probs * (grad_probs - row_term[:, q_span])).astype(BF16)
                    grad_values = jnp.dot(probs.astype(BF16), grad, preferred_element_type=F32)
                    grad_keys = jnp.dot(grad_scores, q, preferred_element_type=F32)
                    blocks = grad_keys.shape[0] // BLOCK
                    for b in range(blocks):
                        part = slice(b * BLOCK, (b + 1) * BLOCK)
                        if b in sums:
                            sums[b] = (sums[b][0] + grad_keys[part], sums[b][1] + grad_values[part])
                        else:
                            sums[b] = (grad_keys[part], grad_values[part])
                    grad_q = jnp.dot(turned_keys[shared, k_span], grad_scores, preferred_element_type=F32)
                    if first:
                        dq_ref[own, q_span] = grad_q
                    else:
                        dq_ref[own, q_span] = dq_in[own, q_span] + grad_q
            for b, pair in sums.items():
                part = slice(b * BLOCK, (b + 1) * BLOCK)
                for i in range(2):
                    value = pair[i]
                    if arrives:
                        value = value + arrived_ref[i, part, shared].astype(F32)
                    dkv_ref[i, part, shared] = value.astype(BF16)

    if own_chunk:
        work()
    else:
        pl.when(place_ref[0] >= distance)(work)

        @pl.when(place_ref[0] < distance)
        def _():
            dkv_ref[...] = jnp.zeros_like(dkv_ref)
            dq_ref[...] = jnp.zeros_like(dq_ref) if first else dq_in[...]


def back_chunk(place, distance, queries, keyval, grad_heads, state, stats, arrived, dq):
    length, width = queries.shape
    kv_half = keyval.shape[1] // 2
    pairs = kv_half // 128
    q_columns = width // pairs
    heads = q_columns // HD
    q_spec = pl.BlockSpec((length, q_columns), lambda i, s: (0, i))
    state_spec = pl.BlockSpec((q_columns, length), lambda i, s: (i, 0))
    stat_spec = pl.BlockSpec((1, 2 * heads, length), lambda i, s: (i, 0, 0))
    dkv_spec = pl.BlockSpec((2, keyval.shape[0], 128), lambda i, s: (0, 0, i))
    in_specs = [
        q_spec,
        pl.BlockSpec((keyval.shape[0], 128), lambda i, s: (0, i)),
        pl.BlockSpec((keyval.shape[0], 128), lambda i, s: (0, pairs + i)),
        q_spec,
        state_spec,
        stat_spec,
    ]
    operands = [queries, keyval, keyval, grad_heads, state, stats]
    if arrived is not None:
        in_specs.append(dkv_spec)
        operands.append(arrived)
    if dq is not None:
        in_specs.append(state_spec)
        operands.append(dq)
    work = length * keyval.shape[0] * width
    return pl.pallas_call(
        functools.partial(back_kernel, dq is None, distance == 0, distance, arrived is not None),
        out_shape=[
            jax.ShapeDtypeStruct((2, keyval.shape[0], kv_half), BF16),
            jax.ShapeDtypeStruct((width, length), F32),
        ],
        grid_spec=pltpu.PrefetchScalarGridSpec(
            num_scalar_prefetch=1, grid=(pairs,), in_specs=in_specs, out_specs=[dkv_spec, state_spec]
        ),
        compiler_params=pltpu.CompilerParams(vmem_limit_bytes=VMEM_LIMIT),
        cost_estimate=SMALL,
        name="back",
    )(place, *operands)


def sum_hops(experts_first=False):
    hops = {}
    for axis in ("dp", "experts", "context"):
        bit = 1
        hops[axis] = []
        while bit < lax.axis_size(axis):
            hops[axis].append((axis, bit))
            bit *= 2
    core, along_x = hops["dp"][:1], hops["dp"][1:]
    middle = hops["experts"] + along_x if experts_first else along_x + hops["experts"]
    return core + middle + hops["context"]


def put_arranged(value, columns, place_ref, plan, plain, arranged, keep_ref, send_ref):
    contexts, spans, masks = plan
    part = value.shape[0] // len(masks)
    half = value.shape[0] // 2
    width = value.shape[1]
    plain[:, :width] = value
    for number, (owner_mask, context_mask, span_mask) in enumerate(masks):
        block = (
            lax.bitwise_xor(place_ref[0], owner_mask) * contexts
            + lax.bitwise_xor(place_ref[1], context_mask)
        ) * spans + lax.bitwise_xor(place_ref[2], span_mask)
        source = pl.ds(pl.multiple_of(block * part, part), part)
        arranged[number * part : (number + 1) * part, :width] = plain[source, :width]
    keep_ref[:, columns] = arranged[:half, :width].astype(BF16)
    send_ref[:, columns] = arranged[half:, :width].astype(BF16)


def sum_plan(experts_first=False):
    contexts, spans = lax.axis_size("context"), lax.axis_size("dp")
    hops = sum_hops(experts_first)
    masks = []
    for number in range(2 ** len(hops)):
        mask = {"experts": 0, "context": 0, "dp": 0}
        for i, (axis, bit) in enumerate(hops):
            if (number >> (len(hops) - 1 - i)) & 1:
                mask[axis] |= bit
        masks.append((mask["experts"], mask["context"], mask["dp"]))
    return contexts, spans, masks


def summed(pair, start=0, stop=None, experts_first=False):
    keep, send = pair
    hops = sum_hops(experts_first)
    for i in range(start, len(hops) if stop is None else stop):
        total = keep.astype(F32) + hop(send, *hops[i]).astype(F32)
        rows = total.shape[0] // 2
        if i + 1 == len(hops):
            return total
        keep, send = total[:rows], total[rows:].astype(BF16)
    return keep, send


def turned_back(rows, cos, sin):
    parts = []
    for head in range(rows.shape[0] // HD):
        first = rows[head * HD : head * HD + HD // 2]
        second = rows[head * HD + HD // 2 : (head + 1) * HD]
        parts += [first * cos + second * sin, second * cos - first * sin]
    return jnp.concatenate(parts, axis=0)


STEP = 256


def step_columns():
    step = pl.program_id(0)
    return step, pl.ds(pl.multiple_of(step * STEP, STEP), STEP)


def out_grad_kernel(plan, steps, place_ref, low_ref, grad_ref, moe_ref, logits_ref, gain_ref, keep_ref, send_ref,
                    plain, arranged):
    step, columns = step_columns()

    @pl.when(step < steps)
    def _():
        value = lax.dot_general(low_ref[...], grad_ref[...], TN, preferred_element_type=F32)
        put_arranged(value, columns, place_ref, plan, plain, arranged, keep_ref, send_ref)

    @pl.when(step == steps)
    def _():
        lanes = lax.broadcasted_iota(jnp.int32, logits_ref.shape, 1)
        ones = jnp.where(lanes == EXPERTS, 1.0, 0.0).astype(BF16)
        value = lax.dot_general(moe_ref[...], logits_ref[...], TN, preferred_element_type=F32)
        value = value + lax.dot_general(gain_ref[...], ones, TN, preferred_element_type=F32)
        put_arranged(value, slice(steps * STEP, steps * STEP + 128), place_ref, plan, plain, arranged, keep_ref, send_ref)


def out_grad(place, attn_low, grad_attn, moe_low, grad_logits, gain_terms):
    length, rows = attn_low.shape
    width = grad_attn.shape[1]
    steps = width // STEP
    whole = lambda array: pl.BlockSpec(array.shape, lambda i, s: (0, 0))
    shape = jax.ShapeDtypeStruct((rows // 2, width + 128), BF16)
    return pl.pallas_call(
        functools.partial(out_grad_kernel, sum_plan(True), steps),
        out_shape=[shape, shape],
        grid_spec=pltpu.PrefetchScalarGridSpec(
            num_scalar_prefetch=1,
            grid=(steps + 1,),
            in_specs=[
                whole(attn_low),
                pl.BlockSpec((length, STEP), lambda i, s: (0, jnp.minimum(i, steps - 1))),
                whole(moe_low),
                whole(grad_logits),
                whole(gain_terms),
            ],
            out_specs=[whole(shape), whole(shape)],
            scratch_shapes=[pltpu.VMEM((rows, STEP), F32)] * 2,
        ),
        compiler_params=pltpu.CompilerParams(vmem_limit_bytes=VMEM_LIMIT),
        cost_estimate=SMALL,
        name="out_grad",
    )(place, attn_low, grad_attn, moe_low, grad_logits, gain_terms)


def query_grad_kernel(plan, scale, place_ref, dq_ref, cos_ref, sin_ref, low_ref, weight_ref, keep_ref, send_ref,
                      normed_ref, plain, arranged):
    step, columns = step_columns()
    turned = turned_back(dq_ref[...] * scale, cos_ref[...], sin_ref[...])
    low = jnp.transpose(turned).astype(BF16)
    value = lax.dot_general(low_ref[...], low, TN, preferred_element_type=F32)
    put_arranged(value, columns, place_ref, plan, plain, arranged, keep_ref, send_ref)
    part = lax.dot_general(low, weight_ref[...], NT, preferred_element_type=F32)

    @pl.when(step == 0)
    def _():
        normed_ref[...] = part

    @pl.when(step > 0)
    def _():
        normed_ref[...] = normed_ref[...] + part


def query_grad(place, grad_queries, cos, sin, normed_low, query_weight, scale):
    columns, length = grad_queries.shape
    rows = normed_low.shape[1]
    whole = lambda array: pl.BlockSpec(array.shape, lambda i, s: (0, 0))
    shape = jax.ShapeDtypeStruct((rows // 2, columns), BF16)
    normed = jax.ShapeDtypeStruct((length, rows), F32)
    return pl.pallas_call(
        functools.partial(query_grad_kernel, sum_plan(True), scale),
        out_shape=[shape, shape, normed],
        grid_spec=pltpu.PrefetchScalarGridSpec(
            num_scalar_prefetch=1,
            grid=(columns // STEP,),
            in_specs=[
                pl.BlockSpec((STEP, length), lambda i, s: (i, 0)),
                whole(cos),
                whole(sin),
                whole(normed_low),
                pl.BlockSpec((rows, STEP), lambda i, s: (0, i)),
            ],
            out_specs=[whole(shape), whole(shape), whole(normed)],
            scratch_shapes=[pltpu.VMEM((rows, STEP), F32)] * 2,
        ),
        compiler_params=pltpu.CompilerParams(vmem_limit_bytes=VMEM_LIMIT),
        cost_estimate=SMALL,
        name="query_grad",
    )(place, grad_queries, cos, sin, normed_low, query_weight)


def keyval_grad_kernel(plan, steps, place_ref, own_ref, arrived_ref, cos_ref, sin_ref, low_ref, weight_ref, part_ref,
                       input_ref, inverse_ref, gain_ref, middle_ref, keep_ref, send_ref, result_ref, total,
                       plain, arranged):
    step, columns = step_columns()

    def take(low):
        value = lax.dot_general(low_ref[...], low, TN, preferred_element_type=F32)
        put_arranged(value, columns, place_ref, plan, plain, arranged, keep_ref, send_ref)
        part = lax.dot_general(low, weight_ref[...], NT, preferred_element_type=F32)

        @pl.when(step == 0)
        def _():
            total[...] = part_ref[...] + part

        @pl.when(step > 0)
        def _():
            total[...] = total[...] + part

    def sum_block():
        return own_ref[0].astype(F32) + arrived_ref[0].astype(F32)

    @pl.when(step < steps // 2)
    def _():
        turned = turned_back(jnp.transpose(sum_block()), cos_ref[...], sin_ref[...])
        take(jnp.transpose(turned).astype(BF16))

    @pl.when(jnp.logical_and(step >= steps // 2, step < steps))
    def _():
        take(sum_block().astype(BF16))

    @pl.when(step == steps)
    def _():
        grad = total[...]
        inputs = input_ref[...].astype(F32)
        inverse = inverse_ref[...][:, 0:1]
        scaled = gain_ref[...] * grad
        mean = jnp.mean(inputs * scaled, axis=1, keepdims=True)
        result = inverse * scaled - inputs * (inverse * inverse * inverse * mean) + middle_ref[...]
        result_ref[...] = result.astype(BF16)
        terms = (grad * inputs * inverse).astype(BF16)
        ones = jnp.ones((terms.shape[0], 128), BF16)
        value = lax.dot_general(terms, ones, TN, preferred_element_type=F32)
        put_arranged(value, slice(steps * STEP, steps * STEP + 128), place_ref, plan, plain, arranged, keep_ref, send_ref)


def keyval_grad(place, own, arrived, cos, sin, normed_low, keyval_weight, part, inputs, inverse, gain, grad_middle):
    length, rows = normed_low.shape
    width = keyval_weight.shape[1]
    steps = width // STEP
    half = steps // 2
    whole = lambda array: pl.BlockSpec(array.shape, lambda i, s: (0,) * len(array.shape))
    shape = jax.ShapeDtypeStruct((rows // 2, width + 128), BF16)
    result = jax.ShapeDtypeStruct((length, rows), BF16)
    at = lambda i: jnp.minimum(i, steps - 1)
    chunk = pl.BlockSpec((1, length, STEP), lambda i, s: (at(i) // half, 0, at(i) % half))
    return pl.pallas_call(
        functools.partial(keyval_grad_kernel, sum_plan(), steps),
        out_shape=[shape, shape, result],
        grid_spec=pltpu.PrefetchScalarGridSpec(
            num_scalar_prefetch=1,
            grid=(steps + 1,),
            in_specs=[
                chunk,
                chunk,
                whole(cos),
                whole(sin),
                whole(normed_low),
                pl.BlockSpec((rows, STEP), lambda i, s: (0, at(i))),
                whole(part),
                whole(inputs),
                whole(inverse),
                whole(gain),
                whole(grad_middle),
            ],
            out_specs=[whole(shape), whole(shape), whole(result)],
            scratch_shapes=[pltpu.VMEM((length, rows), F32)] + [pltpu.VMEM((rows, STEP), F32)] * 2,
        ),
        compiler_params=pltpu.CompilerParams(vmem_limit_bytes=VMEM_LIMIT),
        cost_estimate=SMALL,
        name="keyval_grad",
    )(place, own, arrived, cos, sin, normed_low, keyval_weight, part, inputs, inverse, gain, grad_middle)


def on_device(
    decoder_input,
    gain_attn,
    query_weight,
    keyval_weight,
    output_weight,
    gain_moe,
    w_router,
    w_gateup,
    w_down,
    top_idx,
    slot_order,
    cotangent,
):
    owners, contexts, spans = (lax.axis_size(a) for a in ("experts", "context", "dp"))
    inputs = decoder_input[0].astype(jnp.float32)
    length = inputs.shape[0]
    width = inputs.shape[1]
    half = length // 2
    heads = query_weight.shape[1] // HD
    kv_width = keyval_weight.shape[1]
    kv_half = kv_width // 2
    scale = HD ** (-0.5)
    local_experts = w_gateup.shape[0]
    own_experts = local_experts // spans
    y_place, z_place, dp_place = (lax.axis_index(a) for a in ("experts", "context", "dp"))

    ids = top_idx[0].T
    chosen = jnp.any(ids[None, :, :] == jnp.arange(EXPERTS)[:, None, None], axis=1)
    rank_order = slot_order[0, 0]
    earlier = (rank_order[:, None] < rank_order[None, :]).astype(BF16)
    before = jnp.dot(chosen.astype(BF16), earlier, preferred_element_type=F32)
    kept = jnp.logical_and(chosen, before < CAP)
    slot_table = jnp.where(kept, before, -1.0)
    upstream_low = cotangent[0]
    upstream = upstream_low.astype(jnp.float32)
    pair_experts = 2 * own_experts
    other_core = jnp.bitwise_xor(dp_place, 1)
    expert_place = jnp.stack(
        [
            y_place * local_experts + dp_place * own_experts,
            y_place * local_experts + other_core * own_experts,
        ]
    ).astype(jnp.int32)
    own_upstream = jnp.concatenate([upstream_low, packed_rows(slot_table, width).astype(BF16)], axis=0)

    offset = z_place * length
    cos_table, sin_table = rotary_tables(offset, length, HD)
    cos_rows, sin_rows = (jnp.transpose(table[:, 0]) for table in (cos_table, sin_table))
    sum_place = jnp.stack([y_place, z_place, dp_place]).astype(jnp.int32)
    normed_rows, inverse_attn = norm_forward(inputs, gain_attn)
    normed_low = normed_rows.astype(jnp.bfloat16)
    query_unrotated = jnp.dot(normed_low, query_weight, preferred_element_type=jnp.float32)
    keyval_unrotated = jnp.dot(normed_low, keyval_weight, preferred_element_type=jnp.float32)
    queries = (
        rotate(query_unrotated.reshape(length, heads, HD), cos_table, sin_table)
        .astype(jnp.bfloat16)
        .reshape(length, heads * HD)
    ) * jnp.asarray(scale, BF16)
    keys_turned = rotate(
        keyval_unrotated[:, :kv_half].reshape(length, KVH, HD), cos_table, sin_table
    ).reshape(length, kv_half)
    keyval = jnp.concatenate([keys_turned, keyval_unrotated[:, kv_half:]], axis=1).astype(
        jnp.bfloat16
    )
    z_index = jnp.stack([z_place]).astype(jnp.int32)
    near_upstream = gather_near(own_upstream)
    groups = 2 * owners
    upstream_groups = [(rows,) for rows in [own_upstream] + near_upstream]
    attended, grad_state = None, None
    chunk = keyval
    chunks = [keyval]
    for distance in range(contexts):
        arriving = None
        if distance < contexts - 1:
            upward = [(i, i + 1) for i in range(distance, contexts - 1)]
            arriving = lax.ppermute(chunk, "context", upward)
        attended = attend_chunk(
            z_index,
            distance,
            distance == contexts - 1,
            queries,
            chunk,
            None if attended is None else attended[:2],
        )
        if arriving is not None:
            if distance == 1 or contexts < 3:
                near_upstream = after(near_upstream, attended[1])
                upstream_groups = upstream_groups[:groups] + gather_far(near_upstream, half)
            for group in range(groups):
                if group * (contexts - 1) // groups == distance:
                    pieces = after(upstream_groups[group], attended[1])
                    grad_state = dispatch(
                        expert_place, group, groups, pair_experts, half, pieces, None, grad_state
                    )
            chunk, attended, grad_state = lax.optimization_barrier((arriving, attended, grad_state))
            chunks.append(chunk)
    attention_output, attention_stats, attn_low = attended
    slot_grads, slot_rows = grad_state
    residual_middle = inputs + jnp.dot(attn_low, output_weight, preferred_element_type=jnp.float32)
    normed_moe, inverse_moe = norm_forward(residual_middle, gain_moe)
    moe_low = normed_moe.astype(jnp.bfloat16)
    logits = lax.dot_general(
        w_router, moe_low, (((0,), (1,)), ((), ())), preferred_element_type=jnp.float32
    )
    top_logit = jnp.max(jnp.where(chosen, logits, MASKED), axis=0, keepdims=True)
    raised = jnp.where(chosen, jnp.exp(logits - top_logit), 0.0)
    gates = raised / jnp.sum(raised, axis=0, keepdims=True)

    own_rows = jnp.concatenate([moe_low, packed_rows(gates, width).astype(BF16)], axis=0)
    near_rows = gather_near(own_rows)

    def place_rows(group, pieces, row_state):
        return dispatch(
            expert_place, group, groups, pair_experts, half, pieces, slot_rows, row_state
        )

    row_state = place_rows(0, (own_rows,), None)
    near_rows, row_state = lax.optimization_barrier((near_rows, row_state))
    far_rows = gather_far(near_rows, half)
    for group, rows in enumerate(near_rows):
        row_state = place_rows(1 + group, (rows,), row_state)
    far_rows, row_state = lax.optimization_barrier((far_rows, row_state))
    for group, pieces in enumerate(far_rows):
        row_state = place_rows(1 + owners + group, pieces, row_state)
    slots, slot_gates, gate_rows = row_state
    extra_rows = EXPERTS * length // width
    total = groups * CAP
    slots = slots.reshape(pair_experts, total, width)
    slot_gates = slot_gates.reshape(pair_experts, total, 128)
    slot_grads = slot_grads.reshape(pair_experts, total, width)

    def work(number, count, own, gate, arrived):
        owner = dp_place if own else other_core
        work_place = jnp.stack([owner * own_experts + number, owner]).astype(jnp.int32)
        return experts_work(
            work_place,
            number if own else own_experts + number,
            count,
            after(slots, gate),
            slot_grads,
            slot_gates,
            w_gateup,
            w_down,
            contexts,
            spans,
            arrived,
        )

    outs, rows, terms = ([None] * pair_experts for _ in range(3))
    crossing, finals = [None] * own_experts, []

    def exchange_x(stacked):
        part = stacked.shape[1] // spans
        return stacked, x_hop(stacked[:, 2 * part :])

    def exchange_core(stacked, across):
        part = stacked.shape[1] // spans
        beside = core_hop(jnp.concatenate([stacked[:, part : 2 * part], across[:, part:]], axis=1))
        return stacked[:, :part], beside[:, :part], across[:, :part], beside[:, part:]

    gate = slot_gates
    count = min(2, own_experts)
    for own in (False, True):
        for start in range(0, own_experts, count):
            results, pieces = work(start, count, own, gate, crossing[start] if own else None)
            for number in range(start, start + count):
                slot = number if own else own_experts + number
                outs[slot], rows[slot], terms[slot] = results[number - start]
            gate = results[-1][2]
            if own:
                finals.append(lax.psum_scatter(pieces, "context", scatter_dimension=0, tiled=False))
            else:
                crossed_pieces = core_hop(pieces)
                for number in range(start, start + count):
                    crossing[number] = (crossed_pieces, number - start)

    def row_part(group, parts=()):
        results = 2 if group > owners else 1
        return combine(expert_place, group, results, slot_rows, None, rows, terms, extra_rows, parts)

    def mixture_part(group, gate, parts=()):
        results = 2 if group > owners else 1
        return combine(
            expert_place, group, results, after(slot_rows, gate), gate_rows, outs, None, 0, parts
        )

    row_sums, mixtures = [None] * groups, [None] * groups
    far_groups = range(1 + owners, groups)
    near_groups = range(1, 1 + owners)
    for group in far_groups:
        row_sums[group] = row_part(group)
    far_sums = return_far(row_sums)
    row_sums[0] = row_part(0)
    gate = row_sums[0]
    for group in far_groups:
        mixtures[group] = mixture_part(group, gate)
        gate = mixtures[group]
    far_sums = after(far_sums, gate)
    for group in near_groups:
        row_sums[group] = row_part(group, far_parts(far_sums, group))
    arrivals = return_near(row_sums)
    mixtures[0] = mixture_part(0, row_sums[near_groups[-1]])
    arrivals = after(arrivals, mixtures[0])
    row_total = return_total(row_sums[0], arrivals)
    for group in far_groups:
        mixtures[group] = after(mixtures[group], row_total)
    far_mixtures = return_far(mixtures)
    grad_gate_terms = unpacked_rows(row_total[length:], length)
    grad_moe_rows = row_total[:length]
    grad_selected = grad_gate_terms - gates * jnp.sum(grad_gate_terms, axis=0, keepdims=True)
    grad_logits = grad_selected.astype(BF16)
    grad_moe_rows = grad_moe_rows + lax.dot_general(
        grad_logits, w_router, (((0,), (1,)), ((), ())), preferred_element_type=jnp.float32
    )
    grad_middle, gain_moe_terms = norm_backward(
        residual_middle, inverse_moe, gain_moe, grad_moe_rows
    )
    grad_middle = grad_middle + upstream
    grad_attn = grad_middle.astype(jnp.bfloat16)
    grad_heads = (
        jnp.einsum("td,fd->tf", grad_attn, output_weight, preferred_element_type=jnp.float32)
        .astype(jnp.bfloat16)
    )
    def back(distance, grad_heads, arrived, grad_queries):
        return back_chunk(
            z_index,
            distance,
            queries,
            chunks[distance],
            grad_heads,
            attention_output,
            attention_stats,
            arrived,
            grad_queries,
        )

    def down(distance, grad_chunk):
        pairs = [(i, i - 1) for i in range(distance, contexts)]
        return lax.ppermute(grad_chunk, "context", pairs)

    grad_queries, arrived = None, None
    early_exchange = None
    for distance in reversed(range(1, contexts)):
        grad_chunk, grad_queries = back(distance, grad_heads, arrived, grad_queries)
        arrived = down(distance, grad_chunk)
        if distance == contexts - 1:
            far_mixtures = after(far_mixtures, grad_chunk)
            gate = grad_chunk
            for group in near_groups:
                mixtures[group] = mixture_part(group, gate, far_parts(far_mixtures, group))
                gate = mixtures[group]
            mixture_arrivals = return_near(mixtures)
            own_chunk, grad_queries = back(0, after(grad_heads, gate), None, grad_queries)
            arrived, grad_queries = lax.optimization_barrier((arrived, grad_queries))
        elif distance == contexts - 2:
            out_sums = out_grad(
                sum_place,
                attn_low,
                after(grad_attn, grad_chunk),
                moe_low,
                jnp.pad(grad_logits.T, ((0, 0), (0, 128 - EXPERTS))),
                gain_moe_terms.astype(BF16),
            )
            mixture_arrivals = after(mixture_arrivals, out_sums)
            mixed = return_total(mixtures[0], mixture_arrivals)
            layer_output = (residual_middle + mixed).astype(jnp.bfloat16)[None]
            if len(finals) > 1:
                early_exchange = exchange_x(after(finals[0], grad_chunk))
            arrived, out_sums, layer_output, early_exchange = lax.optimization_barrier(
                (arrived, out_sums, layer_output, early_exchange)
            )
    blocks = []
    if early_exchange is not None:
        early_exchange, grad_chunk = lax.optimization_barrier((early_exchange, grad_chunk))
        blocks.append(exchange_core(*early_exchange))
    out_sums = summed(after(out_sums, grad_chunk), 0, 1, True)
    *query_sums, grad_normed = query_grad(
        sum_place, grad_queries, cos_rows, sin_rows, normed_low, query_weight, scale
    )
    arrived, grad_normed, out_sums, blocks, query_sums = lax.optimization_barrier(
        (arrived, grad_normed, out_sums, blocks, query_sums)
    )
    query_sums = summed(query_sums, 0, 1, True)
    out_sums = summed(out_sums, 1, 2, True)
    *keyval_sums, grad_input = keyval_grad(
        sum_place,
        own_chunk,
        arrived,
        cos_rows,
        sin_rows,
        normed_low,
        keyval_weight,
        grad_normed,
        decoder_input[0],
        jnp.broadcast_to(inverse_attn, (length, 128)),
        gain_attn[None, :],
        grad_middle,
    )
    grad_input = grad_input[None]
    chains = [keyval_sums, query_sums, out_sums]
    steps = [0, 1, 2]
    order = [False, True, True]
    stops = len(sum_hops())
    chains = list(lax.optimization_barrier(tuple(chains)))
    round_number = 0
    last_exchange = exchange_x(after(finals[-1], chains[0]))
    while min(steps) < stops:
        for i in range(len(chains)):
            if steps[i] < stops:
                chains[i] = summed(chains[i], steps[i], steps[i] + 1, order[i])
                steps[i] += 1
        chains = list(lax.optimization_barrier(tuple(chains)))
        if round_number == 2:
            blocks.append(exchange_core(*after(last_exchange, chains[0])))
        round_number += 1
    late, grad_query, early = chains
    grad_out = early[:, :width]
    grad_router = early[:, width : width + EXPERTS]
    grad_gain_moe = early[:, width + EXPERTS]
    grad_keyval = late[:, :kv_width]
    grad_gain_attn = late[:, kv_width]

    near_blocks = jnp.stack(
        [jnp.concatenate([block[place] for block in blocks], axis=0) for place in range(spans)]
    )
    arranged = jnp.concatenate(
        [
            lax.dynamic_index_in_dim(near_blocks, jnp.bitwise_xor(dp_place, b), 0, keepdims=False)
            for b in range(spans)
        ],
        axis=0,
    ).astype(F32)
    grad_gateup = arranged[:, :, : w_gateup.shape[2]]
    grad_down = jnp.transpose(arranged[:, :, w_gateup.shape[2] :], (0, 2, 1))
    return (
        layer_output,
        grad_input,
        grad_gain_attn,
        grad_query,
        grad_keyval,
        grad_out,
        grad_gain_moe,
        grad_router,
        grad_gateup,
        grad_down,
    )


def solution(mesh):
    in_specs = (
        P(("experts", "dp"), "context", None),
        P(),
        P(),
        P(),
        P(),
        P(),
        P(),
        P("experts", None, None),
        P("experts", None, None),
        P(("experts", "dp"), "context", None),
        P(("experts", "dp"), "context", None),
        P(("experts", "dp"), "context", None),
    )
    out_specs = (
        P(("experts", "dp"), "context", None),
        P(("experts", "dp"), "context", None),
        P(("experts", "context", "dp")),
        P(("experts", "context", "dp"), None),
        P(("experts", "context", "dp"), None),
        P(("experts", "context", "dp"), None),
        P(("experts", "context", "dp")),
        P(("experts", "context", "dp"), None),
        P("experts", ("context", "dp"), None),
        P("experts", None, ("context", "dp")),
    )
    return jax.shard_map(
        on_device, mesh=mesh, in_specs=in_specs, out_specs=out_specs, check_vma=False
    )
```

```python
import functools

import jax
import jax.numpy as jnp
from jax import lax
from jax.experimental import pallas as pl
from jax.experimental.pallas import tpu as pltpu
from jax.sharding import PartitionSpec as P

KVH = 8
HD = 64
FF = 512
EXPERTS = 32
TOPK = 8
BLOCK = 256
CAP = 160


EPSILON = 1e-06
MASKED = -1e30
VMEM_LIMIT = 56 * 1024 * 1024
SMALL = pl.CostEstimate(flops=1, bytes_accessed=1, transcendentals=0)
F32 = jnp.float32
NT = (((1,), (1,)), ((), ()))
TN = (((0,), (0,)), ((), ()))
BF16 = jnp.bfloat16


def rotary_tables(offset, length, head_size):
    half_size = head_size // 2
    places = (offset + jnp.arange(length)).astype(jnp.float32)
    frequency = 10000.0 ** (-jnp.arange(half_size).astype(jnp.float32) * 2.0 / head_size)
    angles = places[:, None] * frequency[None, :]
    return (jnp.cos(angles)[:, None, :], jnp.sin(angles)[:, None, :])


def rotate(tensor, cos_table, sin_table):
    half_size = tensor.shape[-1] // 2
    first_half = tensor[..., :half_size]
    second_half = tensor[..., half_size:]
    return jnp.concatenate(
        [
            first_half * cos_table - second_half * sin_table,
            second_half * cos_table + first_half * sin_table,
        ],
        axis=-1,
    )


def norm_forward(tensor, gain):
    inverse = lax.rsqrt(jnp.mean(tensor * tensor, axis=-1, keepdims=True) + EPSILON)
    return (tensor * inverse * gain, inverse)


def norm_backward(tensor, inverse, gain, upstream):
    scaled = gain * upstream
    grad_gain = upstream * tensor * inverse
    grad_tensor = inverse * scaled - tensor * inverse**3 * jnp.mean(
        tensor * scaled, axis=-1, keepdims=True
    )
    return (grad_tensor, grad_gain)


def hop(value, axis, stride):
    count = lax.axis_size(axis)
    return lax.ppermute(value, axis, [(i, i ^ stride) for i in range(count)])


def turn(value, axis, step):
    count = lax.axis_size(axis)
    return lax.ppermute(value, axis, [(i, (i + step) % count) for i in range(count)])


def core_hop(value):
    return hop(value, "dp", 1)


def x_hop(value):
    return hop(value, "dp", lax.axis_size("dp") // 2)


def add_low(*terms):
    total = terms[0].astype(F32)
    for term in terms[1:]:
        total = total + term.astype(F32)
    return total.astype(BF16)


def packed_rows(table, width):
    experts, tokens = table.shape
    parts = width // tokens
    return jnp.transpose(
        table.reshape(parts, experts // parts, tokens), (1, 0, 2)
    ).reshape(experts // parts, width)


def unpacked_rows(rows, tokens):
    count, width = rows.shape
    parts = width // tokens
    return jnp.transpose(rows.reshape(count, parts, tokens), (1, 0, 2)).reshape(
        count * parts, tokens
    )


def after(value, *others):
    return lax.optimization_barrier((value, others))[0]


def gather_near(whole):
    owners = lax.axis_size("experts")
    return [x_hop(whole)] + [turn(whole, "experts", k) for k in range(1, owners)]


def gather_far(near, half):
    owners = lax.axis_size("experts")
    return [(x_hop(near[k][:half]), turn(near[0][half:], "experts", k)) for k in range(1, owners)]


def return_far(sums):
    owners = lax.axis_size("experts")
    return [
        (x_hop(sums[owners + k][0]), turn(sums[owners + k][1], "experts", -k)) for k in range(1, owners)
    ]


def far_parts(far, group):
    if group == 1:
        return [(1, pieces[1]) for pieces in far]
    return [(0, far[group - 2][0])]


def return_near(sums):
    owners = lax.axis_size("experts")
    return [x_hop(sums[1])] + [turn(sums[1 + k], "experts", -k) for k in range(1, owners)]


def return_total(own, arrivals):
    total = own.astype(F32)
    for piece in arrivals:
        total = total + piece.astype(F32)
    return total


def picked_row(block, expert, tokens):
    rows = block.shape[0]
    part, row = lax.div(expert, rows), lax.rem(expert, rows)
    chosen = block[:, :tokens]
    for number in range(1, block.shape[1] // tokens):
        chosen = jnp.where(part == number, block[:, number * tokens : (number + 1) * tokens], chosen)
    places = lax.broadcasted_iota(jnp.int32, chosen.shape, 0)
    return jnp.sum(jnp.where(places == row, chosen, 0.0), axis=0, keepdims=True)


def expert_of(place_ref, number, pair_experts):
    own = pair_experts // 2
    return place_ref[0] + number if number < own else place_ref[1] + number - own


def one_hot(slot_row):
    places = lax.broadcasted_iota(jnp.int32, (CAP, slot_row.shape[1]), 0).astype(F32)
    return places == slot_row


def dispatch_kernel(pair_experts, half, pieces, with_gates, place_ref, *refs):
    if pieces == 1:
        first, second = refs[0].at[:half], refs[0].at[half:]
    else:
        first, second = refs[:2]
    if with_gates:
        slots_ref = refs[pieces]
        out_ref, gate_ref, table_ref = refs[-3:]
    else:
        out_ref, table_ref = refs[-2:]
    tokens = 2 * half
    extra = second[half:, :].astype(F32)
    picks = []
    for e in range(pair_experts):
        row = picked_row(extra, expert_of(place_ref, e, pair_experts), tokens)
        table_ref[0, e : e + 1, :] = row
        if with_gates:
            match = one_hot(slots_ref[0, e : e + 1, :])
            gates = jnp.sum(jnp.where(match, row, 0.0), axis=1, keepdims=True)
            gate_ref[e, 0] = jnp.broadcast_to(gates, gate_ref.shape[2:])
        else:
            match = one_hot(row)
        picks.append(jnp.where(match, 1.0, 0.0).astype(BF16))
    pick = jnp.concatenate(picks, axis=0)
    rows = jnp.dot(pick[:, :half], first[...], preferred_element_type=F32) + jnp.dot(
        pick[:, half:], second[:half, :], preferred_element_type=F32
    )
    for e in range(pair_experts):
        out_ref[e, 0] = rows[e * CAP : (e + 1) * CAP].astype(BF16)


def dispatch(place, group, groups, pair_experts, half, pieces, slots, earlier):
    width = pieces[0].shape[1]
    tokens = 2 * half
    whole = lambda array: pl.BlockSpec(array.shape, lambda i, s: (0, 0))
    operands = list(pieces)
    in_specs = [whole(array) for array in operands]
    slots_shape = (pair_experts, groups, CAP, width)
    gate_shape = (pair_experts, groups, CAP, 128)
    table_shape = (groups, pair_experts, tokens)
    table_spec = pl.BlockSpec((1, pair_experts, tokens), lambda i, s: (group, 0, 0))
    out_specs = [pl.BlockSpec((pair_experts, 1, CAP, width), lambda i, s: (0, group, 0, 0))]
    out_shape = [jax.ShapeDtypeStruct(slots_shape, BF16)]
    if slots is not None:
        operands.append(slots)
        in_specs.append(table_spec)
        out_specs.append(pl.BlockSpec((pair_experts, 1, CAP, 128), lambda i, s: (0, group, 0, 0)))
        out_shape.append(jax.ShapeDtypeStruct(gate_shape, F32))
    out_specs.append(table_spec)
    out_shape.append(jax.ShapeDtypeStruct(table_shape, F32))
    aliases = {}
    if earlier is not None:
        aliases = {1 + len(operands) + i: i for i in range(len(earlier))}
        in_specs += [pl.BlockSpec(memory_space=pl.ANY)] * len(earlier)
        operands = operands + list(earlier)
    return pl.pallas_call(
        functools.partial(dispatch_kernel, pair_experts, half, len(pieces), slots is not None),
        out_shape=out_shape,
        grid_spec=pltpu.PrefetchScalarGridSpec(
            num_scalar_prefetch=1, grid=(1,), in_specs=in_specs, out_specs=out_specs
        ),
        input_output_aliases=aliases,
        compiler_params=pltpu.CompilerParams(vmem_limit_bytes=VMEM_LIMIT),
        cost_estimate=SMALL,
        name="dispatch",
    )(place, *operands)


def experts_kernel(first_slot, count, chunk, spans, arrived_at, place_ref, *refs):
    own = arrived_at is not None
    xs_ref, us_ref, gates_ref, up_ref, down_ref = refs[:5]
    arrived_ref, refs = (refs[5], refs[6:]) if own else (None, refs[5:])
    results, refs = refs[: 3 * count], refs[3 * count :]
    pieces_ref, refs = refs[0], refs[1:]
    x_all, gu_all, gate_all, up_all, down_all, out_all, row_all, term_all, pieces_all = refs[:9]
    grad_all, hidden_all, piece, *arrived_all, load_sems, store_sems = refs[9:]
    total = x_all.shape[1]
    ff = down_all.shape[1]
    contexts = pieces_all.shape[1]
    rows = piece.shape[0]
    part = rows // spans
    width = grad_all.shape[1]

    def loads_of(e):
        slot, weights = first_slot + e, place_ref[0] + e
        sources = [
            (xs_ref.at[slot], x_all.at[e]),
            (up_ref.at[weights], up_all.at[e]),
            (us_ref.at[slot], gu_all.at[e]),
            (gates_ref.at[slot], gate_all.at[e]),
            (down_ref.at[weights], down_all.at[e]),
        ]
        if own:
            sources.append((arrived_ref.at[pl.ds(0, contexts), arrived_at + e], arrived_all[0].at[e]))
        return [
            pltpu.make_async_copy(source, target, load_sems.at[e, i])
            for i, (source, target) in enumerate(sources)
        ]

    stores = []

    def store(source, target):
        stores.append(pltpu.make_async_copy(source, target, store_sems.at[len(stores)]))
        stores[-1].start()

    def start(loads):
        for load in loads:
            load.start()

    loads = loads_of(0)
    start(loads)
    for e in range(count):
        outs_ref, rows_ref, terms_ref = results[3 * e : 3 * e + 3]
        following = loads_of(e + 1) if e + 1 < count else []
        loads[0].wait()
        loads[1].wait()
        for number in range(total // chunk):
            span = slice(number * chunk, (number + 1) * chunk)
            at = pl.ds(number * chunk, chunk)
            both = jnp.dot(x_all[e, span], up_all[e], preferred_element_type=F32)
            if number == 0:
                for load in loads[2:]:
                    load.wait()
                start(following)
            gate_pre, up_pre = both[:, :ff], both[:, ff:]
            gu = (gu_all[e, span].astype(F32) * gate_all[e, span, 0:1]).astype(BF16)
            gu_all[e, span] = gu
            sigmoid = jax.nn.sigmoid(gate_pre)
            activated = gate_pre * sigmoid
            hidden = (activated * up_pre).astype(BF16)
            hidden_all[span] = hidden
            grad_hidden = lax.dot_general(gu, down_all[e], NT, preferred_element_type=F32)
            out_all[e, span] = jnp.dot(hidden, down_all[e], preferred_element_type=F32).astype(BF16)
            store(out_all.at[e, at], outs_ref.at[at])
            terms = jnp.sum(grad_hidden * hidden.astype(F32), axis=1, keepdims=True)
            term_all[e, span] = jnp.broadcast_to(terms, (chunk, term_all.shape[2]))
            store(term_all.at[e, at], terms_ref.at[at])
            grad_gate = grad_hidden * up_pre * sigmoid * (1.0 + gate_pre * (1.0 - sigmoid))
            grad_both = jnp.concatenate(
                [grad_gate.astype(BF16), (grad_hidden * activated).astype(BF16)], axis=1
            )
            grad_all[span] = grad_both
            row_all[e, span] = lax.dot_general(
                grad_both, up_all[e], NT, preferred_element_type=F32
            ).astype(BF16)
            store(row_all.at[e, at], rows_ref.at[at])
        for number in range(contexts):
            columns = slice(number * rows, (number + 1) * rows)
            piece[:, :width] = lax.dot_general(
                x_all[e, :, columns], grad_all[...], TN, preferred_element_type=F32
            )
            piece[:, width:] = lax.dot_general(
                gu_all[e, :, columns], hidden_all[...], TN, preferred_element_type=F32
            )
            for near in range(spans):
                wanted = lax.bitwise_xor(place_ref[1], near)
                value = piece[pl.ds(pl.multiple_of(wanted * part, part), part), :]
                to = slice(near * part, (near + 1) * part)
                if own:
                    value = value + arrived_all[0][e, number, to, :].astype(F32)
                pieces_all[e, number, to, :] = value.astype(BF16)
            store(pieces_all.at[e, number], pieces_ref.at[number, e])
        loads = following
    for copy in stores:
        copy.wait()


def experts_work(place, first_slot, count, slots, slot_grads, slot_gates, w_gateup, w_down, contexts, spans, arrived):
    total, width = slots.shape[1:]
    ff = w_down.shape[1]
    chunk = 2 * CAP
    rows = width // contexts
    own = arrived is not None
    piece_width = w_gateup.shape[2] + ff
    operands = [slots, slot_grads, slot_gates, w_gateup, w_down]
    out_shape = [
        jax.ShapeDtypeStruct((total, width), BF16),
        jax.ShapeDtypeStruct((total, width), BF16),
        jax.ShapeDtypeStruct((total, 128), F32),
    ] * count
    out_shape.append(jax.ShapeDtypeStruct((contexts, count, rows, piece_width), BF16))
    scratch = [
        pltpu.VMEM((count, total, width), BF16),
        pltpu.VMEM((count, total, width), BF16),
        pltpu.VMEM((count, total, 128), F32),
        pltpu.VMEM((count,) + w_gateup.shape[1:], BF16),
        pltpu.VMEM((count,) + w_down.shape[1:], BF16),
        pltpu.VMEM((count, total, width), BF16),
        pltpu.VMEM((count, total, width), BF16),
        pltpu.VMEM((count, total, 128), F32),
        pltpu.VMEM((count, contexts, rows, piece_width), BF16),
        pltpu.VMEM((total, 2 * ff), BF16),
        pltpu.VMEM((total, ff), BF16),
        pltpu.VMEM((rows, piece_width), F32),
    ]
    if own:
        operands.append(arrived[0])
        scratch.append(pltpu.VMEM((count, contexts, rows, piece_width), BF16))
    scratch.append(pltpu.SemaphoreType.DMA((count, 7)))
    scratch.append(pltpu.SemaphoreType.DMA((count * (3 * (total // chunk) + contexts),)))
    results = pl.pallas_call(
        functools.partial(
            experts_kernel, first_slot, count, chunk, spans, arrived[1] if own else None
        ),
        out_shape=out_shape,
        grid_spec=pltpu.PrefetchScalarGridSpec(
            num_scalar_prefetch=1,
            grid=(1,),
            in_specs=[pl.BlockSpec(memory_space=pl.ANY)] * len(operands),
            out_specs=[pl.BlockSpec(memory_space=pl.ANY)] * len(out_shape),
            scratch_shapes=scratch,
        ),
        compiler_params=pltpu.CompilerParams(vmem_limit_bytes=VMEM_LIMIT),
        cost_estimate=SMALL,
        name="experts",
    )(place, *operands)
    return [results[3 * e : 3 * e + 3] for e in range(count)], results[3 * count]


def combine_kernel(pair_experts, half, extra_rows, added, results, with_terms, place_ref, slots_ref, *refs):
    scale_ref, terms = None, ()
    if with_terms:
        values = refs[:pair_experts]
        terms = refs[pair_experts : 2 * pair_experts]
        refs = refs[2 * pair_experts :]
    else:
        scale_ref = refs[0]
        values = refs[1 : 1 + pair_experts]
        refs = refs[1 + pair_experts :]
    added_refs = refs[: len(added)]
    if results == 1:
        first, second = refs[-1].at[:half], refs[-1].at[half:]
    else:
        first, second = refs[-2:]
    tokens = 2 * half
    extra_places = lax.broadcasted_iota(jnp.int32, (max(extra_rows, 8), tokens), 0)
    picks = []
    extras = [jnp.zeros(extra_places.shape, F32) for _ in range(first.shape[1] // tokens)]
    for e in range(pair_experts):
        match = one_hot(slots_ref[0, e : e + 1, :])
        if with_terms:
            picks.append(jnp.where(match, 1.0, 0.0).astype(BF16))
            term_row = jnp.sum(jnp.where(match, terms[e][:, 0:1], 0.0), axis=0, keepdims=True)
            expert = expert_of(place_ref, e, pair_experts)
            part, row = lax.div(expert, extra_rows), lax.rem(expert, extra_rows)
            for k in range(len(extras)):
                extras[k] = jnp.where(
                    jnp.logical_and(extra_places == row, part == k), term_row, extras[k]
                )
        else:
            picks.append(jnp.where(match, scale_ref[0, e : e + 1, :], 0.0).astype(BF16))
    pick = jnp.concatenate(picks, axis=0)
    block = jnp.concatenate([ref[...] for ref in values], axis=0)
    summed = lax.dot_general(pick, block, (((0,), (0,)), ((), ())), preferred_element_type=F32)
    halves = [summed[:half], summed[half:]]
    for piece, ref in zip(added, added_refs):
        halves[piece] = halves[piece] + ref[:half, :].astype(F32)
        if with_terms and piece == 1:
            extras = [
                extra + ref[half:, k * tokens : (k + 1) * tokens].astype(F32) for k, extra in enumerate(extras)
            ]
    first[...] = halves[0].astype(BF16)
    second[:half, :] = halves[1].astype(BF16)
    if with_terms:
        for k, extra in enumerate(extras):
            second[half:, k * tokens : (k + 1) * tokens] = extra.astype(BF16)


def combine(place, group, results, slot_table, scales, values, terms, extra_rows, parts=()):
    pair_experts = len(values)
    tokens = slot_table.shape[2]
    width = values[0].shape[1]
    half = tokens // 2
    table_spec = pl.BlockSpec((1,) + slot_table.shape[1:], lambda i, s: (group, 0, 0))
    whole = lambda array: pl.BlockSpec(array.shape, lambda i, s: (0, 0))
    in_specs = [table_spec]
    operands = [slot_table]
    if terms is None:
        in_specs.append(table_spec)
        operands.append(scales)
        extra_rows = 0
    in_specs += [pl.BlockSpec((CAP, width), lambda i, s: (group, 0))] * pair_experts
    operands += values
    if terms is not None:
        in_specs += [pl.BlockSpec((CAP, 128), lambda i, s: (group, 0))] * pair_experts
        operands += terms
    in_specs += [whole(array) for _, array in parts]
    operands += [array for _, array in parts]
    counts = [tokens + extra_rows] if results == 1 else [half, half + extra_rows]
    out_shape = [jax.ShapeDtypeStruct((count, width), BF16) for count in counts]
    result = pl.pallas_call(
        functools.partial(
            combine_kernel,
            pair_experts,
            half,
            extra_rows,
            [piece for piece, _ in parts],
            results,
            terms is not None,
        ),
        out_shape=out_shape,
        grid_spec=pltpu.PrefetchScalarGridSpec(
            num_scalar_prefetch=1,
            grid=(1,),
            in_specs=in_specs,
            out_specs=[whole(shape) for shape in out_shape],
        ),
        compiler_params=pltpu.CompilerParams(vmem_limit_bytes=VMEM_LIMIT),
        cost_estimate=SMALL,
        name="combine",
    )(place, *operands)
    return result[0] if results == 1 else result


def attend_kernel(first, last, distance, place_ref, q_ref, k_ref, v_ref, *refs):
    if first:
        state_in, stat_in = None, None
    else:
        state_in, stat_in = refs[:2]
        refs = refs[2:]
    state_ref, stat_ref = refs[:2]
    keys_count = k_ref.shape[0]
    length = q_ref.shape[0]
    heads = q_ref.shape[1] // HD
    grouped = heads // (k_ref.shape[1] // HD)

    def pieces():
        if first:
            return [(slice(b * BLOCK, (b + 1) * BLOCK), slice(0, (b + 1) * BLOCK)) for b in range(length // BLOCK)]
        return [(slice(0, length), slice(0, keys_count))]

    def work():
        turned_values = jnp.transpose(v_ref[...])
        for head in range(heads):
            kv_head = head // grouped
            own = slice(head * HD, (head + 1) * HD)
            shared = slice(kv_head * HD, (kv_head + 1) * HD)
            for q_span, k_span in pieces():
                scores = lax.dot_general(
                    k_ref[k_span, shared], q_ref[q_span, own], NT, preferred_element_type=F32
                )
                top = jnp.max(scores, axis=0, keepdims=True)
                if not first:
                    before = stat_in[0, head : head + 1, q_span]
                    top = jnp.maximum(top, before)
                weights = jnp.exp(scores - top)
                total = jnp.sum(weights, axis=0, keepdims=True)
                update = jnp.dot(
                    turned_values[shared, k_span], weights.astype(BF16), preferred_element_type=F32
                )
                if not first:
                    factor = jnp.exp(before - top)
                    total = total + factor * stat_in[0, heads + head : heads + head + 1, q_span]
                    update = update + factor * state_in[own, q_span]
                stat_ref[0, head : head + 1, q_span] = top
                stat_ref[0, heads + head : heads + head + 1, q_span] = total
                state_ref[own, q_span] = update

    if first:
        work()
    else:
        pl.when(place_ref[0] >= distance)(work)

        @pl.when(place_ref[0] < distance)
        def _():
            state_ref[...] = state_in[...]
            stat_ref[...] = stat_in[...]

    if last:
        low_ref = refs[2]
        for head in range(heads):
            own = slice(head * HD, (head + 1) * HD)
            total = stat_ref[0, heads + head : heads + head + 1, :]
            state_ref[own, :] = state_ref[own, :] / total
            stat_ref[0, head : head + 1, :] = stat_ref[0, head : head + 1, :] + jnp.log(total)
        low_ref[...] = jnp.transpose(state_ref[...]).astype(BF16)


def attend_chunk(place, distance, last, queries, keyval, state):
    length, width = queries.shape
    kv_half = keyval.shape[1] // 2
    pairs = kv_half // 128
    q_columns = width // pairs
    heads = q_columns // HD
    first = state is None
    q_spec = pl.BlockSpec((length, q_columns), lambda i, s: (0, i))
    state_spec = pl.BlockSpec((q_columns, length), lambda i, s: (i, 0))
    stat_spec = pl.BlockSpec((1, 2 * heads, length), lambda i, s: (i, 0, 0))
    in_specs = [
        q_spec,
        pl.BlockSpec((keyval.shape[0], 128), lambda i, s: (0, i)),
        pl.BlockSpec((keyval.shape[0], 128), lambda i, s: (0, pairs + i)),
    ]
    operands = [queries, keyval, keyval]
    out_specs = [state_spec, stat_spec]
    out_shape = [
        jax.ShapeDtypeStruct((width, length), F32),
        jax.ShapeDtypeStruct((pairs, 2 * heads, length), F32),
    ]
    if not first:
        in_specs += [state_spec, stat_spec]
        operands += list(state)
    if last:
        out_specs.append(q_spec)
        out_shape.append(jax.ShapeDtypeStruct((length, width), BF16))
    work = length * keyval.shape[0] * width
    return pl.pallas_call(
        functools.partial(attend_kernel, first, last, distance),
        out_shape=out_shape,
        grid_spec=pltpu.PrefetchScalarGridSpec(
            num_scalar_prefetch=1, grid=(pairs,), in_specs=in_specs, out_specs=out_specs
        ),
        compiler_params=pltpu.CompilerParams(vmem_limit_bytes=VMEM_LIMIT),
        cost_estimate=SMALL,
        name="attend",
    )(place, *operands)


def back_kernel(first, own_chunk, distance, arrives, place_ref, q_ref, k_ref, v_ref, grad_ref, state_ref, stat_ref, *refs):
    arrived_ref = None
    if arrives:
        arrived_ref, refs = refs[0], refs[1:]
    dq_in = None
    if not first:
        dq_in, refs = refs[0], refs[1:]
    dkv_ref, dq_ref = refs
    length = q_ref.shape[0]
    keys_count = k_ref.shape[0]
    heads = q_ref.shape[1] // HD
    kv_heads = k_ref.shape[1] // HD
    grouped = heads // kv_heads

    def work():
        turned_keys = jnp.transpose(k_ref[...])
        turned_grads = jnp.transpose(grad_ref[...].astype(F32))
        if own_chunk:
            pieces = [
                (slice(b * BLOCK, (b + 1) * BLOCK), slice(0, (b + 1) * BLOCK)) for b in range(length // BLOCK)
            ]
        else:
            pieces = [(slice(0, length), slice(0, keys_count))]
        for kv_head in range(kv_heads):
            shared = slice(kv_head * HD, (kv_head + 1) * HD)
            sums = {}
            for head in range(kv_head * grouped, (kv_head + 1) * grouped):
                own = slice(head * HD, (head + 1) * HD)
                row_term = jnp.sum(turned_grads[own, :] * state_ref[own, :], axis=0, keepdims=True)
                for q_span, k_span in pieces:
                    q = q_ref[q_span, own]
                    grad = grad_ref[q_span, own]
                    scores = lax.dot_general(k_ref[k_span, shared], q, NT, preferred_element_type=F32)
                    probs = jnp.exp(scores - stat_ref[0, head : head + 1, q_span])
                    grad_probs = lax.dot_general(v_ref[k_span, shared], grad, NT, preferred_element_type=F32)
                    grad_scores = (probs * (grad_probs - row_term[:, q_span])).astype(BF16)
                    grad_values = jnp.dot(probs.astype(BF16), grad, preferred_element_type=F32)
                    grad_keys = jnp.dot(grad_scores, q, preferred_element_type=F32)
                    blocks = grad_keys.shape[0] // BLOCK
                    for b in range(blocks):
                        part = slice(b * BLOCK, (b + 1) * BLOCK)
                        if b in sums:
                            sums[b] = (sums[b][0] + grad_keys[part], sums[b][1] + grad_values[part])
                        else:
                            sums[b] = (grad_keys[part], grad_values[part])
                    grad_q = jnp.dot(turned_keys[shared, k_span], grad_scores, preferred_element_type=F32)
                    if first:
                        dq_ref[own, q_span] = grad_q
                    else:
                        dq_ref[own, q_span] = dq_in[own, q_span] + grad_q
            for b, pair in sums.items():
                part = slice(b * BLOCK, (b + 1) * BLOCK)
                for i in range(2):
                    value = pair[i]
                    if arrives:
                        value = value + arrived_ref[i, part, shared].astype(F32)
                    dkv_ref[i, part, shared] = value.astype(BF16)

    if own_chunk:
        work()
    else:
        pl.when(place_ref[0] >= distance)(work)

        @pl.when(place_ref[0] < distance)
        def _():
            dkv_ref[...] = jnp.zeros_like(dkv_ref)
            dq_ref[...] = jnp.zeros_like(dq_ref) if first else dq_in[...]


def back_chunk(place, distance, queries, keyval, grad_heads, state, stats, arrived, dq):
    length, width = queries.shape
    kv_half = keyval.shape[1] // 2
    pairs = kv_half // 128
    q_columns = width // pairs
    heads = q_columns // HD
    q_spec = pl.BlockSpec((length, q_columns), lambda i, s: (0, i))
    state_spec = pl.BlockSpec((q_columns, length), lambda i, s: (i, 0))
    stat_spec = pl.BlockSpec((1, 2 * heads, length), lambda i, s: (i, 0, 0))
    dkv_spec = pl.BlockSpec((2, keyval.shape[0], 128), lambda i, s: (0, 0, i))
    in_specs = [
        q_spec,
        pl.BlockSpec((keyval.shape[0], 128), lambda i, s: (0, i)),
        pl.BlockSpec((keyval.shape[0], 128), lambda i, s: (0, pairs + i)),
        q_spec,
        state_spec,
        stat_spec,
    ]
    operands = [queries, keyval, keyval, grad_heads, state, stats]
    if arrived is not None:
        in_specs.append(dkv_spec)
        operands.append(arrived)
    if dq is not None:
        in_specs.append(state_spec)
        operands.append(dq)
    work = length * keyval.shape[0] * width
    return pl.pallas_call(
        functools.partial(back_kernel, dq is None, distance == 0, distance, arrived is not None),
        out_shape=[
            jax.ShapeDtypeStruct((2, keyval.shape[0], kv_half), BF16),
            jax.ShapeDtypeStruct((width, length), F32),
        ],
        grid_spec=pltpu.PrefetchScalarGridSpec(
            num_scalar_prefetch=1, grid=(pairs,), in_specs=in_specs, out_specs=[dkv_spec, state_spec]
        ),
        compiler_params=pltpu.CompilerParams(vmem_limit_bytes=VMEM_LIMIT),
        cost_estimate=SMALL,
        name="back",
    )(place, *operands)


def sum_hops(experts_first=False):
    hops = {}
    for axis in ("dp", "experts", "context"):
        bit = 1
        hops[axis] = []
        while bit < lax.axis_size(axis):
            hops[axis].append((axis, bit))
            bit *= 2
    core, along_x = hops["dp"][:1], hops["dp"][1:]
    middle = hops["experts"] + along_x if experts_first else along_x + hops["experts"]
    return core + middle + hops["context"]


def put_arranged(value, columns, place_ref, plan, plain, arranged, keep_ref, send_ref):
    contexts, spans, masks = plan
    part = value.shape[0] // len(masks)
    half = value.shape[0] // 2
    width = value.shape[1]
    plain[:, :width] = value
    for number, (owner_mask, context_mask, span_mask) in enumerate(masks):
        block = (
            lax.bitwise_xor(place_ref[0], owner_mask) * contexts
            + lax.bitwise_xor(place_ref[1], context_mask)
        ) * spans + lax.bitwise_xor(place_ref[2], span_mask)
        source = pl.ds(pl.multiple_of(block * part, part), part)
        arranged[number * part : (number + 1) * part, :width] = plain[source, :width]
    keep_ref[:, columns] = arranged[:half, :width].astype(BF16)
    send_ref[:, columns] = arranged[half:, :width].astype(BF16)


def sum_plan(experts_first=False):
    contexts, spans = lax.axis_size("context"), lax.axis_size("dp")
    hops = sum_hops(experts_first)
    masks = []
    for number in range(2 ** len(hops)):
        mask = {"experts": 0, "context": 0, "dp": 0}
        for i, (axis, bit) in enumerate(hops):
            if (number >> (len(hops) - 1 - i)) & 1:
                mask[axis] |= bit
        masks.append((mask["experts"], mask["context"], mask["dp"]))
    return contexts, spans, masks


def summed(pair, start=0, stop=None, experts_first=False):
    keep, send = pair
    hops = sum_hops(experts_first)
    for i in range(start, len(hops) if stop is None else stop):
        total = keep.astype(F32) + hop(send, *hops[i]).astype(F32)
        rows = total.shape[0] // 2
        if i + 1 == len(hops):
            return total
        keep, send = total[:rows], total[rows:].astype(BF16)
    return keep, send


def turned_back(rows, cos, sin):
    parts = []
    for head in range(rows.shape[0] // HD):
        first = rows[head * HD : head * HD + HD // 2]
        second = rows[head * HD + HD // 2 : (head + 1) * HD]
        parts += [first * cos + second * sin, second * cos - first * sin]
    return jnp.concatenate(parts, axis=0)


STEP = 256


def step_columns():
    step = pl.program_id(0)
    return step, pl.ds(pl.multiple_of(step * STEP, STEP), STEP)


def out_grad_kernel(plan, steps, place_ref, low_ref, grad_ref, moe_ref, logits_ref, gain_ref, keep_ref, send_ref,
                    plain, arranged):
    step, columns = step_columns()

    @pl.when(step < steps)
    def _():
        value = lax.dot_general(low_ref[...], grad_ref[...], TN, preferred_element_type=F32)
        put_arranged(value, columns, place_ref, plan, plain, arranged, keep_ref, send_ref)

    @pl.when(step == steps)
    def _():
        lanes = lax.broadcasted_iota(jnp.int32, logits_ref.shape, 1)
        ones = jnp.where(lanes == EXPERTS, 1.0, 0.0).astype(BF16)
        value = lax.dot_general(moe_ref[...], logits_ref[...], TN, preferred_element_type=F32)
        value = value + lax.dot_general(gain_ref[...], ones, TN, preferred_element_type=F32)
        put_arranged(value, slice(steps * STEP, steps * STEP + 128), place_ref, plan, plain, arranged, keep_ref, send_ref)


def out_grad(place, attn_low, grad_attn, moe_low, grad_logits, gain_terms):
    length, rows = attn_low.shape
    width = grad_attn.shape[1]
    steps = width // STEP
    whole = lambda array: pl.BlockSpec(array.shape, lambda i, s: (0, 0))
    shape = jax.ShapeDtypeStruct((rows // 2, width + 128), BF16)
    return pl.pallas_call(
        functools.partial(out_grad_kernel, sum_plan(True), steps),
        out_shape=[shape, shape],
        grid_spec=pltpu.PrefetchScalarGridSpec(
            num_scalar_prefetch=1,
            grid=(steps + 1,),
            in_specs=[
                whole(attn_low),
                pl.BlockSpec((length, STEP), lambda i, s: (0, jnp.minimum(i, steps - 1))),
                whole(moe_low),
                whole(grad_logits),
                whole(gain_terms),
            ],
            out_specs=[whole(shape), whole(shape)],
            scratch_shapes=[pltpu.VMEM((rows, STEP), F32)] * 2,
        ),
        compiler_params=pltpu.CompilerParams(vmem_limit_bytes=VMEM_LIMIT),
        cost_estimate=SMALL,
        name="out_grad",
    )(place, attn_low, grad_attn, moe_low, grad_logits, gain_terms)


def query_grad_kernel(plan, scale, place_ref, dq_ref, cos_ref, sin_ref, low_ref, weight_ref, keep_ref, send_ref,
                      normed_ref, plain, arranged):
    step, columns = step_columns()
    turned = turned_back(dq_ref[...] * scale, cos_ref[...], sin_ref[...])
    low = jnp.transpose(turned).astype(BF16)
    value = lax.dot_general(low_ref[...], low, TN, preferred_element_type=F32)
    put_arranged(value, columns, place_ref, plan, plain, arranged, keep_ref, send_ref)
    part = lax.dot_general(low, weight_ref[...], NT, preferred_element_type=F32)

    @pl.when(step == 0)
    def _():
        normed_ref[...] = part

    @pl.when(step > 0)
    def _():
        normed_ref[...] = normed_ref[...] + part


def query_grad(place, grad_queries, cos, sin, normed_low, query_weight, scale):
    columns, length = grad_queries.shape
    rows = normed_low.shape[1]
    whole = lambda array: pl.BlockSpec(array.shape, lambda i, s: (0, 0))
    shape = jax.ShapeDtypeStruct((rows // 2, columns), BF16)
    normed = jax.ShapeDtypeStruct((length, rows), F32)
    return pl.pallas_call(
        functools.partial(query_grad_kernel, sum_plan(True), scale),
        out_shape=[shape, shape, normed],
        grid_spec=pltpu.PrefetchScalarGridSpec(
            num_scalar_prefetch=1,
            grid=(columns // STEP,),
            in_specs=[
                pl.BlockSpec((STEP, length), lambda i, s: (i, 0)),
                whole(cos),
                whole(sin),
                whole(normed_low),
                pl.BlockSpec((rows, STEP), lambda i, s: (0, i)),
            ],
            out_specs=[whole(shape), whole(shape), whole(normed)],
            scratch_shapes=[pltpu.VMEM((rows, STEP), F32)] * 2,
        ),
        compiler_params=pltpu.CompilerParams(vmem_limit_bytes=VMEM_LIMIT),
        cost_estimate=SMALL,
        name="query_grad",
    )(place, grad_queries, cos, sin, normed_low, query_weight)


def keyval_grad_kernel(plan, steps, place_ref, own_ref, arrived_ref, cos_ref, sin_ref, low_ref, weight_ref, part_ref,
                       input_ref, inverse_ref, gain_ref, middle_ref, keep_ref, send_ref, result_ref, total,
                       plain, arranged):
    step, columns = step_columns()

    def take(low):
        value = lax.dot_general(low_ref[...], low, TN, preferred_element_type=F32)
        put_arranged(value, columns, place_ref, plan, plain, arranged, keep_ref, send_ref)
        part = lax.dot_general(low, weight_ref[...], NT, preferred_element_type=F32)

        @pl.when(step == 0)
        def _():
            total[...] = part_ref[...] + part

        @pl.when(step > 0)
        def _():
            total[...] = total[...] + part

    def sum_block():
        return own_ref[0].astype(F32) + arrived_ref[0].astype(F32)

    @pl.when(step < steps // 2)
    def _():
        turned = turned_back(jnp.transpose(sum_block()), cos_ref[...], sin_ref[...])
        take(jnp.transpose(turned).astype(BF16))

    @pl.when(jnp.logical_and(step >= steps // 2, step < steps))
    def _():
        take(sum_block().astype(BF16))

    @pl.when(step == steps)
    def _():
        grad = total[...]
        inputs = input_ref[...].astype(F32)
        inverse = inverse_ref[...][:, 0:1]
        scaled = gain_ref[...] * grad
        mean = jnp.mean(inputs * scaled, axis=1, keepdims=True)
        result = inverse * scaled - inputs * (inverse * inverse * inverse * mean) + middle_ref[...]
        result_ref[...] = result.astype(BF16)
        terms = (grad * inputs * inverse).astype(BF16)
        ones = jnp.ones((terms.shape[0], 128), BF16)
        value = lax.dot_general(terms, ones, TN, preferred_element_type=F32)
        put_arranged(value, slice(steps * STEP, steps * STEP + 128), place_ref, plan, plain, arranged, keep_ref, send_ref)


def keyval_grad(place, own, arrived, cos, sin, normed_low, keyval_weight, part, inputs, inverse, gain, grad_middle):
    length, rows = normed_low.shape
    width = keyval_weight.shape[1]
    steps = width // STEP
    half = steps // 2
    whole = lambda array: pl.BlockSpec(array.shape, lambda i, s: (0,) * len(array.shape))
    shape = jax.ShapeDtypeStruct((rows // 2, width + 128), BF16)
    result = jax.ShapeDtypeStruct((length, rows), BF16)
    at = lambda i: jnp.minimum(i, steps - 1)
    chunk = pl.BlockSpec((1, length, STEP), lambda i, s: (at(i) // half, 0, at(i) % half))
    return pl.pallas_call(
        functools.partial(keyval_grad_kernel, sum_plan(), steps),
        out_shape=[shape, shape, result],
        grid_spec=pltpu.PrefetchScalarGridSpec(
            num_scalar_prefetch=1,
            grid=(steps + 1,),
            in_specs=[
                chunk,
                chunk,
                whole(cos),
                whole(sin),
                whole(normed_low),
                pl.BlockSpec((rows, STEP), lambda i, s: (0, at(i))),
                whole(part),
                whole(inputs),
                whole(inverse),
                whole(gain),
                whole(grad_middle),
            ],
            out_specs=[whole(shape), whole(shape), whole(result)],
            scratch_shapes=[pltpu.VMEM((length, rows), F32)] + [pltpu.VMEM((rows, STEP), F32)] * 2,
        ),
        compiler_params=pltpu.CompilerParams(vmem_limit_bytes=VMEM_LIMIT),
        cost_estimate=SMALL,
        name="keyval_grad",
    )(place, own, arrived, cos, sin, normed_low, keyval_weight, part, inputs, inverse, gain, grad_middle)


def on_device(
    decoder_input,
    gain_attn,
    query_weight,
    keyval_weight,
    output_weight,
    gain_moe,
    w_router,
    w_gateup,
    w_down,
    top_idx,
    slot_order,
    cotangent,
):
    owners, contexts, spans = (lax.axis_size(a) for a in ("experts", "context", "dp"))
    inputs = decoder_input[0].astype(jnp.float32)
    length = inputs.shape[0]
    width = inputs.shape[1]
    half = length // 2
    heads = query_weight.shape[1] // HD
    kv_width = keyval_weight.shape[1]
    kv_half = kv_width // 2
    scale = HD ** (-0.5)
    local_experts = w_gateup.shape[0]
    own_experts = local_experts // spans
    y_place, z_place, dp_place = (lax.axis_index(a) for a in ("experts", "context", "dp"))

    ids = top_idx[0].T
    chosen = jnp.any(ids[None, :, :] == jnp.arange(EXPERTS)[:, None, None], axis=1)
    rank_order = slot_order[0, 0]
    earlier = (rank_order[:, None] < rank_order[None, :]).astype(BF16)
    before = jnp.dot(chosen.astype(BF16), earlier, preferred_element_type=F32)
    kept = jnp.logical_and(chosen, before < CAP)
    slot_table = jnp.where(kept, before, -1.0)
    upstream_low = cotangent[0]
    upstream = upstream_low.astype(jnp.float32)
    pair_experts = 2 * own_experts
    other_core = jnp.bitwise_xor(dp_place, 1)
    expert_place = jnp.stack(
        [
            y_place * local_experts + dp_place * own_experts,
            y_place * local_experts + other_core * own_experts,
        ]
    ).astype(jnp.int32)
    own_upstream = jnp.concatenate([upstream_low, packed_rows(slot_table, width).astype(BF16)], axis=0)

    offset = z_place * length
    cos_table, sin_table = rotary_tables(offset, length, HD)
    cos_rows, sin_rows = (jnp.transpose(table[:, 0]) for table in (cos_table, sin_table))
    sum_place = jnp.stack([y_place, z_place, dp_place]).astype(jnp.int32)
    normed_rows, inverse_attn = norm_forward(inputs, gain_attn)
    normed_low = normed_rows.astype(jnp.bfloat16)
    query_unrotated = jnp.dot(normed_low, query_weight, preferred_element_type=jnp.float32)
    keyval_unrotated = jnp.dot(normed_low, keyval_weight, preferred_element_type=jnp.float32)
    queries = (
        rotate(query_unrotated.reshape(length, heads, HD), cos_table, sin_table)
        .astype(jnp.bfloat16)
        .reshape(length, heads * HD)
    ) * jnp.asarray(scale, BF16)
    keys_turned = rotate(
        keyval_unrotated[:, :kv_half].reshape(length, KVH, HD), cos_table, sin_table
    ).reshape(length, kv_half)
    keyval = jnp.concatenate([keys_turned, keyval_unrotated[:, kv_half:]], axis=1).astype(
        jnp.bfloat16
    )
    z_index = jnp.stack([z_place]).astype(jnp.int32)
    near_upstream = gather_near(own_upstream)
    groups = 2 * owners
    upstream_groups = [(rows,) for rows in [own_upstream] + near_upstream]
    attended, grad_state = None, None
    chunk = keyval
    chunks = [keyval]
    for distance in range(contexts):
        arriving = None
        if distance < contexts - 1:
            upward = [(i, i + 1) for i in range(distance, contexts - 1)]
            arriving = lax.ppermute(chunk, "context", upward)
        attended = attend_chunk(
            z_index,
            distance,
            distance == contexts - 1,
            queries,
            chunk,
            None if attended is None else attended[:2],
        )
        if arriving is not None:
            if distance == 1 or contexts < 3:
                near_upstream = after(near_upstream, attended[1])
                upstream_groups = upstream_groups[:groups] + gather_far(near_upstream, half)
            for group in range(groups):
                if group * (contexts - 1) // groups == distance:
                    pieces = after(upstream_groups[group], attended[1])
                    grad_state = dispatch(
                        expert_place, group, groups, pair_experts, half, pieces, None, grad_state
                    )
            chunk, attended, grad_state = lax.optimization_barrier((arriving, attended, grad_state))
            chunks.append(chunk)
    attention_output, attention_stats, attn_low = attended
    slot_grads, slot_rows = grad_state
    residual_middle = inputs + jnp.dot(attn_low, output_weight, preferred_element_type=jnp.float32)
    normed_moe, inverse_moe = norm_forward(residual_middle, gain_moe)
    moe_low = normed_moe.astype(jnp.bfloat16)
    logits = lax.dot_general(
        w_router, moe_low, (((0,), (1,)), ((), ())), preferred_element_type=jnp.float32
    )
    top_logit = jnp.max(jnp.where(chosen, logits, MASKED), axis=0, keepdims=True)
    raised = jnp.where(chosen, jnp.exp(logits - top_logit), 0.0)
    gates = raised / jnp.sum(raised, axis=0, keepdims=True)

    own_rows = jnp.concatenate([moe_low, packed_rows(gates, width).astype(BF16)], axis=0)
    near_rows = gather_near(own_rows)

    def place_rows(group, pieces, row_state):
        return dispatch(
            expert_place, group, groups, pair_experts, half, pieces, slot_rows, row_state
        )

    row_state = place_rows(0, (own_rows,), None)
    near_rows, row_state = lax.optimization_barrier((near_rows, row_state))
    far_rows = gather_far(near_rows, half)
    for group, rows in enumerate(near_rows):
        row_state = place_rows(1 + group, (rows,), row_state)
    far_rows, row_state = lax.optimization_barrier((far_rows, row_state))
    for group, pieces in enumerate(far_rows):
        row_state = place_rows(1 + owners + group, pieces, row_state)
    slots, slot_gates, gate_rows = row_state
    extra_rows = EXPERTS * length // width
    total = groups * CAP
    slots = slots.reshape(pair_experts, total, width)
    slot_gates = slot_gates.reshape(pair_experts, total, 128)
    slot_grads = slot_grads.reshape(pair_experts, total, width)

    def work(number, count, own, gate, arrived):
        owner = dp_place if own else other_core
        work_place = jnp.stack([owner * own_experts + number, owner]).astype(jnp.int32)
        return experts_work(
            work_place,
            number if own else own_experts + number,
            count,
            after(slots, gate),
            slot_grads,
            slot_gates,
            w_gateup,
            w_down,
            contexts,
            spans,
            arrived,
        )

    outs, rows, terms = ([None] * pair_experts for _ in range(3))
    crossing, finals = [None] * own_experts, []

    def exchange_x(stacked):
        part = stacked.shape[1] // spans
        return stacked, x_hop(stacked[:, 2 * part :])

    def exchange_core(stacked, across):
        part = stacked.shape[1] // spans
        beside = core_hop(jnp.concatenate([stacked[:, part : 2 * part], across[:, part:]], axis=1))
        return stacked[:, :part], beside[:, :part], across[:, :part], beside[:, part:]

    gate = slot_gates
    count = min(2, own_experts)
    for own in (False, True):
        for start in range(0, own_experts, count):
            results, pieces = work(start, count, own, gate, crossing[start] if own else None)
            for number in range(start, start + count):
                slot = number if own else own_experts + number
                outs[slot], rows[slot], terms[slot] = results[number - start]
            gate = results[-1][2]
            if own:
                following = range(start + count, min(start + 2 * count, own_experts))
                if following:
                    pieces, crossed_pieces = lax.optimization_barrier((pieces, crossing[following[0]][0]))
                    for number in following:
                        crossing[number] = (crossed_pieces, number - following[0])
                finals.append(lax.psum_scatter(pieces, "context", scatter_dimension=0, tiled=False))
            else:
                crossed_pieces = core_hop(pieces)
                for number in range(start, start + count):
                    crossing[number] = (crossed_pieces, number - start)

    def row_part(group, parts=()):
        results = 2 if group > owners else 1
        return combine(expert_place, group, results, slot_rows, None, rows, terms, extra_rows, parts)

    def mixture_part(group, gate, parts=()):
        results = 2 if group > owners else 1
        return combine(
            expert_place, group, results, after(slot_rows, gate), gate_rows, outs, None, 0, parts
        )

    row_sums, mixtures = [None] * groups, [None] * groups
    far_groups = range(1 + owners, groups)
    near_groups = range(1, 1 + owners)
    for group in far_groups:
        row_sums[group] = row_part(group)
    far_sums = return_far(row_sums)
    row_sums[0] = row_part(0)
    gate = row_sums[0]
    for group in far_groups:
        mixtures[group] = mixture_part(group, gate)
        gate = mixtures[group]
    far_sums = after(far_sums, gate)
    for group in near_groups:
        row_sums[group] = row_part(group, far_parts(far_sums, group))
    arrivals = return_near(row_sums)
    mixtures[0] = mixture_part(0, row_sums[near_groups[-1]])
    arrivals = after(arrivals, mixtures[0])
    row_total = return_total(row_sums[0], arrivals)
    for group in far_groups:
        mixtures[group] = after(mixtures[group], row_total)
    far_mixtures = return_far(mixtures)
    grad_gate_terms = unpacked_rows(row_total[length:], length)
    grad_moe_rows = row_total[:length]
    grad_selected = grad_gate_terms - gates * jnp.sum(grad_gate_terms, axis=0, keepdims=True)
    grad_logits = grad_selected.astype(BF16)
    grad_moe_rows = grad_moe_rows + lax.dot_general(
        grad_logits, w_router, (((0,), (1,)), ((), ())), preferred_element_type=jnp.float32
    )
    grad_middle, gain_moe_terms = norm_backward(
        residual_middle, inverse_moe, gain_moe, grad_moe_rows
    )
    grad_middle = grad_middle + upstream
    grad_attn = grad_middle.astype(jnp.bfloat16)
    grad_heads = (
        jnp.einsum("td,fd->tf", grad_attn, output_weight, preferred_element_type=jnp.float32)
        .astype(jnp.bfloat16)
    )
    def back(distance, grad_heads, arrived, grad_queries):
        return back_chunk(
            z_index,
            distance,
            queries,
            chunks[distance],
            grad_heads,
            attention_output,
            attention_stats,
            arrived,
            grad_queries,
        )

    def down(distance, grad_chunk):
        pairs = [(i, i - 1) for i in range(distance, contexts)]
        return lax.ppermute(grad_chunk, "context", pairs)

    grad_queries, arrived = None, None
    early_exchange = None
    for distance in reversed(range(1, contexts)):
        grad_chunk, grad_queries = back(distance, grad_heads, arrived, grad_queries)
        arrived = down(distance, grad_chunk)
        if distance == contexts - 1:
            far_mixtures = after(far_mixtures, grad_chunk)
            gate = grad_chunk
            for group in near_groups:
                mixtures[group] = mixture_part(group, gate, far_parts(far_mixtures, group))
                gate = mixtures[group]
            mixture_arrivals = return_near(mixtures)
            own_chunk, grad_queries = back(0, after(grad_heads, gate), None, grad_queries)
            arrived, grad_queries = lax.optimization_barrier((arrived, grad_queries))
        elif distance == contexts - 2:
            out_sums = out_grad(
                sum_place,
                attn_low,
                after(grad_attn, grad_chunk),
                moe_low,
                jnp.pad(grad_logits.T, ((0, 0), (0, 128 - EXPERTS))),
                gain_moe_terms.astype(BF16),
            )
            mixture_arrivals = after(mixture_arrivals, out_sums)
            mixed = return_total(mixtures[0], mixture_arrivals)
            layer_output = (residual_middle + mixed).astype(jnp.bfloat16)[None]
            if len(finals) > 1:
                early_exchange = exchange_x(after(finals[0], grad_chunk))
            arrived, out_sums, layer_output, early_exchange = lax.optimization_barrier(
                (arrived, out_sums, layer_output, early_exchange)
            )
    blocks = []
    if early_exchange is not None:
        early_exchange, grad_chunk = lax.optimization_barrier((early_exchange, grad_chunk))
        blocks.append(exchange_core(*early_exchange))
    out_sums = summed(after(out_sums, grad_chunk), 0, 1, True)
    *query_sums, grad_normed = query_grad(
        sum_place, grad_queries, cos_rows, sin_rows, normed_low, query_weight, scale
    )
    arrived, grad_normed, out_sums, blocks, query_sums = lax.optimization_barrier(
        (arrived, grad_normed, out_sums, blocks, query_sums)
    )
    query_sums = summed(query_sums, 0, 1, True)
    out_sums = summed(out_sums, 1, 2, True)
    *keyval_sums, grad_input = keyval_grad(
        sum_place,
        own_chunk,
        arrived,
        cos_rows,
        sin_rows,
        normed_low,
        keyval_weight,
        grad_normed,
        decoder_input[0],
        jnp.broadcast_to(inverse_attn, (length, 128)),
        gain_attn[None, :],
        grad_middle,
    )
    grad_input = grad_input[None]
    chains = [keyval_sums, query_sums, out_sums]
    steps = [0, 1, 2]
    order = [False, True, True]
    stops = len(sum_hops())
    chains = list(lax.optimization_barrier(tuple(chains)))
    round_number = 0
    last_exchange = exchange_x(after(finals[-1], chains[0]))
    while min(steps) < stops:
        for i in range(len(chains)):
            if steps[i] < stops:
                chains[i] = summed(chains[i], steps[i], steps[i] + 1, order[i])
                steps[i] += 1
        chains = list(lax.optimization_barrier(tuple(chains)))
        if round_number == 2:
            blocks.append(exchange_core(*after(last_exchange, chains[0])))
        round_number += 1
    late, grad_query, early = chains
    grad_out = early[:, :width]
    grad_router = early[:, width : width + EXPERTS]
    grad_gain_moe = early[:, width + EXPERTS]
    grad_keyval = late[:, :kv_width]
    grad_gain_attn = late[:, kv_width]

    near_blocks = jnp.stack(
        [jnp.concatenate([block[place] for block in blocks], axis=0) for place in range(spans)]
    )
    arranged = jnp.concatenate(
        [
            lax.dynamic_index_in_dim(near_blocks, jnp.bitwise_xor(dp_place, b), 0, keepdims=False)
            for b in range(spans)
        ],
        axis=0,
    ).astype(F32)
    grad_gateup = arranged[:, :, : w_gateup.shape[2]]
    grad_down = jnp.transpose(arranged[:, :, w_gateup.shape[2] :], (0, 2, 1))
    return (
        layer_output,
        grad_input,
        grad_gain_attn,
        grad_query,
        grad_keyval,
        grad_out,
        grad_gain_moe,
        grad_router,
        grad_gateup,
        grad_down,
    )


def solution(mesh):
    in_specs = (
        P(("experts", "dp"), "context", None),
        P(),
        P(),
        P(),
        P(),
        P(),
        P(),
        P("experts", None, None),
        P("experts", None, None),
        P(("experts", "dp"), "context", None),
        P(("experts", "dp"), "context", None),
        P(("experts", "dp"), "context", None),
    )
    out_specs = (
        P(("experts", "dp"), "context", None),
        P(("experts", "dp"), "context", None),
        P(("experts", "context", "dp")),
        P(("experts", "context", "dp"), None),
        P(("experts", "context", "dp"), None),
        P(("experts", "context", "dp"), None),
        P(("experts", "context", "dp")),
        P(("experts", "context", "dp"), None),
        P("experts", ("context", "dp"), None),
        P("experts", None, ("context", "dp")),
    )
    return jax.shard_map(
        on_device, mesh=mesh, in_specs=in_specs, out_specs=out_specs, check_vma=False
    )
```
